32 devices in a mesh: dp: 2 (over y), shard: 16 (over z, x, core).
Axes of the slice: x: 2, y: 2, z: 4, core: 2. Of those that a mesh axis runs over, the one named last changes fastest.
Arguments:
- tokens: bfloat16 [32768, 768], P(('dp', 'shard')), may hold values from -6 to 6
- cotangent: bfloat16 [32768, 768], P(('dp', 'shard')), may hold values from -6 to 6
- lengths: int32 [32], P(('dp', 'shard')), may hold values from 341 to 1024, as said below
- attn_gain: bfloat16 [768], P(('dp', 'shard')), may hold values from 0.5 to 1.5
- attn_shift: bfloat16 [768], P(('dp', 'shard')), may hold values from -1.5 to 1.5
- qkv_weight: bfloat16 [768, 2304], P(('dp', 'shard')), may hold values from -0.21875 to 0.21875
- qv_bias: bfloat16 [2, 768], P(None, ('dp', 'shard')), may hold values from -1.5 to 1.5
- proj_weight: bfloat16 [768, 768], P(('dp', 'shard')), may hold values from -3.5 to 3.5
- proj_bias: bfloat16 [768], P(('dp', 'shard')), may hold values from -1.5 to 1.5
- mlp_gain: bfloat16 [768], P(('dp', 'shard')), may hold values from 0.5 to 1.5
- mlp_shift: bfloat16 [768], P(('dp', 'shard')), may hold values from -1.5 to 1.5
- up_weight: bfloat16 [768, 3072], P(('dp', 'shard')), may hold values from -0.21875 to 0.21875
- up_bias: bfloat16 [3072], P(('dp', 'shard')), may hold values from -1.5 to 1.5
- down_weight: bfloat16 [3072, 768], P(('dp', 'shard')), may hold values from -0.109375 to 0.109375
- down_bias: bfloat16 [768], P(('dp', 'shard')), may hold values from -1.5 to 1.5
Outputs:
- block_out: bfloat16 [32768, 768], P(('dp', 'shard'))
- input_grad: bfloat16 [32768, 768], P(('dp', 'shard'))
- grad_attn_gain: float32 [768], P(('dp', 'shard'))
- grad_attn_shift: float32 [768], P(('dp', 'shard'))
- grad_qkv_weight: float32 [768, 2304], P(('dp', 'shard'))
- grad_qv_bias: float32 [2, 768], P(None, ('dp', 'shard'))
- grad_proj_weight: float32 [768, 768], P(('dp', 'shard'))
- grad_proj_bias: float32 [768], P(('dp', 'shard'))
- grad_mlp_gain: float32 [768], P(('dp', 'shard'))
- grad_mlp_shift: float32 [768], P(('dp', 'shard'))
- grad_up_weight: float32 [768, 3072], P(('dp', 'shard'))
- grad_up_bias: float32 [3072], P(('dp', 'shard'))
- grad_down_weight: float32 [3072, 768], P(('dp', 'shard'))
- grad_down_bias: float32 [768], P(('dp', 'shard'))
The draws below stay inside these ranges and needn't reach their ends.
Inputs may be any that keep to these rules, and one draw needn't show every extreme that they name: `lengths`: A clip holds 1024 valid patches (full clip) or 341 to 1024 // 2 (patchout clip); slots from the count on are padding whose keys are masked.
All inputs are finite; a program needn't handle non-finite values.
Results may differ from the reference program's by a relative error of at most 0.012.
Values may be sent and summed in bfloat16 or wider, within the bound.
A program may use at most 256 MiB of HBM per device.

```python
import jax
import jax.numpy as jnp
from jax import lax

D = 768
HEADS = 12
HD = 64
FF = 3072
SEQ = 1024
CLIPS = 32
TOKENS = 32768


def draw_lengths(key, part):
    key = jax.random.fold_in(key, 11)
    first_key, second_key, third_key = jax.random.split(key, 3)
    is_full = jax.random.randint(first_key, (CLIPS,), 0, 2)
    patchout = jax.random.randint(second_key, (CLIPS,), SEQ // 3, SEQ // 2 + 1)
    chosen = jax.random.randint(third_key, (), 0, CLIPS)
    places = jnp.arange(CLIPS)
    is_full = jnp.where(places == chosen, 1, is_full)
    is_full = jnp.where(places == (chosen + 1) % CLIPS, 0, is_full)
    patchout = jnp.where(places == (chosen + 1) % CLIPS, SEQ // 3, patchout)
    return jnp.where(is_full == 1, SEQ, patchout).astype(jnp.int32)


def spiked(array, stream_key, source, target, shards_of, factor):
    owner, partner = [(jnp.arange(array.shape[position]) // (array.shape[position] // shards_of)).reshape([-1 if axis == position else 1 for axis in range(array.ndim)]) for position in (source, target)]
    chosen = jax.random.permutation(stream_key, shards_of)[partner]
    strong = (owner == chosen) | (owner == (partner + shards_of // 2) % shards_of)
    return jnp.where(strong, factor * array, array)


def level_of(stream_key, shape, cuts, low, top_value):
    level, own = 1.0, jax.random.fold_in(stream_key, 6)
    for dim, blocks in cuts:
        heights = jnp.exp(jax.random.uniform(jax.random.fold_in(own, dim), (blocks,), jnp.float32, low / len(cuts), top_value / len(cuts)))
        level = level * jnp.repeat(heights, shape[dim] // blocks).reshape([-1 if axis == dim else 1 for axis in range(len(shape))])
    return level


def gaussian(rng, extent, scale, most, shards=(), held_as=jnp.bfloat16):
    values = scale * jax.random.normal(rng, extent, jnp.float32)
    if shards:
        values = values * level_of(rng, extent, shards, -0.22, 0.18)
    return jnp.clip(values, -most, most).astype(held_as)


def heavy_noise(rng, shape, width, limit, shards, heavy, dtype=jnp.bfloat16):
    values = width * jax.random.normal(rng, shape, jnp.float32)
    if shards:
        values = values * level_of(rng, shape, shards, -0.22, 0.18)
    return jnp.clip(spiked(values, jax.random.fold_in(rng, 3), *heavy), -limit, limit).astype(dtype)


def setup_inputs(seed: int = 0) -> dict:
    streams_of = jax.random.split(jax.random.key(seed), 16)
    tokens = gaussian(streams_of[0], (TOKENS, D), 1.0, 6.0, ((0, 32),))
    cotangent = heavy_noise(streams_of[1], (TOKENS, D), 1.0, 6.0, ((0, 32),), (0, 1, 32, 2.75))
    lengths = draw_lengths(jax.random.fold_in(streams_of[15], 71), 0)
    attn_gain = jnp.clip(1.0 + 0.1 * jax.random.normal(streams_of[3], (D,), jnp.float32), 0.5, 1.5).astype(jnp.bfloat16)
    attn_shift = gaussian(streams_of[4], (D,), 0.3, 1.5, ((0, 32),))
    qkv_weight = gaussian(streams_of[5], (D, 3 * D), D ** -0.5, 0.21875, ((0, 32),))
    qv_bias = gaussian(streams_of[6], (2, D), 0.3, 1.5, ((1, 32),))
    proj_weight = gaussian(streams_of[7], (D, D), (max(D * 4 // SEQ, 1)) ** -0.5, 3.5, ((0, 32),))
    proj_bias = gaussian(streams_of[8], (D,), 0.3, 1.5, ((0, 32),))
    mlp_gain = jnp.clip(1.0 + 0.1 * jax.random.normal(streams_of[9], (D,), jnp.float32), 0.5, 1.5).astype(jnp.bfloat16)
    mlp_shift = gaussian(streams_of[10], (D,), 0.3, 1.5, ((0, 32),))
    up_weight = gaussian(streams_of[11], (D, FF), D ** -0.5, 0.21875, ((0, 32),))
    up_bias = gaussian(streams_of[12], (FF,), 0.3, 1.5, ((0, 32),))
    down_weight = gaussian(streams_of[13], (FF, D), FF ** -0.5, 0.109375, ((0, 32),))
    down_bias = gaussian(streams_of[14], (D,), 0.3, 1.5, ((0, 32),))
    return dict(tokens=tokens, cotangent=cotangent, lengths=lengths, attn_gain=attn_gain, attn_shift=attn_shift, qkv_weight=qkv_weight, qv_bias=qv_bias, proj_weight=proj_weight, proj_bias=proj_bias, mlp_gain=mlp_gain, mlp_shift=mlp_shift, up_weight=up_weight, up_bias=up_bias, down_weight=down_weight, down_bias=down_bias)


@jax.custom_vjp
def low(v):
    return lax.optimization_barrier(v.astype(jnp.bfloat16)).astype(jnp.float32)

@jax.custom_vjp
def low_back(v):
    return v

def low_keep(v):
    return (low(v), None)

def low_pass(kept, grad):
    return (grad,)

def back_keep(v):
    return (v, None)

def back_low(kept, grad):
    return (low(grad),)
low.defvjp(low_keep, low_pass)
low_back.defvjp(back_keep, back_low)
epsilon = 1e-06
masked_score = -1000000000.0

def layer_norm(values, gain, shift):
    center = lax.optimization_barrier(jnp.mean(values, -1, keepdims=True))
    centered = values - center
    spread = lax.optimization_barrier(jnp.mean(centered * centered, -1, keepdims=True))
    return centered * lax.rsqrt(spread + epsilon) * gain + shift

def gelu_exact(values):
    return 0.5 * values * (1.0 + jax.scipy.special.erf(values * 0.7071067811865476))

def layer(clip_rows, length, params):
    attn_gain, attn_shift, qkv_weight, qv_bias, proj_weight, proj_bias, mlp_gain, mlp_shift, up_weight, up_bias, down_weight, down_bias = params
    highest = lax.Precision.HIGHEST
    normed_one = low(layer_norm(clip_rows, attn_gain, attn_shift))
    full_bias = jnp.concatenate([qv_bias[0], jnp.zeros((D,), jnp.float32), qv_bias[1]])
    projected = low(low_back(jnp.dot(normed_one, qkv_weight, precision=highest) + full_bias))
    split = projected.reshape(SEQ, 3, HEADS, HD)
    queries = split[:, 0]
    key_rows = split[:, 1]
    value_rows = split[:, 2]
    key_mask = jnp.arange(SEQ) < length
    scaling = HD ** (-0.5)
    block_rows = min(512, SEQ)

    def one_block(query_block):
        scores = jnp.einsum('qhd,khd->hqk', query_block, key_rows, precision=highest) * scaling
        scores = low_back(jnp.where(key_mask[None, None, :], scores, masked_score))
        row_top = lax.optimization_barrier(jnp.max(scores, -1, keepdims=True))
        exponent = jnp.exp(scores - row_top)
        attention = low(exponent / lax.optimization_barrier(jnp.sum(exponent, -1, keepdims=True)))
        return jnp.einsum('hqk,khd->qhd', attention, value_rows, precision=highest)
    mixed = lax.map(jax.checkpoint(one_block), queries.reshape(SEQ // block_rows, block_rows, HEADS, HD))
    attended = low(low_back(mixed.reshape(SEQ, D)))
    branch = low_back(jnp.dot(attended, proj_weight, precision=highest) + proj_bias)
    residual = clip_rows + branch
    normed_two = low(layer_norm(residual, mlp_gain, mlp_shift))
    hidden = low_back(jnp.dot(normed_two, up_weight, precision=highest) + up_bias)
    active = low(gelu_exact(hidden))
    return residual + low_back(jnp.dot(active, down_weight, precision=highest) + down_bias)

def reference(tokens, cotangent, lengths, attn_gain, attn_shift, qkv_weight, qv_bias, proj_weight, proj_bias, mlp_gain, mlp_shift, up_weight, up_bias, down_weight, down_bias):
    params = tuple((item.astype(jnp.float32) for item in (attn_gain, attn_shift, qkv_weight, qv_bias, proj_weight, proj_bias, mlp_gain, mlp_shift, up_weight, up_bias, down_weight, down_bias)))
    inputs = tokens.astype(jnp.float32).reshape(CLIPS, SEQ, D)
    grads_in = cotangent.astype(jnp.float32).reshape(CLIPS, SEQ, D)

    def one_clip(carry, item):
        clip_rows, clip_grad, length = item

        def forward(rows_value, param_value):
            return layer(rows_value, length, param_value)
        result, pull = jax.vjp(forward, clip_rows, params)
        grad_rows, grad_params = pull(clip_grad)
        carry = tuple((total + part for total, part in zip(carry, grad_params)))
        return (carry, (result.astype(jnp.bfloat16), grad_rows.astype(jnp.bfloat16)))
    start = tuple((jnp.zeros(item.shape, jnp.float32) for item in params))
    totals, outputs = lax.scan(one_clip, start, (inputs, grads_in, lengths))
    block_out = outputs[0].reshape(TOKENS, D)
    input_grad = outputs[1].reshape(TOKENS, D)
    return (block_out, input_grad, totals[0], totals[1], totals[2], totals[3], totals[4], totals[5], totals[6], totals[7], totals[8], totals[9], totals[10], totals[11])
```

```python
import functools

import jax
import jax.numpy as jnp
from jax import lax
from jax.experimental import pallas as pl
from jax.experimental.pallas import tpu as pltpu
from jax.sharding import PartitionSpec as P

f32 = jnp.float32
bf16 = jnp.bfloat16
HD = 64
PAIR = 2 * HD
EPS = 1e-06
MASKED = -1e30
AXES = ("dp", "shard")
VMEM_LIMIT = 63 * 2**20

AG, AS, QB, VB, PB, MG, MS, DB, UB = range(9)


def dg(a, b, ca, cb):
    return lax.dot_general(a, b, (((ca,), (cb,)), ((), ())), preferred_element_type=f32)


def rows_of(v):
    return v.reshape(-1, v.shape[-1])


def norm_parts(v):
    center = v - jnp.mean(v, -1, keepdims=True)
    inv = lax.rsqrt(jnp.mean(center * center, -1, keepdims=True) + EPS)
    return center * inv, inv


def norm_back(n, inv, z):
    return inv * (z - jnp.mean(z, -1, keepdims=True) - n * jnp.mean(z * n, -1, keepdims=True))


def key_bias(length, seq):
    return jnp.where(lax.broadcasted_iota(jnp.int32, (seq, 1), 0) < length, 0.0, MASKED).astype(f32)


def head_only(v, hh):
    lane = lax.broadcasted_iota(jnp.int32, (1, PAIR), 1)
    return jnp.where(lane // HD == hh, v, jnp.zeros((), v.dtype))


class Place:
    def __init__(self, nz):
        shard = lax.axis_index("shard")
        self.nz = nz
        self.y = lax.axis_index("dp")
        self.c = lax.rem(shard, 2)
        self.x = lax.rem(lax.div(shard, 2), 2)
        self.z = lax.div(shard, 4)
        fy, fx = 1 - 2 * self.y, 1 - 2 * self.x
        self.ay, self.ax = self.y + (1 - self.c) * fy, self.x + self.c * fx
        self.by, self.bx = self.y + self.c * fy, self.x + (1 - self.c) * fx

    def device(self, y, z, x, c):
        return (y, (z * 2 + x) * 2 + c)

    def peer(self):
        return self.device(self.y, self.z, self.x, 1 - self.c)

    def along_z(self, k):
        return self.device(self.y, lax.rem(self.z + k, self.nz), self.x, self.c)

    def a(self):
        return self.device(self.ay, self.z, self.ax, self.c)

    def b(self):
        return self.device(self.by, self.z, self.bx, self.c)

    def partners(self):
        return [self.peer(), self.a(), self.b()] + [self.along_z(k) for k in range(1, self.nz)]


def enter(place):
    barrier = pltpu.get_barrier_semaphore()
    partners = place.partners()
    for d in partners:
        pl.semaphore_signal(barrier, inc=1, device_id=d, device_id_type=pl.DeviceIdType.MESH)
    pl.semaphore_wait(barrier, len(partners))


def remote(src, dst, send, recv, device):
    return pltpu.make_async_remote_copy(
        src_ref=src, dst_ref=dst, send_sem=send, recv_sem=recv, device_id=device,
        device_id_type=pl.DeviceIdType.MESH,
    )


class Gather:
    def __init__(self, place, block, column, swap, send, recv):
        self.p, self.block, self.column, self.swap = place, block, column, swap
        self.send, self.recv = send, recv
        self.started = []

    def move(self, slot, src, dst, device):
        return remote(src, dst, self.send.at[slot], self.recv.at[slot], device)

    def go(self, copy):
        copy.start()
        self.started.append(copy)

    def exchange(self):
        src, dst, _ = self.swap
        return self.move(0, src, dst, self.p.peer())

    def X(self):
        self.go(self.exchange())

    def zs(self):
        p = self.p
        own = self.block(p.y, p.z, p.x, p.c)
        return [self.move(k, own, own, p.along_z(k)) for k in range(1, p.nz)]

    def over(self, slot, y, x, device):
        v = self.column(y, x, self.p.c)
        return self.move(slot, v, v, device)

    def to_b(self):
        return self.over(4, self.p.y, self.p.x, self.p.b())

    def to_a(self, second):
        p = self.p
        y, x = (p.by, p.bx) if second else (p.y, p.x)
        return self.over(5 + second, y, x, p.a())

    def across(self, i):
        p = self.p
        y, x = [(p.y, p.x), (p.by, p.bx), (p.ay, p.ax), (1 - p.y, 1 - p.x)][i]
        return self.over(7 + i, y, x, p.peer())

    def Z(self):
        if self.swap is not None:
            self.exchange().wait_recv()
            self.swap[2]()
        for cp in self.zs():
            self.go(cp)

    def B(self):
        for cp in self.zs():
            cp.wait_recv()
        self.go(self.to_b())
        self.go(self.to_a(0))
        self.go(self.across(0))

    def A(self):
        self.to_b().wait_recv()
        self.go(self.to_a(1))
        self.go(self.across(1))

    def C(self):
        self.to_a(0).wait_recv()
        self.go(self.across(2))
        self.to_a(1).wait_recv()
        self.go(self.across(3))

    def D(self):
        for i in range(4):
            self.across(i).wait_recv()

    def finish(self):
        if self.swap is not None:
            self.exchange().wait_send()
        for cp in self.zs() + [self.to_b(), self.to_a(0), self.to_a(1)] + [self.across(i) for i in range(4)]:
            cp.wait_send()


def pair_rows(first, second):
    return jnp.concatenate([first.astype(f32), second.astype(f32)], 0).astype(bf16)


def expand_table(vbuf, vec, own, ff_own):
    many = vbuf.shape[0] * vbuf.shape[1] * vbuf.shape[2] * vbuf.shape[3]
    width = vec.shape[1]
    ff = many * ff_own
    flat = vbuf[...].reshape(many * 16, PAIR)

    def spread(n, each):
        lane = lax.broadcasted_iota(jnp.int32, (PAIR, n), 1)
        return (lax.rem(lane, each) == lax.broadcasted_iota(jnp.int32, (PAIR, n), 0)).astype(f32).astype(bf16)

    full = dg(flat, spread(width, own), 1, 0).reshape(many, 16, width)
    where = lax.broadcasted_iota(jnp.int32, (many, 1, width), 2) - own * lax.broadcasted_iota(
        jnp.int32, (many, 1, width), 0
    )
    vec[0:16, :] = jnp.sum(jnp.where((where >= 0) & (where < own), full, 0.0), 0)
    pick = (
        lax.broadcasted_iota(jnp.int32, (many, many * 16), 1)
        == 16 * lax.broadcasted_iota(jnp.int32, (many, many * 16), 0) + 8
    )
    row = dg(pick.astype(f32).astype(bf16), flat, 1, 0).astype(bf16)
    full = dg(row, spread(ff, ff_own), 1, 0)
    where = lax.broadcasted_iota(jnp.int32, (many, ff), 1) - ff_own * lax.broadcasted_iota(jnp.int32, (many, ff), 0)
    up = jnp.sum(jnp.where((where >= 0) & (where < ff_own), full, 0.0), 0, keepdims=True)
    for j in range(ff // width):
        vec[UB + j : UB + j + 1, :] = up[:, j * width : (j + 1) * width]


def gather_items(place, own_down, wqkv, wproj, wup, wdown, vbuf, xs, xr, send, recv):
    p = place
    (xs_qkv, xs_proj, xs_up), (xr_qkv, xr_proj, xr_up) = xs, xr
    own = wqkv.shape[-2] // 2

    def joined(mine, theirs, write):
        def go():
            m, t = mine()[:own].astype(f32), theirs()[:own].astype(f32)
            lo, hi = jnp.where(p.c == 0, m, t), jnp.where(p.c == 0, t, m)
            write(jnp.concatenate([lo, hi], 0).astype(bf16))
        return go

    items = []

    def add(block, column, swap):
        i = len(items)
        items.append(Gather(p, block, column, swap, send.at[i], recv.at[i]))

    add(lambda y, z, x, c: vbuf.at[y, z, x, c], lambda y, x, c: vbuf.at[y, :, x, c], None)

    def add_swapped(view, xs_of, xr_of):
        block = lambda y, z, x, c: view(c).at[y, z, x]
        column = lambda y, x, c: view(c).at[y, :, x]

        def write(v):
            view(p.c)[p.y, p.z, p.x] = v

        add(block, column, (xs_of(1 - p.c), xr_of, joined(lambda: xs_of(p.c)[...], lambda: xr_of[...], write)))

    for g in range(wqkv.shape[0]):
        add_swapped(lambda c, g=g: wqkv.at[g, c], lambda c, g=g: xs_qkv.at[g, c], xr_qkv.at[g])
    add_swapped(lambda c: wproj.at[c], lambda c: xs_proj.at[c], xr_proj)
    part = wdown.shape[-2] // 2
    for k in range(2):
        rows = pl.ds(k * part, part)
        add(
            lambda y, z, x, c, rows=rows: wdown.at[y, z, x, c, rows],
            lambda y, x, c, rows=rows: wdown.at[y, :, x, c, rows],
            None,
        )
    for k in range(2):
        add_swapped(lambda c, k=k: wup.at[c, k], lambda c, k=k: xs_up.at[c, k], xr_up.at[k])
    return items


VECI, G0, G1, G2, PROJ, D0, D1, U0, U1 = range(9)
FORWARD_PLAN = {
    "start": "",
    "stats": [("B", VECI), ("B", G0), ("Z", G1), ("A", VECI), ("A", G0), ("B", G1), ("Z", G2),
              ("C", VECI), ("C", G0), ("A", G1), ("B", G2), ("Z", PROJ), ("D", VECI)],
    "norm": [("D", G0), ("C", G1), ("A", G2), ("B", PROJ), ("Z", D0)],
    0: [("C", G2), ("A", PROJ), ("B", D0), ("Z", D1)],
    1: [("D", G1), ("C", PROJ), ("A", D0), ("B", D1), ("Z", U0)],
    2: [("C", D0), ("A", D1), ("B", U0), ("Z", U1)],
    3: [("D", G2), ("C", D1), ("A", U0), ("B", U1)],
    4: [("C", U0), ("A", U1)],
    5: [("C", U1), ("D", PROJ)],
    "branch": [("D", D0), ("D", D1), ("D", U0)],
    "mlp": [("D", U1)],
}


def forward_kernel(
    comm, len_ref, tok_ref, cot_ref, vec_in, wqkv_in, wproj_in, wup_in, wdown_in,
    out_hbm, proj_hbm, ot_hbm, lse_hbm, do_hbm, gmid_hbm, n1t_hbm, gup_hbm, gdown_hbm, gproj_hbm, vg_ref, *rest,
):
    seq, width = tok_ref.shape
    chunks = gup_hbm.shape[0]
    if comm:
        wqkv_hbm, vec_hbm = rest[:2]
        rest = rest[2:]
    n1, n1t, proj, ot, att, lse, res, n2, n2t, acc, gn2, act, gh, gstage, sems = rest[:15]
    pairs = proj.shape[0]
    copies = []

    def send_out(src, dst, sem):
        cp = pltpu.make_async_copy(src, dst, sem)
        cp.start()
        return cp

    if comm:
        vec_ref, wqkv, wproj, wup, wdown, vbuf, xs_qkv, xs_proj, xs_up, xr_qkv, xr_proj, xr_up, send, recv = rest[15:]
        place = Place(wqkv.shape[3])
        own = wqkv_in.shape[0]
        items = gather_items(
            place, wdown_in, wqkv, wproj, wup, wdown, vbuf, (xs_qkv, xs_proj, xs_up), (xr_qkv, xr_proj, xr_up),
            send, recv,
        )

        def w_qkv(p):
            return rows_of(wqkv[lax.div(p, 2), lax.rem(p, 2)])

        def w_up(j):
            return rows_of(wup[j // 2, j % 2])

        def w_down(j):
            zs = wdown.shape[1] // 2
            return rows_of(wdown[j // 2, zs * (j % 2) : zs * (j % 2) + zs])

        def w_proj(i):
            return rows_of(wproj[i])

        def tick(name):
            for step, i in FORWARD_PLAN[name]:
                getattr(items[i], step)()

        order = (0, 2, 1, 3)
    else:
        vec_ref = vec_in

        def w_qkv(p):
            return wqkv_in[p]

        def w_up(j):
            return wup_in[j]

        def w_down(j):
            return wdown_in[j]

        def w_proj(i):
            return wproj_in[i]

        def tick(name):
            pass

        order = range(chunks)

    def vec(i):
        return vec_ref[i : i + 1, :]

    rb = 256
    if comm:
        half = width // 2
        vbuf[place.y, place.z, place.x, place.c] = vec_in[...]
        wdown[place.y, place.z, place.x, place.c] = wdown_in[...]
        for p in range(pairs):
            for t in range(3):
                lanes = slice(t * width + p * PAIR, t * width + (p + 1) * PAIR)
                xs_qkv[p // 2, p % 2, 0:own, t * PAIR : (t + 1) * PAIR] = wqkv_in[:, lanes]
        for i in range(2):
            xs_proj[i, 0:own, :] = wproj_in[:, i * half : (i + 1) * half]
        for j in range(chunks):
            xs_up[j // 2, j % 2, 0:own, :] = wup_in[:, j * width : (j + 1) * width]
        enter(place)
        for i in (G0, G1, G2, PROJ, U0, U1):
            items[i].X()
        items[VECI].Z()
        items[G0].Z()

    @pl.loop(0, seq // rb)
    def _(r):
        sl = pl.ds(pl.multiple_of(r * rb, rb), rb)
        n, _inv = norm_parts(tok_ref[sl, :].astype(f32))
        res[sl, :] = n

    tick("stats")
    if comm:
        expand_table(vbuf, vec_ref, own, wdown_in.shape[0])
        copies_late = [send_out(vec_ref, vec_hbm, sems.at[8 + pairs])]

    @pl.loop(0, seq // rb)
    def _(r):
        sl = pl.ds(pl.multiple_of(r * rb, rb), rb)
        n1[sl, :] = (res[sl, :] * vec(AG) + vec(AS)).astype(bf16)

    n1t[...] = n1[...].T
    copies.append(send_out(n1t, n1t_hbm, sems.at[0]))
    tick("norm")

    bias_k = key_bias(len_ref[0], seq)
    ones = jnp.ones((16, seq), bf16)
    qv_bias = [(vec(QB)[:, i * PAIR : (i + 1) * PAIR], vec(VB)[:, i * PAIR : (i + 1) * PAIR]) for i in range(pairs)]

    def pick(p, choices):
        v = choices[0]
        for i in range(1, pairs):
            v = jnp.where(p == i, choices[i], v)
        return v

    @pl.loop(0, pairs)
    def _(p):
        qkv = dg(n1[...], w_qkv(p), 1, 0)
        proj[p, :, 0:PAIR] = (qkv[:, 0:PAIR] + pick(p, [q for q, v in qv_bias])).astype(bf16)
        proj[p, :, PAIR : 2 * PAIR] = qkv[:, PAIR : 2 * PAIR].astype(bf16)
        proj[p, :, 2 * PAIR :] = (qkv[:, 2 * PAIR :] + pick(p, [v for q, v in qv_bias])).astype(bf16)
        k2 = proj[p, :, PAIR : 2 * PAIR]
        v2t = proj[p, :, 2 * PAIR :].T
        q2 = proj[p, :, 0:PAIR] * jnp.asarray(HD**-0.5, bf16)
        for hh in range(2):
            rows = slice(HD * hh, HD * hh + HD)
            s = dg(k2, head_only(q2, hh), 1, 1) + bias_k
            top = jnp.max(s, 0, keepdims=True)
            e = jnp.exp(s - top).astype(bf16)
            o = dg(jnp.concatenate([v2t[rows], ones], 0), e, 1, 0)
            total = o[HD : HD + 1]
            ot[p, rows, :] = (o[:HD] / total).astype(bf16)
            lse[2 * p + hh] = jnp.broadcast_to(top + jnp.log(total), (8, seq))
        if comm:
            for i in range(pairs):

                @pl.when(p == i)
                def _(i=i):
                    tick(i)

    if comm:
        for g in range(wqkv.shape[0]):
            for c in range(2):
                copies_late.append(
                    send_out(wqkv.at[g, c], wqkv_hbm.at[g, c], sems.at[9 + pairs + 2 * g + c])
                )
    for p in range(pairs):
        att[:, p * PAIR : (p + 1) * PAIR] = ot[p].T
    copies.append(send_out(proj, proj_hbm, sems.at[1]))
    copies.append(send_out(ot, ot_hbm, sems.at[2]))
    copies.append(send_out(lse, lse_hbm, sems.at[3]))

    half = width // 2

    @pl.loop(0, seq // rb)
    def _(r):
        sl = pl.ds(pl.multiple_of(r * rb, rb), rb)
        a = att[sl, :]
        branch = jnp.concatenate([dg(a, w_proj(i), 1, 0) for i in range(2)], 1)
        v = tok_ref[sl, :].astype(f32) + branch + vec(PB)
        res[sl, :] = v
        acc[sl, :] = v + vec(DB)
        gn2[sl, :] = jnp.zeros((rb, width), f32)
        n, _inv = norm_parts(v)
        n2[sl, :] = (n * vec(MG) + vec(MS)).astype(bf16)

    n2t[...] = n2[...].T
    tick("branch")

    rm = 512
    for turn, j in enumerate(order):
        if turn == 2:
            tick("mlp")
        vg_ref[4 + j : 5 + j, :] = jnp.zeros((1, width), f32)

        @pl.loop(0, seq // rm)
        def _(r, j=j):
            sl = pl.ds(pl.multiple_of(r * rm, rm), rm)
            h = dg(n2[sl, :], w_up(j), 1, 0) + vec(UB + j)
            phi = 0.5 * (1.0 + lax.erf(h * 0.7071067811865476))
            a = (h * phi).astype(bf16)
            act[sl, :] = a
            acc[sl, :] += dg(a, w_down(j), 1, 0)
            ga = dg(cot_ref[sl, :], w_down(j), 1, 1)
            g = (ga * (phi + h * jnp.exp(-0.5 * h * h) * 0.3989422804014327)).astype(bf16)
            gh[sl, :] = g
            gn2[sl, :] += dg(g, w_up(j), 1, 1)
            vg_ref[4 + j : 5 + j, :] += jnp.sum(g.astype(f32), 0, keepdims=True)

        if turn > 0:
            copies[-1].wait()
            copies[-2].wait()
            del copies[-2:]
        gstage[0] = dg(act[...], cot_ref[...], 0, 0).astype(bf16)
        copies.append(send_out(gstage.at[0], gdown_hbm.at[j], sems.at[4]))
        gstage[1] = dg(n2t[...], gh[...], 1, 0).astype(bf16)
        copies.append(send_out(gstage.at[1], gup_hbm.at[j], sems.at[5]))

    vg_ref[0:4, :] = jnp.zeros((4, width), f32)

    @pl.loop(0, seq // rb)
    def _(r):
        sl = pl.ds(pl.multiple_of(r * rb, rb), rb)
        n2[sl, :] = acc[sl, :].astype(bf16)
        g = gn2[sl, :]
        n, inv = norm_parts(res[sl, :])
        cot = cot_ref[sl, :].astype(f32)
        mid = cot + norm_back(n, inv, g * vec(MG))
        acc[sl, :] = mid
        low = mid.astype(bf16)
        act[sl, :] = low
        vg_ref[0:1, :] += jnp.sum(g * n, 0, keepdims=True)
        vg_ref[1:2, :] += jnp.sum(g, 0, keepdims=True)
        vg_ref[2:3, :] += jnp.sum(low.astype(f32), 0, keepdims=True)
        vg_ref[3:4, :] += jnp.sum(cot, 0, keepdims=True)
        back = dg(low[:, :half], w_proj(0), 1, 1) + dg(low[:, half:], w_proj(1), 1, 1)
        gh[sl, :] = back.astype(bf16)

    last = [copies.pop(), copies.pop()]
    copies.append(send_out(n2, out_hbm, sems.at[6]))
    copies.append(send_out(acc, gmid_hbm, sems.at[7]))
    for p in range(pairs):
        copies.append(send_out(gh.at[:, p * PAIR : (p + 1) * PAIR], do_hbm.at[p], sems.at[8 + p]))
    for cp in last:
        cp.wait()
    for i in range(2):
        gstage[i, :, :half] = dg(rows_of(ot[...]), act[:, i * half : (i + 1) * half], 1, 0).astype(bf16)
        copies.append(send_out(gstage.at[i, :, pl.ds(0, half)], gproj_hbm.at[i], sems.at[4 + i]))
    if comm:
        copies += copies_late
        for item in items:
            item.finish()
    for cp in copies:
        cp.wait()


def backward_kernel(
    len_ref, tok_ref, vec_ref, proj_hbm, ot_hbm, lse_hbm, do_hbm, gmid_hbm, n1t_hbm, wqkv_ref,
    gin_hbm, gqkv_hbm, vg_ref,
    proj, ot, lse, do, gmid, n1t, gqkv, gin, sems,
):
    seq, width = tok_ref.shape
    pairs = proj.shape[0]

    def start(src, dst, sem):
        cp = pltpu.make_async_copy(src, dst, sem)
        cp.start()
        return cp

    loads = [
        start(proj_hbm, proj, sems.at[0]),
        start(do_hbm, do, sems.at[1]),
        start(ot_hbm, ot, sems.at[2]),
        start(lse_hbm, lse, sems.at[3]),
        start(n1t_hbm, n1t, sems.at[4]),
        start(gmid_hbm, gmid, sems.at[5]),
    ]
    for cp in loads:
        cp.wait()

    bias_k = key_bias(len_ref[0], seq)
    qb = 512
    scale = HD**-0.5

    @pl.loop(0, pairs)
    def _(p):
        k2 = proj[p, :, PAIR : 2 * PAIR]
        v2 = proj[p, :, 2 * PAIR :]
        k2t = k2.T
        dk = dv = None
        dqt = []
        for hh in range(2):
            rows = slice(HD * hh, HD * hh + HD)
            parts = []
            for i in range(seq // qb):
                sl = slice(i * qb, (i + 1) * qb)
                qm = head_only(proj[p, sl, 0:PAIR] * jnp.asarray(scale, bf16), hh)
                d = do[p, sl, :]
                dm = head_only(d, hh)
                dt = d.astype(f32).T[rows]
                delta = jnp.sum(dt * ot[p, rows, sl].astype(f32), 0, keepdims=True)
                e = jnp.exp(dg(k2, qm, 1, 1) + bias_k - lse[2 * p + hh, 0:1, sl])
                ds = (e * (dg(v2, dm, 1, 1) - delta)).astype(bf16)
                t = dg(e.astype(bf16), dm, 1, 0)
                dv = t if dv is None else dv + t
                t = dg(ds, qm, 1, 0)
                dk = t if dk is None else dk + t
                parts.append(dg(k2t[rows], ds, 1, 0) * scale)
            dqt.append(jnp.concatenate(parts, 1))
        proj[p, :, 0:PAIR] = jnp.concatenate(dqt, 0).T.astype(bf16)
        proj[p, :, PAIR : 2 * PAIR] = dk.astype(bf16)
        proj[p, :, 2 * PAIR :] = dv.astype(bf16)

    vg_ref[...] = jnp.zeros(vg_ref.shape, f32)
    outs = []
    for p in range(pairs):
        cols = slice(p * PAIR, (p + 1) * PAIR)
        g = proj[p]
        sums = jnp.sum(g.astype(f32), 0, keepdims=True)
        vg_ref[2:3, cols] = sums[:, 0:PAIR]
        vg_ref[3:4, cols] = sums[:, 2 * PAIR :]
        gqkv[p] = dg(n1t[...], g, 1, 0).astype(bf16)
        outs.append(start(gqkv.at[p], gqkv_hbm.at[p], sems.at[6 + p]))

    rb = 256

    @pl.loop(0, seq // rb)
    def _(r):
        sl = pl.ds(pl.multiple_of(r * rb, rb), rb)
        g = dg(proj[0, sl, :], rows_of(wqkv_ref[0]), 1, 1)
        for p in range(1, pairs):
            g += dg(proj[p, sl, :], rows_of(wqkv_ref[p]), 1, 1)
        n, inv = norm_parts(tok_ref[sl, :].astype(f32))
        gin[sl, :] = (gmid[sl, :] + norm_back(n, inv, g * vec_ref[AG : AG + 1, :])).astype(bf16)
        vg_ref[0:1, :] += jnp.sum(g * n, 0, keepdims=True)
        vg_ref[1:2, :] += jnp.sum(g, 0, keepdims=True)

    outs.append(start(gin, gin_hbm, sems.at[0]))
    for cp in outs:
        cp.wait()


def specs(kinds):
    table = {"s": pltpu.SMEM, "v": pltpu.VMEM, "h": pl.ANY}
    return [pl.BlockSpec(memory_space=table[k]) for k in kinds]


def sds(shape, dtype):
    return jax.ShapeDtypeStruct(shape, dtype)


def run_forward(nz, lengths, tokens, cotangent, vecs, wqkv, wproj, wup, wdown):
    seq, width = tokens.shape
    pairs = width // PAIR
    half = width // 2
    out_shape = [
        sds((seq, width), bf16),
        sds((pairs, seq, 3 * PAIR), bf16),
        sds((pairs, PAIR, seq), bf16),
        sds((2 * pairs, 8, seq), f32),
        sds((pairs, seq, PAIR), bf16),
        sds((seq, width), f32),
        sds((width, seq), bf16),
    ]
    scratch = [
        pltpu.VMEM((seq, width), bf16),
        pltpu.VMEM((width, seq), bf16),
        pltpu.VMEM((pairs, seq, 3 * PAIR), bf16),
        pltpu.VMEM((pairs, PAIR, seq), bf16),
        pltpu.VMEM((seq, width), bf16),
        pltpu.VMEM((2 * pairs, 8, seq), f32),
        pltpu.VMEM((seq, width), f32),
        pltpu.VMEM((seq, width), bf16),
        pltpu.VMEM((width, seq), bf16),
        pltpu.VMEM((seq, width), f32),
        pltpu.VMEM((seq, width), f32),
        pltpu.VMEM((seq, width), bf16),
        pltpu.VMEM((seq, width), bf16),
        pltpu.VMEM((2, width, width), bf16),
        pltpu.SemaphoreType.DMA((9 + 2 * pairs,)),
    ]
    params = dict(vmem_limit_bytes=VMEM_LIMIT)
    if nz:
        chunks = wup.shape[1] // width
        own, rows = wup.shape[0], wdown.shape[0]
        chip = (2, nz, 2, 2 * own)
        padded = 32
        groups = pairs // 2
        scratch += [
            pltpu.VMEM((16, width), f32),
            pltpu.VMEM((groups, 2) + chip + (3 * PAIR,), bf16),
            pltpu.VMEM((2,) + chip + (half,), bf16),
            pltpu.VMEM((2, chunks // 2) + chip + (width,), bf16),
            pltpu.VMEM((2, nz, 2, 2, rows, width), bf16),
            pltpu.VMEM((2, nz, 2, 2, 16, PAIR), bf16),
            pltpu.VMEM((groups, 2, padded, 3 * PAIR), bf16),
            pltpu.VMEM((2, padded, half), bf16),
            pltpu.VMEM((2, chunks // 2, padded, width), bf16),
            pltpu.VMEM((groups, padded, 3 * PAIR), bf16),
            pltpu.VMEM((padded, half), bf16),
            pltpu.VMEM((chunks // 2, padded, width), bf16),
            pltpu.SemaphoreType.DMA((9, 11)),
            pltpu.SemaphoreType.DMA((9, 11)),
        ]
        params.update(collective_id=0, has_side_effects=True)
        extra = [sds((groups, 2) + chip + (3 * PAIR,), bf16), sds((16, width), f32)]
    else:
        chunks = wup.shape[0]
        extra = []
    out_shape += [
        sds((chunks, width, width), bf16),
        sds((chunks, width, width), bf16),
        sds((2, width, half), bf16),
        sds((8, width), f32),
    ]
    return pl.pallas_call(
        functools.partial(forward_kernel, bool(nz)),
        in_specs=specs("svvvvvvv"),
        out_specs=specs("hhhhhhhhhhv" + "h" * len(extra)),
        out_shape=out_shape + extra,
        scratch_shapes=scratch,
        compiler_params=pltpu.CompilerParams(**params),
        name="layer_forward",
    )(lengths, tokens, cotangent, vecs, wqkv, wproj, wup, wdown)


def run_backward(lengths, tokens, vecs, proj, ot, lse, do, gmid, n1t, wqkv):
    seq, width = tokens.shape
    pairs = width // PAIR
    return pl.pallas_call(
        backward_kernel,
        in_specs=specs("svvhhhhhhv"),
        out_specs=specs("hhv"),
        out_shape=[
            sds((seq, width), bf16),
            sds((pairs, width, 3 * PAIR), bf16),
            sds((8, width), f32),
        ],
        scratch_shapes=[
            pltpu.VMEM((pairs, seq, 3 * PAIR), bf16),
            pltpu.VMEM((pairs, PAIR, seq), bf16),
            pltpu.VMEM((2 * pairs, 8, seq), f32),
            pltpu.VMEM((pairs, seq, PAIR), bf16),
            pltpu.VMEM((seq, width), f32),
            pltpu.VMEM((width, seq), bf16),
            pltpu.VMEM((pairs, width, 3 * PAIR), bf16),
            pltpu.VMEM((seq, width), bf16),
            pltpu.SemaphoreType.DMA((6 + pairs,)),
        ],
        compiler_params=pltpu.CompilerParams(vmem_limit_bytes=VMEM_LIMIT),
        name="attention_backward",
    )(lengths, tokens, vecs, proj, ot, lse, do, gmid, n1t, wqkv)


def gathered(item, axis=0):
    return lax.all_gather(item, AXES, axis=axis, tiled=True)


def scattered(item, axis=0):
    return lax.psum_scatter(item, AXES, scatter_dimension=axis, tiled=True)


def per_device(
    nz, tokens, cotangent, lengths, attn_gain, attn_shift, qkv_weight, qv_bias, proj_weight, proj_bias,
    mlp_gain, mlp_shift, up_weight, up_bias, down_weight, down_bias,
):
    seq, width = tokens.shape
    pairs = width // PAIR
    own = attn_gain.shape[0]
    chunks = up_weight.shape[1] // width
    small = jnp.stack([attn_gain, attn_shift, qv_bias[0], qv_bias[1], proj_bias, mlp_gain, mlp_shift, down_bias])
    if nz:
        vecs = jnp.concatenate(
            [
                jnp.pad(small, ((0, 0), (0, PAIR - own))),
                jnp.pad(up_bias[None], ((0, 7), (0, PAIR - up_bias.shape[0]))),
            ]
        )
        block_out, proj, ot, lse, do, gmid, n1t, gup, gdown, gproj, vg_one, wqkv, vecs = run_forward(
            nz, lengths, tokens, cotangent, vecs, qkv_weight, proj_weight, up_weight, down_weight
        )
        wqkv = wqkv.reshape(pairs, width, 3 * PAIR)
        many = width // own
    else:
        allvec = gathered(jnp.concatenate([small.reshape(-1), up_bias])[None])
        many = allvec.shape[0]
        table = allvec[:, : 8 * own].reshape(many, 8, own).transpose(1, 0, 2).reshape(8, width)
        vecs = jnp.concatenate([table, allvec[:, 8 * own :].reshape(chunks, width)], 0).astype(f32)
        wqkv = gathered(qkv_weight).reshape(width, 3, pairs, PAIR).transpose(2, 0, 1, 3).reshape(pairs, width, 3 * PAIR)
        wproj = gathered(proj_weight).reshape(width, 2, width // 2).transpose(1, 0, 2)
        wup = gathered(up_weight).reshape(width, chunks, width).transpose(1, 0, 2)
        wdown = gathered(down_weight).reshape(chunks, width, width)
        block_out, proj, ot, lse, do, gmid, n1t, gup, gdown, gproj, vg_one = run_forward(
            nz, lengths, tokens, cotangent, vecs, wqkv, wproj, wup, wdown
        )
    input_grad, gqkv, vg_two = run_backward(lengths, tokens, vecs, proj, ot, lse, do, gmid, n1t, wqkv)
    g_down = scattered(gdown.astype(f32).reshape(chunks * width, width))
    g_up = scattered(gup.astype(f32).transpose(1, 0, 2).reshape(width, chunks * width))
    g_proj = scattered(gproj.astype(f32).transpose(1, 0, 2).reshape(width, width))
    g_qkv = scattered(
        gqkv.astype(f32).reshape(pairs, width, 3, PAIR).transpose(1, 2, 0, 3).reshape(width, 3 * width)
    )
    rest = jnp.concatenate([vg_two[:4], vg_one[:4]], 0).reshape(8, many, own).transpose(1, 0, 2).reshape(many, -1)
    rest = jnp.concatenate([rest, vg_one[4:].reshape(many, -1)], 1)
    mine = scattered(rest)[0]
    v = mine[: 8 * own].reshape(8, own)
    return (
        block_out, input_grad, v[0], v[1], g_qkv, v[2:4], g_proj, v[6], v[4], v[5],
        g_up, mine[8 * own :], g_down, v[7],
    )


def chips_along_z(mesh):
    dp, shard = mesh.shape["dp"], mesh.shape["shard"]
    return shard // 4 if dp == 2 and shard == 16 else 0


def solution(mesh):
    one, two, mid = P(AXES), P(AXES, None), P(None, AXES)
    return jax.shard_map(
        functools.partial(per_device, chips_along_z(mesh)),
        mesh=mesh,
        in_specs=(two, two, one, one, one, two, mid, two, one, one, one, two, one, two, one),
        out_specs=(two, two, one, one, two, mid, two, one, one, one, two, one, two, one),
        check_vma=False,
    )
```

```python
import functools

import jax
import jax.numpy as jnp
from jax import lax
from jax.experimental import pallas as pl
from jax.experimental.pallas import tpu as pltpu
from jax.sharding import PartitionSpec as P

f32 = jnp.float32
bf16 = jnp.bfloat16
HD = 64
PAIR = 2 * HD
EPS = 1e-06
MASKED = -1e30
AXES = ("dp", "shard")
VMEM_LIMIT = 63 * 2**20

AG, AS, QB, VB, PB, MG, MS, DB, UB = range(9)


def dg(a, b, ca, cb):
    return lax.dot_general(a, b, (((ca,), (cb,)), ((), ())), preferred_element_type=f32)


def rows_of(v):
    return v.reshape(-1, v.shape[-1])


def norm_parts(v):
    center = v - jnp.mean(v, -1, keepdims=True)
    inv = lax.rsqrt(jnp.mean(center * center, -1, keepdims=True) + EPS)
    return center * inv, inv


def norm_back(n, inv, z):
    return inv * (z - jnp.mean(z, -1, keepdims=True) - n * jnp.mean(z * n, -1, keepdims=True))


def key_bias(length, seq):
    return jnp.where(lax.broadcasted_iota(jnp.int32, (seq, 1), 0) < length, 0.0, MASKED).astype(f32)


def head_only(v, hh):
    lane = lax.broadcasted_iota(jnp.int32, (1, PAIR), 1)
    return jnp.where(lane // HD == hh, v, jnp.zeros((), v.dtype))


class Place:
    def __init__(self, nz):
        shard = lax.axis_index("shard")
        self.nz = nz
        self.y = lax.axis_index("dp")
        self.c = lax.rem(shard, 2)
        self.x = lax.rem(lax.div(shard, 2), 2)
        self.z = lax.div(shard, 4)
        fy, fx = 1 - 2 * self.y, 1 - 2 * self.x
        self.ay, self.ax = self.y + (1 - self.c) * fy, self.x + self.c * fx
        self.by, self.bx = self.y + self.c * fy, self.x + (1 - self.c) * fx

    def device(self, y, z, x, c):
        return (y, (z * 2 + x) * 2 + c)

    def peer(self):
        return self.device(self.y, self.z, self.x, 1 - self.c)

    def along_z(self, k):
        return self.device(self.y, lax.rem(self.z + k, self.nz), self.x, self.c)

    def a(self):
        return self.device(self.ay, self.z, self.ax, self.c)

    def b(self):
        return self.device(self.by, self.z, self.bx, self.c)

    def partners(self):
        return [self.peer(), self.a(), self.b()] + [self.along_z(k) for k in range(1, self.nz)]


def enter(place):
    barrier = pltpu.get_barrier_semaphore()
    partners = place.partners()
    for d in partners:
        pl.semaphore_signal(barrier, inc=1, device_id=d, device_id_type=pl.DeviceIdType.MESH)
    pl.semaphore_wait(barrier, len(partners))


def remote(src, dst, send, recv, device):
    return pltpu.make_async_remote_copy(
        src_ref=src, dst_ref=dst, send_sem=send, recv_sem=recv, device_id=device,
        device_id_type=pl.DeviceIdType.MESH,
    )


class Gather:
    def __init__(self, place, block, column, swap, send, recv):
        self.p, self.block, self.column, self.swap = place, block, column, swap
        self.send, self.recv = send, recv
        self.started = []

    def move(self, slot, src, dst, device):
        return remote(src, dst, self.send.at[slot], self.recv.at[slot], device)

    def go(self, copy):
        copy.start()
        self.started.append(copy)

    def exchange(self):
        src, dst, _ = self.swap
        return self.move(0, src, dst, self.p.peer())

    def X(self):
        self.go(self.exchange())

    def zs(self):
        p = self.p
        own = self.block(p.y, p.z, p.x, p.c)
        return [self.move(k, own, own, p.along_z(k)) for k in range(1, p.nz)]

    def over(self, slot, y, x, device):
        v = self.column(y, x, self.p.c)
        return self.move(slot, v, v, device)

    def to_b(self):
        return self.over(4, self.p.y, self.p.x, self.p.b())

    def to_a(self, second):
        p = self.p
        y, x = (p.by, p.bx) if second else (p.y, p.x)
        return self.over(5 + second, y, x, p.a())

    def across(self, i):
        p = self.p
        y, x = [(p.y, p.x), (p.by, p.bx), (p.ay, p.ax), (1 - p.y, 1 - p.x)][i]
        return self.over(7 + i, y, x, p.peer())

    def Z(self):
        if self.swap is not None:
            self.exchange().wait_recv()
            self.swap[2]()
        for cp in self.zs():
            self.go(cp)

    def B(self):
        for cp in self.zs():
            cp.wait_recv()
        self.go(self.to_b())
        self.go(self.to_a(0))
        self.go(self.across(0))

    def A(self):
        self.to_b().wait_recv()
        self.go(self.to_a(1))
        self.go(self.across(1))

    def C(self):
        self.to_a(0).wait_recv()
        self.go(self.across(2))
        self.to_a(1).wait_recv()
        self.go(self.across(3))

    def D(self):
        for i in range(4):
            self.across(i).wait_recv()

    def finish(self):
        if self.swap is not None:
            self.exchange().wait_send()
        for cp in self.zs() + [self.to_b(), self.to_a(0), self.to_a(1)] + [self.across(i) for i in range(4)]:
            cp.wait_send()


class Scatter:
    def __init__(self, place, half, own, load, bufs, send, recv, local, finish):
        self.p, self.half, self.own, self.load = place, half, own, load
        self.r0, self.r1, self.r2, self.r3 = bufs
        self.send, self.recv, self.local, self.finish = send, recv, local, finish

    def move(self, slot, src, dst, device):
        return remote(src, dst, self.send.at[slot], self.recv.at[slot], device)

    def swap(self):
        return self.move(0, self.half(1 - self.p.c), self.r0, self.p.peer())

    def to_a(self, i):
        p = self.p
        src = self.own.at[p.ay, :, p.ax] if i == 0 else self.own.at[1 - p.y, :, 1 - p.x]
        return self.move(1 + i, src, self.r1.at[i], p.a())

    def to_b(self):
        p = self.p
        return self.move(3, self.own.at[p.by, :, p.bx], self.r2, p.b())

    def to_z(self, k):
        p = self.p
        return self.move(3 + k, self.own.at[p.y, lax.rem(p.z + k, p.nz), p.x], self.r3.at[k - 1], p.along_z(k))

    def loaded(self):
        return pltpu.make_async_copy(self.half(self.p.c), self.own, self.local)

    def add(self, y, x, other):
        self.own[y, :, x] = (self.own[y, :, x].astype(f32) + other.astype(f32)).astype(bf16)

    def S0(self):
        self.swap().start()
        if self.load:
            self.loaded().start()

    def S1(self):
        p = self.p
        if self.load:
            self.loaded().wait()
        self.swap().wait_recv()
        for i, (y, x) in enumerate([(p.ay, p.ax), (1 - p.y, 1 - p.x), (p.by, p.bx), (p.y, p.x)]):
            self.add(y, x, self.r0[y, :, x])
            if i < 2:
                self.to_a(i).start()

    def S2(self):
        p = self.p
        self.to_a(1).wait_recv()
        self.add(p.by, p.bx, self.r1[1])
        self.to_b().start()
        self.to_a(0).wait_recv()
        self.add(p.y, p.x, self.r1[0])

    def S3(self):
        p = self.p
        self.to_b().wait_recv()
        self.add(p.y, p.x, self.r2[...])
        for k in range(1, p.nz):
            self.to_z(k).start()

    def S4(self):
        p = self.p
        total = self.own[p.y, p.z, p.x].astype(f32)
        for k in range(1, p.nz):
            self.to_z(k).wait_recv()
            total += self.r3[k - 1].astype(f32)
        self.finish(total)

    def end(self):
        for cp in [self.swap(), self.to_a(0), self.to_a(1), self.to_b()] + [
            self.to_z(k) for k in range(1, self.p.nz)
        ]:
            cp.wait_send()


class Handover:
    def __init__(self, place, stage, landing, write, send, recv):
        self.p, self.stage, self.landing, self.write = place, stage, landing, write
        self.copy = remote(stage, landing, send, recv, place.peer())

    def start(self, total):
        own = total.shape[0] // 2
        top, bottom = total[:own], total[own:]
        self.stage[...] = jnp.where(self.p.c == 0, bottom, top)
        self.copy.start()
        self.write(self.p.c, jnp.where(self.p.c == 0, top, bottom))

    def S5(self):
        self.copy.wait_recv()
        self.write(1 - self.p.c, self.landing[...])

    def end(self):
        self.copy.wait_send()


class VectorSum:
    def __init__(self, place, value, bufs, send, recv):
        self.p, self.value, self.bufs, self.send, self.recv = place, value, bufs, send, recv

    def move(self, slot):
        p = self.p
        device = [p.peer(), p.a(), p.b()][slot] if slot < 3 else p.along_z(slot - 2)
        return remote(
            self.value.at[min(slot, 3)], self.bufs.at[slot], self.send.at[slot], self.recv.at[slot], device
        )

    def S0(self):
        self.move(0).start()

    def step(self, slot):
        self.move(slot - 1).wait_recv()
        self.value[slot] = self.value[slot - 1] + self.bufs[slot - 1]
        for k in range(self.p.nz - 1 if slot == 3 else 1):
            self.move(slot + k).start()

    def S1(self):
        self.step(1)

    def S2(self):
        self.step(2)

    def S3(self):
        self.step(3)

    def S4(self):
        total = self.value[3]
        for k in range(self.p.nz - 1):
            self.move(3 + k).wait_recv()
            total += self.bufs[3 + k]
        self.value[4] = total

    def end(self):
        for slot in range(2 + self.p.nz):
            self.move(slot).wait_send()


def expand_table(vbuf, vec, own, ff_own):
    many = vbuf.shape[0] * vbuf.shape[1] * vbuf.shape[2] * vbuf.shape[3]
    width = vec.shape[1]
    ff = many * ff_own
    flat = vbuf[...].reshape(many * 16, PAIR)

    def spread(n, each):
        lane = lax.broadcasted_iota(jnp.int32, (PAIR, n), 1)
        return (lax.rem(lane, each) == lax.broadcasted_iota(jnp.int32, (PAIR, n), 0)).astype(f32).astype(bf16)

    full = dg(flat, spread(width, own), 1, 0).reshape(many, 16, width)
    where = lax.broadcasted_iota(jnp.int32, (many, 1, width), 2) - own * lax.broadcasted_iota(
        jnp.int32, (many, 1, width), 0
    )
    vec[0:16, :] = jnp.sum(jnp.where((where >= 0) & (where < own), full, 0.0), 0)
    pick = (
        lax.broadcasted_iota(jnp.int32, (many, many * 16), 1)
        == 16 * lax.broadcasted_iota(jnp.int32, (many, many * 16), 0) + 8
    )
    row = dg(pick.astype(f32).astype(bf16), flat, 1, 0).astype(bf16)
    full = dg(row, spread(ff, ff_own), 1, 0)
    where = lax.broadcasted_iota(jnp.int32, (many, ff), 1) - ff_own * lax.broadcasted_iota(jnp.int32, (many, ff), 0)
    up = jnp.sum(jnp.where((where >= 0) & (where < ff_own), full, 0.0), 0, keepdims=True)
    for j in range(ff // width):
        vec[UB + j : UB + j + 1, :] = up[:, j * width : (j + 1) * width]


def gather_items(place, own_down, wqkv, wproj, wup, wdown, vbuf, xs, xr, send, recv):
    p = place
    (xs_qkv, xs_proj, xs_up), (xr_qkv, xr_proj, xr_up) = xs, xr
    own = wqkv.shape[-2] // 2

    def joined(mine, theirs, write):
        def go():
            m, t = mine()[:own].astype(f32), theirs()[:own].astype(f32)
            lo, hi = jnp.where(p.c == 0, m, t), jnp.where(p.c == 0, t, m)
            write(jnp.concatenate([lo, hi], 0).astype(bf16))
        return go

    items = []

    def add(block, column, swap):
        i = len(items)
        items.append(Gather(p, block, column, swap, send.at[i], recv.at[i]))

    add(lambda y, z, x, c: vbuf.at[y, z, x, c], lambda y, x, c: vbuf.at[y, :, x, c], None)

    def add_swapped(view, xs_of, xr_of):
        block = lambda y, z, x, c: view(c).at[y, z, x]
        column = lambda y, x, c: view(c).at[y, :, x]

        def write(v):
            view(p.c)[p.y, p.z, p.x] = v

        add(block, column, (xs_of(1 - p.c), xr_of, joined(lambda: xs_of(p.c)[...], lambda: xr_of[...], write)))

    for g in range(wqkv.shape[0]):
        add_swapped(lambda c, g=g: wqkv.at[g, c], lambda c, g=g: xs_qkv.at[g, c], xr_qkv.at[g])
    add_swapped(lambda c: wproj.at[c], lambda c: xs_proj.at[c], xr_proj)
    part = wdown.shape[-2] // 2
    for k in range(2):
        rows = pl.ds(k * part, part)
        add(
            lambda y, z, x, c, rows=rows: wdown.at[y, z, x, c, rows],
            lambda y, x, c, rows=rows: wdown.at[y, :, x, c, rows],
            None,
        )
    for k in range(2):
        add_swapped(lambda c, k=k: wup.at[c, k], lambda c, k=k: xs_up.at[c, k], xr_up.at[k])
    return items


VECI, G0, G1, G2, PROJ, D0, D1, U0, U1 = range(9)
FORWARD_PLAN = {
    "start": "",
    "stats": [("B", VECI), ("B", G0), ("Z", G1), ("A", VECI), ("A", G0), ("B", G1), ("Z", G2),
              ("C", VECI), ("C", G0), ("A", G1), ("B", G2), ("Z", PROJ), ("D", VECI)],
    "norm": [("D", G0), ("C", G1), ("A", G2), ("B", PROJ), ("Z", D0)],
    0: [("C", G2), ("A", PROJ), ("B", D0), ("Z", D1)],
    1: [("D", G1), ("C", PROJ), ("A", D0), ("B", D1), ("Z", U0)],
    2: [("C", D0), ("A", D1), ("B", U0), ("Z", U1)],
    3: [("D", G2), ("C", D1), ("A", U0), ("B", U1)],
    4: [("C", U0), ("A", U1)],
    5: [("C", U1), ("D", PROJ)],
    "branch": [("D", D0), ("D", D1), ("D", U0)],
    "mlp": [("D", U1)],
}


def forward_kernel(
    comm, len_ref, tok_ref, cot_ref, vec_in, wqkv_in, wproj_in, wup_in, wdown_in,
    out_hbm, proj_hbm, ot_hbm, lse_hbm, do_hbm, gmid_hbm, n1t_hbm, gup_hbm, gdown_hbm, gproj_hbm, vg_ref, *rest,
):
    seq, width = tok_ref.shape
    chunks = gup_hbm.shape[0]
    if comm:
        wqkv_hbm, vec_hbm = rest[:2]
        rest = rest[2:]
    n1, n1t, proj, ot, att, lse, res, n2, n2t, acc, gn2, act, gh, gstage, sems = rest[:15]
    pairs = proj.shape[0]
    copies = []

    def send_out(src, dst, sem):
        cp = pltpu.make_async_copy(src, dst, sem)
        cp.start()
        return cp

    if comm:
        vec_ref, wqkv, wproj, wup, wdown, vbuf, xs_qkv, xs_proj, xs_up, xr_qkv, xr_proj, xr_up, send, recv = rest[15:]
        place = Place(wqkv.shape[3])
        own = wqkv_in.shape[0]
        items = gather_items(
            place, wdown_in, wqkv, wproj, wup, wdown, vbuf, (xs_qkv, xs_proj, xs_up), (xr_qkv, xr_proj, xr_up),
            send, recv,
        )

        def w_qkv(p):
            return rows_of(wqkv[lax.div(p, 2), lax.rem(p, 2)])

        def w_up(j):
            return rows_of(wup[j // 2, j % 2])

        def w_down(j):
            zs = wdown.shape[1] // 2
            return rows_of(wdown[j // 2, zs * (j % 2) : zs * (j % 2) + zs])

        def w_proj(i):
            return rows_of(wproj[i])

        def tick(name):
            for step, i in FORWARD_PLAN[name]:
                getattr(items[i], step)()

        order = (0, 2, 1, 3)
    else:
        vec_ref = vec_in

        def w_qkv(p):
            return wqkv_in[p]

        def w_up(j):
            return wup_in[j]

        def w_down(j):
            return wdown_in[j]

        def w_proj(i):
            return wproj_in[i]

        def tick(name):
            pass

        order = range(chunks)

    def vec(i):
        return vec_ref[i : i + 1, :]

    rb = 256
    if comm:
        half = width // 2
        vbuf[place.y, place.z, place.x, place.c] = vec_in[...]
        wdown[place.y, place.z, place.x, place.c] = wdown_in[...]
        for p in range(pairs):
            for t in range(3):
                lanes = slice(t * width + p * PAIR, t * width + (p + 1) * PAIR)
                xs_qkv[p // 2, p % 2, 0:own, t * PAIR : (t + 1) * PAIR] = wqkv_in[:, lanes]
        for i in range(2):
            xs_proj[i, 0:own, :] = wproj_in[:, i * half : (i + 1) * half]
        for j in range(chunks):
            xs_up[j // 2, j % 2, 0:own, :] = wup_in[:, j * width : (j + 1) * width]
        enter(place)
        for i in (G0, G1, G2, PROJ, U0, U1):
            items[i].X()
        items[VECI].Z()
        items[G0].Z()

    @pl.loop(0, seq // rb)
    def _(r):
        sl = pl.ds(pl.multiple_of(r * rb, rb), rb)
        n, _inv = norm_parts(tok_ref[sl, :].astype(f32))
        res[sl, :] = n

    tick("stats")
    if comm:
        expand_table(vbuf, vec_ref, own, wdown_in.shape[0])
        copies_late = [send_out(vec_ref, vec_hbm, sems.at[8 + pairs])]

    @pl.loop(0, seq // rb)
    def _(r):
        sl = pl.ds(pl.multiple_of(r * rb, rb), rb)
        n1[sl, :] = (res[sl, :] * vec(AG) + vec(AS)).astype(bf16)

    n1t[...] = n1[...].T
    copies.append(send_out(n1t, n1t_hbm, sems.at[0]))
    tick("norm")

    bias_k = key_bias(len_ref[0], seq)
    ones = jnp.ones((16, seq), bf16)
    qv_bias = [(vec(QB)[:, i * PAIR : (i + 1) * PAIR], vec(VB)[:, i * PAIR : (i + 1) * PAIR]) for i in range(pairs)]

    def pick(p, choices):
        v = choices[0]
        for i in range(1, pairs):
            v = jnp.where(p == i, choices[i], v)
        return v

    @pl.loop(0, pairs)
    def _(p):
        qkv = dg(n1[...], w_qkv(p), 1, 0)
        proj[p, :, 0:PAIR] = (qkv[:, 0:PAIR] + pick(p, [q for q, v in qv_bias])).astype(bf16)
        proj[p, :, PAIR : 2 * PAIR] = qkv[:, PAIR : 2 * PAIR].astype(bf16)
        proj[p, :, 2 * PAIR :] = (qkv[:, 2 * PAIR :] + pick(p, [v for q, v in qv_bias])).astype(bf16)
        k2 = proj[p, :, PAIR : 2 * PAIR]
        v2t = proj[p, :, 2 * PAIR :].T
        q2 = proj[p, :, 0:PAIR] * jnp.asarray(HD**-0.5, bf16)
        for hh in range(2):
            rows = slice(HD * hh, HD * hh + HD)
            s = dg(k2, head_only(q2, hh), 1, 1) + bias_k
            top = jnp.max(s, 0, keepdims=True)
            e = jnp.exp(s - top).astype(bf16)
            o = dg(jnp.concatenate([v2t[rows], ones], 0), e, 1, 0)
            total = o[HD : HD + 1]
            ot[p, rows, :] = (o[:HD] / total).astype(bf16)
            lse[2 * p + hh] = jnp.broadcast_to(top + jnp.log(total), (8, seq))
        if comm:
            for i in range(pairs):

                @pl.when(p == i)
                def _(i=i):
                    tick(i)

    if comm:
        for g in range(wqkv.shape[0]):
            for c in range(2):
                copies_late.append(
                    send_out(wqkv.at[g, c], wqkv_hbm.at[g, c], sems.at[9 + pairs + 2 * g + c])
                )
    for p in range(pairs):
        att[:, p * PAIR : (p + 1) * PAIR] = ot[p].T
    copies.append(send_out(proj, proj_hbm, sems.at[1]))
    copies.append(send_out(ot, ot_hbm, sems.at[2]))
    copies.append(send_out(lse, lse_hbm, sems.at[3]))

    half = width // 2

    @pl.loop(0, seq // rb)
    def _(r):
        sl = pl.ds(pl.multiple_of(r * rb, rb), rb)
        a = att[sl, :]
        branch = jnp.concatenate([dg(a, w_proj(i), 1, 0) for i in range(2)], 1)
        v = tok_ref[sl, :].astype(f32) + branch + vec(PB)
        res[sl, :] = v
        acc[sl, :] = v + vec(DB)
        gn2[sl, :] = jnp.zeros((rb, width), f32)
        n, _inv = norm_parts(v)
        n2[sl, :] = (n * vec(MG) + vec(MS)).astype(bf16)

    n2t[...] = n2[...].T
    tick("branch")

    rm = 512
    for turn, j in enumerate(order):
        if turn == 2:
            tick("mlp")
        vg_ref[4 + j : 5 + j, :] = jnp.zeros((1, width), f32)

        @pl.loop(0, seq // rm)
        def _(r, j=j):
            sl = pl.ds(pl.multiple_of(r * rm, rm), rm)
            h = dg(n2[sl, :], w_up(j), 1, 0) + vec(UB + j)
            phi = 0.5 * (1.0 + lax.erf(h * 0.7071067811865476))
            a = (h * phi).astype(bf16)
            act[sl, :] = a
            acc[sl, :] += dg(a, w_down(j), 1, 0)
            ga = dg(cot_ref[sl, :], w_down(j), 1, 1)
            g = (ga * (phi + h * jnp.exp(-0.5 * h * h) * 0.3989422804014327)).astype(bf16)
            gh[sl, :] = g
            gn2[sl, :] += dg(g, w_up(j), 1, 1)
            vg_ref[4 + j : 5 + j, :] += jnp.sum(g.astype(f32), 0, keepdims=True)

        if turn > 0:
            copies[-1].wait()
            copies[-2].wait()
            del copies[-2:]
        gstage[0] = dg(act[...], cot_ref[...], 0, 0).astype(bf16)
        copies.append(send_out(gstage.at[0], gdown_hbm.at[j], sems.at[4]))
        gstage[1] = dg(n2t[...], gh[...], 1, 0).astype(bf16)
        copies.append(send_out(gstage.at[1], gup_hbm.at[j], sems.at[5]))

    vg_ref[0:4, :] = jnp.zeros((4, width), f32)

    @pl.loop(0, seq // rb)
    def _(r):
        sl = pl.ds(pl.multiple_of(r * rb, rb), rb)
        n2[sl, :] = acc[sl, :].astype(bf16)
        g = gn2[sl, :]
        n, inv = norm_parts(res[sl, :])
        cot = cot_ref[sl, :].astype(f32)
        mid = cot + norm_back(n, inv, g * vec(MG))
        acc[sl, :] = mid
        low = mid.astype(bf16)
        act[sl, :] = low
        vg_ref[0:1, :] += jnp.sum(g * n, 0, keepdims=True)
        vg_ref[1:2, :] += jnp.sum(g, 0, keepdims=True)
        vg_ref[2:3, :] += jnp.sum(low.astype(f32), 0, keepdims=True)
        vg_ref[3:4, :] += jnp.sum(cot, 0, keepdims=True)
        back = dg(low[:, :half], w_proj(0), 1, 1) + dg(low[:, half:], w_proj(1), 1, 1)
        gh[sl, :] = back.astype(bf16)

    last = [copies.pop(), copies.pop()]
    copies.append(send_out(n2, out_hbm, sems.at[6]))
    copies.append(send_out(acc, gmid_hbm, sems.at[7]))
    for p in range(pairs):
        copies.append(send_out(gh.at[:, p * PAIR : (p + 1) * PAIR], do_hbm.at[p], sems.at[8 + p]))
    for cp in last:
        cp.wait()
    for i in range(2):
        gstage[i, :, :half] = dg(rows_of(ot[...]), act[:, i * half : (i + 1) * half], 1, 0).astype(bf16)
        copies.append(send_out(gstage.at[i, :, pl.ds(0, half)], gproj_hbm.at[i], sems.at[4 + i]))
    if comm:
        copies += copies_late
        for item in items:
            item.finish()
    for cp in copies:
        cp.wait()


def slice_lanes(v, first, count):
    lane = lax.broadcasted_iota(jnp.int32, (v.shape[1], PAIR), 0) - first
    out = lax.broadcasted_iota(jnp.int32, (v.shape[1], PAIR), 1)
    pick = ((lane == out) & (out < count)).astype(f32)
    return lax.dot_general(
        v, pick, (((1,), (0,)), ((), ())), precision=lax.Precision.HIGHEST, preferred_element_type=f32
    )


SV1, SD0, SD1, SU0, SU1, SP, SG0, SG1, SG2, SV2 = range(10)
BACKWARD_PLAN = {
    "start": [("S0", SD0), ("S0", SD1), ("S0", SU0), ("S0", SU1), ("S0", SP), ("S0", SV1)],
    "loaded": [("S1", SD0), ("S1", SV1)],
    0: [("S2", SD0), ("S1", SD1), ("S2", SV1)],
    1: [("S0", SG0), ("S3", SD0), ("S2", SD1), ("S1", SU0), ("S3", SV1)],
    2: [("S4", SD0), ("S3", SD1), ("S2", SU0), ("S1", SU1), ("S4", SV1)],
    3: [("S0", SG1), ("S4", SD1), ("S3", SU0), ("S2", SU1), ("S1", SP)],
    4: [("S4", SU0), ("S3", SU1), ("S2", SP), ("S1", SG0)],
    5: [("S0", SG2), ("S5", SU0), ("S4", SU1), ("S3", SP), ("S2", SG0), ("S1", SG1)],
    "rows0": [("S1", SG2), ("S5", SU1), ("S4", SP), ("S3", SG0), ("S2", SG1)],
    "rows1": [("S2", SG2), ("S5", SP), ("S4", SG0), ("S3", SG1)],
    "rows2": [("S3", SG2), ("S5", SG0), ("S4", SG1)],
    "rows3": [("S0", SV2), ("S4", SG2), ("S5", SG1)],
    "end": [("S1", SV2), ("S2", SV2), ("S3", SV2), ("S5", SG2), ("S4", SV2)],
}


def backward_kernel(
    comm, len_ref, tok_ref, vec_ref, proj_hbm, ot_hbm, lse_hbm, do_hbm, gmid_hbm, n1t_hbm, wqkv_ref, *rest
):
    if comm:
        gup_hbm, gdown_hbm, gproj_hbm, vg_in = rest[:4]
        gin_hbm, oqkv, oproj, oup, odown, vg_out = rest[4:10]
        proj, ot, lse, do, gmid, n1t, gqkv, gin, sems, vsum = rest[10:20]
        (aup, adown, aproj, b_up, b_down, b_proj, b_qkv, stage_up, stage_proj, stage_qkv,
         land_up, land_proj, land_qkv, vbufs, send, recv, hsend, hrecv, local) = (
            rest[20:23] + (rest[23:27], rest[27:31], rest[31:35], rest[35:39]) + rest[39:]
        )
        vg_ref = vsum.at[1, 0]
    else:
        gin_hbm, gqkv_hbm, vg_ref = rest[:3]
        proj, ot, lse, do, gmid, n1t, gqkv, gin, sems = rest[3:]
    seq, width = tok_ref.shape
    pairs = proj.shape[0]
    half = width // 2

    def start(src, dst, sem):
        cp = pltpu.make_async_copy(src, dst, sem)
        cp.start()
        return cp

    loads = [
        start(proj_hbm, proj, sems.at[0]),
        start(do_hbm, do, sems.at[1]),
        start(ot_hbm, ot, sems.at[2]),
        start(lse_hbm, lse, sems.at[3]),
        start(n1t_hbm, n1t, sems.at[4]),
        start(gmid_hbm, gmid, sems.at[5]),
    ]

    if comm:
        place = Place(gqkv.shape[3])
        p_ = place
        items = {}
        handovers = {}

        def bufs_of(b, k):
            return tuple(r.at[k] for r in b)

        def add(i, half_of, own, load, bufs, finish):
            items[i] = Scatter(p_, half_of, own, load, bufs, send.at[i], recv.at[i], local.at[i], finish)

        def add_shared(i, half_of, own, load, bufs, stage, landing, write):
            h = Handover(p_, stage, landing, write, hsend.at[i], hrecv.at[i])
            handovers[i] = h
            add(i, half_of, own, load, bufs, h.start)
            items[i].S5 = h.S5

        part = odown.shape[0] // 2
        for k in range(2):
            rows = slice(k * part, (k + 1) * part)

            def write_down(total, rows=rows):
                odown[rows, :] = total

            add(
                SD0 + k, lambda c, k=k: gdown_hbm.at[:, :, :, c, pl.ds(k * part, part)], adown.at[k], True,
                bufs_of(b_down, k), write_down,
            )

            def write_up(c, v, k=k):
                oup[:, pl.ds(pl.multiple_of((2 * c + k) * width, PAIR), width)] = v

            add_shared(
                SU0 + k, lambda c, k=k: gup_hbm.at[c, k], aup.at[k], True, bufs_of(b_up, k),
                stage_up.at[k], land_up.at[k], write_up,
            )

        def write_proj(c, v):
            oproj[:, pl.ds(pl.multiple_of(c * half, PAIR), half)] = v

        add_shared(
            SP, lambda c: gproj_hbm.at[c], aproj, True, b_proj, stage_proj, land_proj, write_proj,
        )
        for g in range(pairs // 2):

            def write_qkv(c, v, g=g):
                for t in range(3):
                    oqkv[:, pl.ds(pl.multiple_of(t * width + (2 * g + c) * PAIR, PAIR), PAIR)] = v[
                        :, t * PAIR : (t + 1) * PAIR
                    ]

            add_shared(
                SG0 + g, lambda c, g=g: gqkv.at[g, c], gqkv.at[g, p_.c], False, bufs_of(b_qkv, g),
                stage_qkv.at[g], land_qkv.at[g], write_qkv,
            )
        for i, v in ((SV1, 0), (SV2, 1)):
            items[i] = VectorSum(p_, vsum.at[v], vbufs.at[v], send.at[i], recv.at[i])
        vsum[0, 0] = vg_in[...]
        enter(place)

        def tick(name):
            for step, i in BACKWARD_PLAN[name]:
                getattr(items[i], step)()
    else:

        def tick(name):
            pass

    tick("start")
    for cp in loads:
        cp.wait()
    vg_ref[...] = jnp.zeros(vg_ref.shape, f32)
    tick("loaded")

    bias_k = key_bias(len_ref[0], seq)
    qb = 512
    scale = HD**-0.5

    def weight_gradient(p):
        cols = slice(p * PAIR, (p + 1) * PAIR)
        g = proj[p]
        sums = jnp.sum(g.astype(f32), 0, keepdims=True)
        vg_ref[2:3, cols] = sums[:, 0:PAIR]
        vg_ref[3:4, cols] = sums[:, 2 * PAIR :]
        v = dg(n1t[...], g, 1, 0).astype(bf16)
        if comm:
            gqkv[p // 2, p % 2] = v.reshape(gqkv.shape[2:])
        else:
            gqkv[p] = v

    @pl.loop(0, pairs)
    def _(p):
        k2 = proj[p, :, PAIR : 2 * PAIR]
        v2 = proj[p, :, 2 * PAIR :]
        k2t = k2.T
        dk = dv = None
        dqt = []
        for hh in range(2):
            rows = slice(HD * hh, HD * hh + HD)
            parts = []
            for i in range(seq // qb):
                sl = slice(i * qb, (i + 1) * qb)
                qm = head_only(proj[p, sl, 0:PAIR] * jnp.asarray(scale, bf16), hh)
                d = do[p, sl, :]
                dm = head_only(d, hh)
                dt = d.astype(f32).T[rows]
                delta = jnp.sum(dt * ot[p, rows, sl].astype(f32), 0, keepdims=True)
                e = jnp.exp(dg(k2, qm, 1, 1) + bias_k - lse[2 * p + hh, 0:1, sl])
                ds = (e * (dg(v2, dm, 1, 1) - delta)).astype(bf16)
                t = dg(e.astype(bf16), dm, 1, 0)
                dv = t if dv is None else dv + t
                t = dg(ds, qm, 1, 0)
                dk = t if dk is None else dk + t
                parts.append(dg(k2t[rows], ds, 1, 0) * scale)
            dqt.append(jnp.concatenate(parts, 1))
        proj[p, :, 0:PAIR] = jnp.concatenate(dqt, 0).T.astype(bf16)
        proj[p, :, PAIR : 2 * PAIR] = dk.astype(bf16)
        proj[p, :, 2 * PAIR :] = dv.astype(bf16)
        for i in range(pairs):

            @pl.when(p == i)
            def _(i=i):
                if i % 2 == 1:
                    weight_gradient(i - 1)
                    weight_gradient(i)
                tick(i)

    outs = []
    if not comm:
        outs = [start(gqkv.at[p], gqkv_hbm.at[p], sems.at[6 + p]) for p in range(pairs)]

    rb = seq // 4

    @pl.loop(0, 4)
    def _(r):
        sl = pl.ds(pl.multiple_of(r * rb, rb), rb)
        g = dg(proj[0, sl, :], wqkv_ref[0], 1, 1)
        for p in range(1, pairs):
            g += dg(proj[p, sl, :], wqkv_ref[p], 1, 1)
        n, inv = norm_parts(tok_ref[sl, :].astype(f32))
        gin[sl, :] = (gmid[sl, :] + norm_back(n, inv, g * vec_ref[AG : AG + 1, :])).astype(bf16)
        vg_ref[0:1, :] += jnp.sum(g * n, 0, keepdims=True)
        vg_ref[1:2, :] += jnp.sum(g, 0, keepdims=True)
        for i in range(4):

            @pl.when(r == i)
            def _(i=i):
                tick(f"rows{i}")

    outs.append(start(gin, gin_hbm, sems.at[0]))
    tick("end")
    if comm:
        own, rows = oqkv.shape[0], odown.shape[0]
        index = ((place.y * place.nz + place.z) * 2 + place.x) * 2 + place.c
        each = width // rows
        one, two = vsum[0, 4], vsum[1, 4]
        vg_out[0:8, :] = slice_lanes(one, index * own, own)
        up = slice_lanes(one, lax.rem(index, each) * rows, rows)
        row = lax.broadcasted_iota(jnp.int32, up.shape, 0)
        vg_out[4:5, :] = jnp.sum(jnp.where(row == 4 + lax.div(index, each), up, 0.0), 0, keepdims=True)
        vg_out[8:16, :] = slice_lanes(two, index * own, own)
        for i in items:
            items[i].end()
        for i in handovers:
            handovers[i].end()
    for cp in outs:
        cp.wait()


def specs(kinds):
    table = {"s": pltpu.SMEM, "v": pltpu.VMEM, "h": pl.ANY}
    return [pl.BlockSpec(memory_space=table[k]) for k in kinds]


def sds(shape, dtype):
    return jax.ShapeDtypeStruct(shape, dtype)


def run_forward(nz, lengths, tokens, cotangent, vecs, wqkv, wproj, wup, wdown):
    seq, width = tokens.shape
    pairs = width // PAIR
    half = width // 2
    out_shape = [
        sds((seq, width), bf16),
        sds((pairs, seq, 3 * PAIR), bf16),
        sds((pairs, PAIR, seq), bf16),
        sds((2 * pairs, 8, seq), f32),
        sds((pairs, seq, PAIR), bf16),
        sds((seq, width), f32),
        sds((width, seq), bf16),
    ]
    scratch = [
        pltpu.VMEM((seq, width), bf16),
        pltpu.VMEM((width, seq), bf16),
        pltpu.VMEM((pairs, seq, 3 * PAIR), bf16),
        pltpu.VMEM((pairs, PAIR, seq), bf16),
        pltpu.VMEM((seq, width), bf16),
        pltpu.VMEM((2 * pairs, 8, seq), f32),
        pltpu.VMEM((seq, width), f32),
        pltpu.VMEM((seq, width), bf16),
        pltpu.VMEM((width, seq), bf16),
        pltpu.VMEM((seq, width), f32),
        pltpu.VMEM((seq, width), f32),
        pltpu.VMEM((seq, width), bf16),
        pltpu.VMEM((seq, width), bf16),
        pltpu.VMEM((2, width, width), bf16),
        pltpu.SemaphoreType.DMA((9 + 2 * pairs,)),
    ]
    params = dict(vmem_limit_bytes=VMEM_LIMIT)
    if nz:
        chunks = wup.shape[1] // width
        own, rows = wup.shape[0], wdown.shape[0]
        chip = (2, nz, 2, 2 * own)
        padded = -(-own // 16) * 16
        groups = pairs // 2
        scratch += [
            pltpu.VMEM((16, width), f32),
            pltpu.VMEM((groups, 2) + chip + (3 * PAIR,), bf16),
            pltpu.VMEM((2,) + chip + (half,), bf16),
            pltpu.VMEM((2, chunks // 2) + chip + (width,), bf16),
            pltpu.VMEM((2, nz, 2, 2, rows, width), bf16),
            pltpu.VMEM((2, nz, 2, 2, 16, PAIR), bf16),
            pltpu.VMEM((groups, 2, padded, 3 * PAIR), bf16),
            pltpu.VMEM((2, padded, half), bf16),
            pltpu.VMEM((2, chunks // 2, padded, width), bf16),
            pltpu.VMEM((groups, padded, 3 * PAIR), bf16),
            pltpu.VMEM((padded, half), bf16),
            pltpu.VMEM((chunks // 2, padded, width), bf16),
            pltpu.SemaphoreType.DMA((9, 11)),
            pltpu.SemaphoreType.DMA((9, 11)),
        ]
        params.update(collective_id=0, has_side_effects=True)
        extra = [sds((groups, 2) + chip + (3 * PAIR,), bf16), sds((16, width), f32)]
    else:
        chunks = wup.shape[0]
        extra = []
    out_shape += [
        sds((chunks, width, width), bf16),
        sds((chunks, width, width), bf16),
        sds((2, width, half), bf16),
        sds((8, width), f32),
    ]
    return pl.pallas_call(
        functools.partial(forward_kernel, bool(nz)),
        in_specs=specs("svvvvvvv"),
        out_specs=specs("hhhhhhhhhhv" + "h" * len(extra)),
        out_shape=out_shape + extra,
        scratch_shapes=scratch,
        compiler_params=pltpu.CompilerParams(**params),
        name="layer_forward",
    )(lengths, tokens, cotangent, vecs, wqkv, wproj, wup, wdown)


def run_backward(nz, lengths, tokens, vecs, proj, ot, lse, do, gmid, n1t, wqkv, *sums):
    seq, width = tokens.shape
    pairs = width // PAIR
    half = width // 2
    scratch = [
        pltpu.VMEM((pairs, seq, 3 * PAIR), bf16),
        pltpu.VMEM((pairs, PAIR, seq), bf16),
        pltpu.VMEM((2 * pairs, 8, seq), f32),
        pltpu.VMEM((pairs, seq, PAIR), bf16),
        pltpu.VMEM((seq, width), f32),
        pltpu.VMEM((width, seq), bf16),
        pltpu.VMEM((pairs, width, 3 * PAIR), bf16),
        pltpu.VMEM((seq, width), bf16),
        pltpu.SemaphoreType.DMA((6 + pairs,)),
    ]
    params = dict(vmem_limit_bytes=VMEM_LIMIT)
    if nz:
        gup, gdown, gproj, vg_one = sums
        chip_rows = width // (4 * nz)
        own = chip_rows // 2
        chip = (2, nz, 2)
        rows = gdown.shape[-2]
        groups, parts = pairs // 2, gup.shape[1]
        scratch[6] = pltpu.VMEM((groups, 2) + chip + (chip_rows, 3 * PAIR), bf16)

        def landing(lead, block):
            return [
                pltpu.VMEM(lead + dims + block, bf16) for dims in (chip, (2, nz), (nz,), (nz - 1,))
            ]

        scratch += (
            [
                pltpu.VMEM((2, 5, 8, width), f32),
                pltpu.VMEM((parts,) + chip + (chip_rows, width), bf16),
                pltpu.VMEM((parts,) + chip + (rows // 2, width), bf16),
                pltpu.VMEM(chip + (chip_rows, half), bf16),
            ]
            + landing((parts,), (chip_rows, width))
            + landing((parts,), (rows // 2, width))
            + landing((), (chip_rows, half))
            + landing((groups,), (chip_rows, 3 * PAIR))
            + [
                pltpu.VMEM((parts, own, width), f32),
                pltpu.VMEM((own, half), f32),
                pltpu.VMEM((groups, own, 3 * PAIR), f32),
            ]
            * 2
            + [
                pltpu.VMEM((2, 2 + nz, 8, width), f32),
                pltpu.SemaphoreType.DMA((10, 3 + nz)),
                pltpu.SemaphoreType.DMA((10, 3 + nz)),
                pltpu.SemaphoreType.DMA((10,)),
                pltpu.SemaphoreType.DMA((10,)),
                pltpu.SemaphoreType.DMA((10,)),
            ]
        )
        out_shape = [
            sds((seq, width), bf16),
            sds((own, 3 * width), f32),
            sds((own, width), f32),
            sds((own, 2 * parts * width), f32),
            sds((rows, width), f32),
            sds((16, PAIR), f32),
        ]
        params.update(collective_id=1, has_side_effects=True)
        ins, outs = "svvhhhhhhvhhhv", "hvvvvv"
    else:
        out_shape = [
            sds((seq, width), bf16),
            sds((pairs, width, 3 * PAIR), bf16),
            sds((8, width), f32),
        ]
        ins, outs = "svvhhhhhhv", "hhv"
    return pl.pallas_call(
        functools.partial(backward_kernel, bool(nz)),
        in_specs=specs(ins),
        out_specs=specs(outs),
        out_shape=out_shape,
        scratch_shapes=scratch,
        compiler_params=pltpu.CompilerParams(**params),
        name="attention_backward",
    )(lengths, tokens, vecs, proj, ot, lse, do, gmid, n1t, wqkv, *sums)


def gathered(item, axis=0):
    return lax.all_gather(item, AXES, axis=axis, tiled=True)


def scattered(item, axis=0):
    return lax.psum_scatter(item, AXES, scatter_dimension=axis, tiled=True)


def per_device(
    nz, tokens, cotangent, lengths, attn_gain, attn_shift, qkv_weight, qv_bias, proj_weight, proj_bias,
    mlp_gain, mlp_shift, up_weight, up_bias, down_weight, down_bias,
):
    seq, width = tokens.shape
    pairs = width // PAIR
    own = attn_gain.shape[0]
    chunks = up_weight.shape[1] // width
    small = jnp.stack([attn_gain, attn_shift, qv_bias[0], qv_bias[1], proj_bias, mlp_gain, mlp_shift, down_bias])
    if nz:
        vecs = jnp.concatenate(
            [
                jnp.pad(small, ((0, 0), (0, PAIR - own))),
                jnp.pad(up_bias[None], ((0, 7), (0, PAIR - up_bias.shape[0]))),
            ]
        )
        block_out, proj, ot, lse, do, gmid, n1t, gup, gdown, gproj, vg_one, wqkv, vecs = run_forward(
            nz, lengths, tokens, cotangent, vecs, qkv_weight, proj_weight, up_weight, down_weight
        )
        rows = down_weight.shape[0]
        input_grad, g_qkv, g_proj, g_up, g_down, v = run_backward(
            nz, lengths, tokens, vecs, proj, ot, lse, do, gmid, n1t, wqkv.reshape(pairs, width, 3 * PAIR),
            gup.reshape(2, chunks // 2, 2, nz, 2, 2 * own, width),
            gdown.reshape(2, nz, 2, 2, rows, width),
            gproj.reshape(2, 2, nz, 2, 2 * own, width // 2),
            vg_one,
        )
        w = v[:, :own]
        return (
            block_out, input_grad, w[8], w[9], g_qkv, w[10:12], g_proj, w[2], w[0], w[1],
            g_up, v[4, : up_bias.shape[0]], g_down, w[3],
        )
    else:
        allvec = gathered(jnp.concatenate([small.reshape(-1), up_bias])[None])
        many = allvec.shape[0]
        table = allvec[:, : 8 * own].reshape(many, 8, own).transpose(1, 0, 2).reshape(8, width)
        vecs = jnp.concatenate([table, allvec[:, 8 * own :].reshape(chunks, width)], 0).astype(f32)
        wqkv = gathered(qkv_weight).reshape(width, 3, pairs, PAIR).transpose(2, 0, 1, 3).reshape(pairs, width, 3 * PAIR)
        wproj = gathered(proj_weight).reshape(width, 2, width // 2).transpose(1, 0, 2)
        wup = gathered(up_weight).reshape(width, chunks, width).transpose(1, 0, 2)
        wdown = gathered(down_weight).reshape(chunks, width, width)
        block_out, proj, ot, lse, do, gmid, n1t, gup, gdown, gproj, vg_one = run_forward(
            nz, lengths, tokens, cotangent, vecs, wqkv, wproj, wup, wdown
        )
    input_grad, gqkv, vg_two = run_backward(nz, lengths, tokens, vecs, proj, ot, lse, do, gmid, n1t, wqkv)
    g_down = scattered(gdown.astype(f32).reshape(chunks * width, width))
    g_up = scattered(gup.astype(f32).transpose(1, 0, 2).reshape(width, chunks * width))
    g_proj = scattered(gproj.astype(f32).transpose(1, 0, 2).reshape(width, width))
    g_qkv = scattered(
        gqkv.astype(f32).reshape(pairs, width, 3, PAIR).transpose(1, 2, 0, 3).reshape(width, 3 * width)
    )
    rest = jnp.concatenate([vg_two[:4], vg_one[:4]], 0).reshape(8, many, own).transpose(1, 0, 2).reshape(many, -1)
    rest = jnp.concatenate([rest, vg_one[4:].reshape(many, -1)], 1)
    mine = scattered(rest)[0]
    v = mine[: 8 * own].reshape(8, own)
    return (
        block_out, input_grad, v[0], v[1], g_qkv, v[2:4], g_proj, v[6], v[4], v[5],
        g_up, mine[8 * own :], g_down, v[7],
    )


def chips_along_z(mesh):
    dp, shard = mesh.shape["dp"], mesh.shape["shard"]
    return shard // 4 if dp == 2 and shard == 16 else 0


def solution(mesh):
    one, two, mid = P(AXES), P(AXES, None), P(None, AXES)
    return jax.shard_map(
        functools.partial(per_device, chips_along_z(mesh)),
        mesh=mesh,
        in_specs=(two, two, one, one, one, two, mid, two, one, one, one, two, one, two, one),
        out_specs=(two, two, one, one, two, mid, two, one, one, one, two, one, two, one),
        check_vma=False,
    )
```

```python
import functools

import jax
import jax.numpy as jnp
from jax import lax
from jax.experimental import pallas as pl
from jax.experimental.pallas import tpu as pltpu
from jax.sharding import PartitionSpec as P

f32 = jnp.float32
bf16 = jnp.bfloat16
HD = 64
PAIR = 2 * HD
EPS = 1e-06
MASKED = -1e30
AXES = ("dp", "shard")
VMEM_LIMIT = 65280 * 2**10

AG, AS, QB, VB, PB, MG, MS, DB, UB = range(9)


def dg(a, b, ca, cb):
    return lax.dot_general(a, b, (((ca,), (cb,)), ((), ())), preferred_element_type=f32)


def rows_of(v):
    return v.reshape(-1, v.shape[-1])


def norm_parts(v):
    center = v - jnp.mean(v, -1, keepdims=True)
    inv = lax.rsqrt(jnp.mean(center * center, -1, keepdims=True) + EPS)
    return center * inv, inv


def norm_back(n, inv, z):
    return inv * (z - jnp.mean(z, -1, keepdims=True) - n * jnp.mean(z * n, -1, keepdims=True))


def key_bias(length, seq):
    return jnp.where(lax.broadcasted_iota(jnp.int32, (seq, 1), 0) < length, 0.0, MASKED).astype(f32)


def head_only(v, hh):
    lane = lax.broadcasted_iota(jnp.int32, (1, PAIR), 1)
    return jnp.where(lane // HD == hh, v, jnp.zeros((), v.dtype))


class Place:
    def __init__(self, nz):
        shard = lax.axis_index("shard")
        self.nz = nz
        self.y = lax.axis_index("dp")
        self.c = lax.rem(shard, 2)
        self.x = lax.rem(lax.div(shard, 2), 2)
        self.z = lax.div(shard, 4)
        fy, fx = 1 - 2 * self.y, 1 - 2 * self.x
        self.ay, self.ax = self.y + (1 - self.c) * fy, self.x + self.c * fx
        self.by, self.bx = self.y + self.c * fy, self.x + (1 - self.c) * fx

    def device(self, y, z, x, c):
        return (y, (z * 2 + x) * 2 + c)

    def peer(self):
        return self.device(self.y, self.z, self.x, 1 - self.c)

    def along_z(self, k):
        return self.device(self.y, lax.rem(self.z + k, self.nz), self.x, self.c)

    def a(self):
        return self.device(self.ay, self.z, self.ax, self.c)

    def b(self):
        return self.device(self.by, self.z, self.bx, self.c)

    def partners(self):
        return [self.peer(), self.a(), self.b()] + [self.along_z(k) for k in range(1, self.nz)]


def enter(place):
    barrier = pltpu.get_barrier_semaphore()
    partners = place.partners()
    for d in partners:
        pl.semaphore_signal(barrier, inc=1, device_id=d, device_id_type=pl.DeviceIdType.MESH)
    pl.semaphore_wait(barrier, len(partners))


def remote(src, dst, send, recv, device):
    return pltpu.make_async_remote_copy(
        src_ref=src, dst_ref=dst, send_sem=send, recv_sem=recv, device_id=device,
        device_id_type=pl.DeviceIdType.MESH,
    )


class Gather:
    def __init__(self, place, block, column, swap, send, recv):
        self.p, self.block, self.column, self.swap = place, block, column, swap
        self.send, self.recv = send, recv
        self.started = []

    def move(self, slot, src, dst, device):
        return remote(src, dst, self.send.at[slot], self.recv.at[slot], device)

    def go(self, copy):
        copy.start()
        self.started.append(copy)

    def exchange(self):
        src, dst, _ = self.swap
        return self.move(0, src, dst, self.p.peer())

    def X(self):
        self.go(self.exchange())

    def zs(self):
        p = self.p
        own = self.block(p.y, p.z, p.x, p.c)
        return [self.move(k, own, own, p.along_z(k)) for k in range(1, p.nz)]

    def over(self, slot, y, x, device):
        v = self.column(y, x, self.p.c)
        return self.move(slot, v, v, device)

    def to_b(self):
        return self.over(4, self.p.y, self.p.x, self.p.b())

    def to_a(self, second):
        p = self.p
        y, x = (p.by, p.bx) if second else (p.y, p.x)
        return self.over(5 + second, y, x, p.a())

    def across(self, i):
        p = self.p
        y, x = [(p.y, p.x), (p.by, p.bx), (p.ay, p.ax), (1 - p.y, 1 - p.x)][i]
        return self.over(7 + i, y, x, p.peer())

    def Z(self):
        if self.swap is not None:
            self.exchange().wait_recv()
            self.swap[2]()
        for cp in self.zs():
            self.go(cp)

    def B(self):
        for cp in self.zs():
            cp.wait_recv()
        self.go(self.to_b())
        self.go(self.to_a(0))
        self.go(self.across(0))

    def A(self):
        self.to_b().wait_recv()
        self.go(self.to_a(1))
        self.go(self.across(1))

    def C(self):
        self.to_a(0).wait_recv()
        self.go(self.across(2))
        self.to_a(1).wait_recv()
        self.go(self.across(3))

    def D(self):
        for i in range(4):
            self.across(i).wait_recv()

    def finish(self):
        if self.swap is not None:
            self.exchange().wait_send()
        for cp in self.zs() + [self.to_b(), self.to_a(0), self.to_a(1)] + [self.across(i) for i in range(4)]:
            cp.wait_send()


class Scatter:
    def __init__(self, place, half, own, bufs, send, recv, total):
        self.p, self.half, self.own = place, half, own
        self.r0, self.r1, self.r2, self.r3 = bufs
        self.send, self.recv, self.total = send, recv, total

    def move(self, slot, src, dst, device):
        return remote(src, dst, self.send.at[slot], self.recv.at[slot], device)

    def swap(self):
        return self.move(0, self.half(1 - self.p.c), self.r0, self.p.peer())

    def to_a(self, i):
        p = self.p
        src = self.own.at[p.ay, :, p.ax] if i == 0 else self.own.at[1 - p.y, :, 1 - p.x]
        return self.move(1 + i, src, self.r1.at[i], p.a())

    def to_b(self):
        p = self.p
        return self.move(3, self.own.at[p.by, :, p.bx], self.r2, p.b())

    def to_z(self, k):
        p = self.p
        return self.move(3 + k, self.own.at[p.y, lax.rem(p.z + k, p.nz), p.x], self.r3.at[k - 1], p.along_z(k))

    def add(self, y, x, other):
        self.own[y, :, x] = (self.own[y, :, x].astype(f32) + other.astype(f32)).astype(bf16)

    def S0(self):
        self.swap().start()

    def S1(self):
        p = self.p
        self.swap().wait_recv()
        for i, (y, x) in enumerate([(p.ay, p.ax), (1 - p.y, 1 - p.x), (p.by, p.bx), (p.y, p.x)]):
            self.add(y, x, self.r0[y, :, x])
            if i < 2:
                self.to_a(i).start()

    def S2(self):
        p = self.p
        self.to_a(1).wait_recv()
        self.add(p.by, p.bx, self.r1[1])
        self.to_b().start()
        self.to_a(0).wait_recv()
        self.add(p.y, p.x, self.r1[0])

    def S3(self):
        p = self.p
        self.to_b().wait_recv()
        self.add(p.y, p.x, self.r2[...])
        for k in range(1, p.nz):
            self.to_z(k).start()

    def S4(self):
        p = self.p
        total = self.own[p.y, p.z, p.x].astype(f32)
        for k in range(1, p.nz):
            self.to_z(k).wait_recv()
            total += self.r3[k - 1].astype(f32)
        self.total(total)

    def finish(self):
        for cp in [self.swap(), self.to_a(0), self.to_a(1), self.to_b()] + [
            self.to_z(k) for k in range(1, self.p.nz)
        ]:
            cp.wait_send()


class Handover:
    def __init__(self, place, stage, landing, write, send, recv):
        self.p, self.stage, self.landing, self.write = place, stage, landing, write
        self.copy = remote(stage, landing, send, recv, place.peer())

    def start(self, total):
        own = total.shape[0] // 2
        top, bottom = total[:own], total[own:]
        self.stage[...] = jnp.where(self.p.c == 0, bottom, top)
        self.copy.start()
        self.write(self.p.c, jnp.where(self.p.c == 0, top, bottom))

    def S5(self):
        self.copy.wait_recv()
        self.write(1 - self.p.c, self.landing[...])

    def end(self):
        self.copy.wait_send()


class VectorSum:
    def __init__(self, place, value, bufs, send, recv):
        self.p, self.value, self.bufs, self.send, self.recv = place, value, bufs, send, recv

    def move(self, slot):
        p = self.p
        device = [p.peer(), p.a(), p.b()][slot] if slot < 3 else p.along_z(slot - 2)
        return remote(
            self.value.at[min(slot, 3)], self.bufs.at[slot], self.send.at[slot], self.recv.at[slot], device
        )

    def S0(self):
        self.move(0).start()

    def step(self, slot):
        self.move(slot - 1).wait_recv()
        self.value[slot] = self.value[slot - 1] + self.bufs[slot - 1]
        for k in range(self.p.nz - 1 if slot == 3 else 1):
            self.move(slot + k).start()

    def S1(self):
        self.step(1)

    def S2(self):
        self.step(2)

    def S3(self):
        self.step(3)

    def S4(self):
        total = self.value[3]
        for k in range(self.p.nz - 1):
            self.move(3 + k).wait_recv()
            total += self.bufs[3 + k]
        self.value[4] = total

    def finish(self):
        for slot in range(2 + self.p.nz):
            self.move(slot).wait_send()


def expand_table(vbuf, vec, own, ff_own):
    many = vbuf.shape[0] * vbuf.shape[1] * vbuf.shape[2] * vbuf.shape[3]
    width = vec.shape[1]
    ff = many * ff_own
    flat = vbuf[...].reshape(many * 16, PAIR)

    def spread(n, each):
        lane = lax.broadcasted_iota(jnp.int32, (PAIR, n), 1)
        return (lax.rem(lane, each) == lax.broadcasted_iota(jnp.int32, (PAIR, n), 0)).astype(f32).astype(bf16)

    full = dg(flat, spread(width, own), 1, 0).reshape(many, 16, width)
    where = lax.broadcasted_iota(jnp.int32, (many, 1, width), 2) - own * lax.broadcasted_iota(
        jnp.int32, (many, 1, width), 0
    )
    vec[0:16, :] = jnp.sum(jnp.where((where >= 0) & (where < own), full, 0.0), 0)
    pick = (
        lax.broadcasted_iota(jnp.int32, (many, many * 16), 1)
        == 16 * lax.broadcasted_iota(jnp.int32, (many, many * 16), 0) + 8
    )
    row = dg(pick.astype(f32).astype(bf16), flat, 1, 0).astype(bf16)
    full = dg(row, spread(ff, ff_own), 1, 0)
    where = lax.broadcasted_iota(jnp.int32, (many, ff), 1) - ff_own * lax.broadcasted_iota(jnp.int32, (many, ff), 0)
    up = jnp.sum(jnp.where((where >= 0) & (where < ff_own), full, 0.0), 0, keepdims=True)
    for j in range(ff // width):
        vec[UB + j : UB + j + 1, :] = up[:, j * width : (j + 1) * width]


def gather_items(place, own_down, wqkv, wproj, wup, wdown, vbuf, xs, xr, send, recv):
    p = place
    (xs_qkv, xs_proj, xs_up), (xr_qkv, xr_proj, xr_up) = xs, xr
    own = wqkv.shape[-2] // 2

    def joined(mine, theirs, write):
        def go():
            m, t = mine()[:own].astype(f32), theirs()[:own].astype(f32)
            lo, hi = jnp.where(p.c == 0, m, t), jnp.where(p.c == 0, t, m)
            write(jnp.concatenate([lo, hi], 0).astype(bf16))
        return go

    items = []

    def add(block, column, swap):
        i = len(items)
        items.append(Gather(p, block, column, swap, send.at[i], recv.at[i]))

    add(lambda y, z, x, c: vbuf.at[y, z, x, c], lambda y, x, c: vbuf.at[y, :, x, c], None)

    def add_swapped(view, xs_of, xr_of):
        block = lambda y, z, x, c: view(c).at[y, z, x]
        column = lambda y, x, c: view(c).at[y, :, x]

        def write(v):
            view(p.c)[p.y, p.z, p.x] = v

        add(block, column, (xs_of(1 - p.c), xr_of, joined(lambda: xs_of(p.c)[...], lambda: xr_of[...], write)))

    for g in range(wqkv.shape[0]):
        add_swapped(lambda c, g=g: wqkv.at[g, c], lambda c, g=g: xs_qkv.at[g, c], xr_qkv.at[g])
    add_swapped(lambda c: wproj.at[c], lambda c: xs_proj.at[c], xr_proj)
    part = wdown.shape[-2] // 2
    for k in range(2):
        rows = pl.ds(k * part, part)
        add(
            lambda y, z, x, c, rows=rows: wdown.at[y, z, x, c, rows],
            lambda y, x, c, rows=rows: wdown.at[y, :, x, c, rows],
            None,
        )
    for k in range(2):
        add_swapped(lambda c, k=k: wup.at[c, k], lambda c, k=k: xs_up.at[c, k], xr_up.at[k])
    return items


def slice_lanes(v, first, count):
    lane = lax.broadcasted_iota(jnp.int32, (v.shape[1], PAIR), 0) - first
    out = lax.broadcasted_iota(jnp.int32, (v.shape[1], PAIR), 1)
    pick = ((lane == out) & (out < count)).astype(f32)
    return lax.dot_general(
        v, pick, (((1,), (0,)), ((), ())), precision=lax.Precision.HIGHEST, preferred_element_type=f32
    )


def attend(k2, v2t, q2, bias_k, write):
    ones = jnp.ones((16, k2.shape[0]), bf16)
    for hh in range(2):
        s = dg(k2, head_only(q2, hh), 1, 1) + bias_k
        top = jnp.max(s, 0, keepdims=True)
        e = jnp.exp(s - top).astype(bf16)
        o = dg(jnp.concatenate([v2t[HD * hh : HD * hh + HD], ones], 0), e, 1, 0)
        total = o[HD : HD + 1]
        write(hh, o[:HD] / total, top + jnp.log(total))


def attend_back(q_of, k2, v2, do_of, ot_of, lse_of, bias_k, block, between):
    seq = k2.shape[0]
    scale = HD**-0.5
    k2t = k2.T
    dk = dv = None
    dqt = []
    for hh in range(2):
        rows = slice(HD * hh, HD * hh + HD)
        parts = []
        for i in range(seq // block):
            sl = slice(i * block, (i + 1) * block)
            qm = head_only(q_of(sl) * jnp.asarray(scale, bf16), hh)
            d = do_of(sl)
            dm = head_only(d, hh)
            delta = jnp.sum(d.astype(f32).T[rows] * ot_of(rows, sl).astype(f32), 0, keepdims=True)
            e = jnp.exp(dg(k2, qm, 1, 1) + bias_k - lse_of(hh, sl))
            ds = (e * (dg(v2, dm, 1, 1) - delta)).astype(bf16)
            t = dg(e.astype(bf16), dm, 1, 0)
            dv = t if dv is None else dv + t
            t = dg(ds, qm, 1, 0)
            dk = t if dk is None else dk + t
            parts.append(dg(k2t[rows], ds, 1, 0) * scale)
        dqt.append(jnp.concatenate(parts, 1))
        if hh == 0:
            between()
    return jnp.concatenate(dqt, 0), dk, dv


def up_step(n2, cot, up, down, up_bias):
    h = dg(n2, up(), 1, 0) + up_bias
    phi = 0.5 * (1.0 + lax.erf(h * 0.7071067811865476))
    a = (h * phi).astype(bf16)
    ga = dg(cot, down(), 1, 1)
    g = (ga * (phi + h * jnp.exp(-0.5 * h * h) * 0.3989422804014327)).astype(bf16)
    return a, g


def pick(index, choices):
    v = choices[0]
    for i in range(1, len(choices)):
        v = jnp.where(index == i, choices[i], v)
    return v


def blocks(count, size, body):
    @pl.loop(0, count)
    def _(r):
        body(r, pl.ds(pl.multiple_of(r * size, size), size))


VECI, G0, G1, G2, PROJ, D0, D1, U0, U1 = range(9)
SV1, SD0, SD1, SU0, SU1, SP, SG0, SG1, SG2, SV2 = range(10, 20)
PLAN = {
    "stats": [("B", VECI), ("B", G0), ("Z", G1), ("A", VECI), ("A", G0), ("B", G1), ("Z", G2),
              ("C", VECI), ("C", G0), ("A", G1), ("B", G2), ("Z", PROJ), ("D", VECI)],
    "norm": [("D", G0), ("C", G1), ("A", G2), ("B", PROJ), ("Z", D0)],
    "f0": [("C", G2), ("A", PROJ), ("B", D0), ("Z", D1)],
    "f1": [("D", G1), ("C", PROJ), ("A", D0), ("B", D1), ("Z", U0)],
    "f2": [("C", D0), ("A", D1), ("B", U0), ("Z", U1)],
    "f3": [("D", G2), ("C", D1), ("A", U0), ("B", U1)],
    "f4": [("C", U0), ("A", U1)],
    "f5": [("C", U1), ("D", PROJ)],
    "m0": [("D", D0), ("D", D1), ("D", U0)],
    "m0g": [("finish", D0), ("finish", D1), ("finish", U0)],
    "m2": [("D", U1), ("finish", U1), ("S0", SU0)],
    "m3": [("S1", SU0)],
    "m4": [("S0", SU1), ("S0", SD0), ("S0", SD1), ("S2", SU0), ("finish", PROJ)],
    "mid": [("S0", SP), ("S0", SV1), ("S1", SU1), ("S3", SU0), ("S1", SD0)],
    "b0h": [("S1", SD1), ("S2", SU1), ("S1", SV1)],
    "b0": [("S1", SP), ("S4", SU0), ("S3", SU1), ("S2", SD0), ("S2", SV1)],
    "b1h": [("S2", SD1), ("S5", SU0), ("S3", SV1)],
    "b1": [("S0", SG0), ("S3", SD0), ("S4", SU1), ("S2", SP), ("S4", SV1)],
    "b2h": [("S1", SG0), ("S3", SD1), ("S5", SU1)],
    "b2": [("S3", SP), ("S4", SD0)],
    "b3h": [("S2", SG0), ("S4", SD1)],
    "b3": [("S0", SG1), ("S4", SP), ("S3", SG0)],
    "b4h": [("S1", SG1), ("S5", SP)],
    "b4": [("S4", SG0), ("S2", SG1)],
    "b5h": [("S5", SG0), ("S3", SG1)],
    "b5": [("S0", SG2)],
    "r0": [("S1", SG2), ("S4", SG1)],
    "r1": [("S2", SG2), ("S5", SG1)],
    "r2": [("S3", SG2)],
    "r3": [("S0", SV2), ("S4", SG2)],
    "end": [("S1", SV2), ("S2", SV2), ("S3", SV2), ("S5", SG2), ("S4", SV2)],
}


def layer_kernel(
    len_ref, tok_hbm, cot_ref, vec_in, wqkv_in, wproj_in, wup_in, wdown_in,
    out_hbm, gin_hbm, oqkv, oproj, oup, odown, vg_out,
    n1, n1t, proj, ot, att, lse, res, n2t, acc, gn2, gh,
    vec_ref, wqkv, wproj, wup, wdown, vbuf, xs_qkv, xs_proj, xs_up, xr_qkv, xr_proj, xr_up, gsend, grecv,
    vsum, up0, up1, up2, up3, down0, down1, down2, down3, proj0, proj1, proj2, proj3, qkv1, qkv2, qkv3,
    qkv0, stage_up, stage_proj, stage_qkv, land_up, land_proj, land_qkv, vbufs, send, recv, hsend, hrecv, sems,
):
    seq, width = cot_ref.shape
    half = width // 2
    pairs = proj.shape[0]
    own, rows = wqkv_in.shape[0], wdown_in.shape[0]
    groups, parts = wqkv.shape[0], wup.shape[1]
    chunks = 2 * parts
    place = Place(wqkv.shape[3])
    p_ = place
    n2, act, gin, tok_early, tok_late = n1, att, att, gh, n1
    vg_one, vg_two = vsum.at[0, 0], vsum.at[1, 0]
    g_qkv = [up0.at[0], up0.at[1], down0.at[0]]

    items = dict(enumerate(gather_items(
        place, wdown_in, wqkv, wproj, wup, wdown, vbuf, (xs_qkv, xs_proj, xs_up), (xr_qkv, xr_proj, xr_up),
        gsend, grecv,
    )))
    handovers = []

    def add(i, half_of, bufs, total):
        k = i - SV1
        items[i] = Scatter(p_, half_of, half_of(p_.c), bufs, send.at[k], recv.at[k], total)

    def add_shared(i, half_of, bufs, stage, landing, write):
        k = i - SV1
        h = Handover(p_, stage, landing, write, hsend.at[k], hrecv.at[k])
        handovers.append(h)
        add(i, half_of, bufs, h.start)
        items[i].S5 = h.S5

    part = rows // 2
    for k in range(2):
        where = slice(k * part, (k + 1) * part)

        def write_down(total, where=where):
            odown[where, :] = total

        add(
            SD0 + k, lambda c, k=k: wdown.at[:, :, :, c, pl.ds(k * part, part)],
            (down0.at[k], down1.at[k], down2.at[k], down3.at[k]), write_down,
        )

        def write_up(c, v, k=k):
            oup[:, pl.ds(pl.multiple_of((2 * c + k) * width, PAIR), width)] = v

        add_shared(
            SU0 + k, lambda c, k=k: wup.at[c, k], (up0.at[k], up1.at[k], up2.at[k], up3.at[k]),
            stage_up.at[k], land_up.at[k], write_up,
        )

    def write_proj(c, v):
        oproj[:, pl.ds(pl.multiple_of(c * half, PAIR), half)] = v

    add_shared(SP, lambda c: wproj.at[c], (proj0, proj1, proj2, proj3), stage_proj, land_proj, write_proj)
    for g in range(groups):

        def write_qkv(c, v, g=g):
            for t in range(3):
                oqkv[:, pl.ds(pl.multiple_of(t * width + (2 * g + c) * PAIR, PAIR), PAIR)] = v[
                    :, t * PAIR : (t + 1) * PAIR
                ]

        add_shared(
            SG0 + g, lambda c, g=g: g_qkv[g].at[:, :, :, :, pl.ds(pl.multiple_of(c * 3 * PAIR, PAIR), 3 * PAIR)],
            (qkv0.at[g], qkv1.at[g], qkv2.at[g], qkv3.at[g]), stage_qkv.at[g], land_qkv.at[g], write_qkv,
        )
    for i, v in ((SV1, 0), (SV2, 1)):
        items[i] = VectorSum(p_, vsum.at[v], vbufs.at[v], send.at[i - SV1], recv.at[i - SV1])
    finished = set()

    def tick(name):
        for step, i in PLAN.get(name, ()):
            getattr(items[i], step)()
            if step == "finish":
                finished.add(i)

    def ticks(index, names):
        for i, name in enumerate(names):
            if PLAN.get(name):

                @pl.when(index == i)
                def _(name=name):
                    tick(name)

    def w_qkv(p):
        return rows_of(wqkv[lax.div(p, 2), lax.rem(p, 2)])

    def w_up(j):
        return rows_of(wup[j // parts, j % parts])

    zs = wdown.shape[1] // 2

    def w_down(j):
        return rows_of(wdown[j // 2, zs * (j % 2) : zs * (j % 2) + zs])

    def w_proj(i):
        return rows_of(wproj[i])

    def vec(i):
        return vec_ref[i : i + 1, :]

    rb = 256
    nb = seq // rb
    tok_copy = pltpu.make_async_copy(tok_hbm, tok_early, sems.at[1])
    tok_copy.start()
    vbuf[p_.y, p_.z, p_.x, p_.c] = vec_in[...]
    for p in range(pairs):
        for t in range(3):
            lanes = slice(t * width + p * PAIR, t * width + (p + 1) * PAIR)
            xs_qkv[p // 2, p % 2, 0:own, t * PAIR : (t + 1) * PAIR] = wqkv_in[:, lanes]
    enter(place)
    for i in (G0, G1, G2):
        items[i].X()
    items[VECI].Z()
    items[G0].Z()
    for i in range(2):
        xs_proj[i, 0:own, :] = wproj_in[:, i * half : (i + 1) * half]
    for j in range(chunks):
        xs_up[j // parts, j % parts, 0:own, :] = wup_in[:, j * width : (j + 1) * width]
    for i in (PROJ, U0, U1):
        items[i].X()
    wdown[p_.y, p_.z, p_.x, p_.c] = wdown_in[...]

    tok_copy.wait()

    def stats(r, sl):
        res[sl, :] = norm_parts(tok_early[sl, :].astype(f32))[0]

    blocks(nb, rb, stats)
    tick("stats")
    expand_table(vbuf, vec_ref, own, rows)

    def norm(r, sl):
        n1[sl, :] = (res[sl, :] * vec(AG) + vec(AS)).astype(bf16)

    blocks(nb, rb, norm)
    n1t[...] = n1[...].T
    tick("norm")

    bias_k = key_bias(len_ref[0], seq)
    q_bias = [vec(QB)[:, i * PAIR : (i + 1) * PAIR] for i in range(pairs)]
    v_bias = [vec(VB)[:, i * PAIR : (i + 1) * PAIR] for i in range(pairs)]

    @pl.loop(0, pairs)
    def _(p):
        qkv = dg(n1[...], w_qkv(p), 1, 0)
        proj[p, :, 0:PAIR] = (qkv[:, 0:PAIR] + pick(p, q_bias)).astype(bf16)
        proj[p, :, PAIR : 2 * PAIR] = qkv[:, PAIR : 2 * PAIR].astype(bf16)
        proj[p, :, 2 * PAIR :] = (qkv[:, 2 * PAIR :] + pick(p, v_bias)).astype(bf16)

        def write(hh, o, total):
            ot[p, HD * hh : HD * hh + HD, :] = o.astype(bf16)
            lse[pl.ds(2 * p + hh, 1), :] = total

        attend(
            proj[p, :, PAIR : 2 * PAIR], proj[p, :, 2 * PAIR :].T,
            proj[p, :, 0:PAIR] * jnp.asarray(HD**-0.5, bf16), bias_k, write,
        )
        ticks(p, [f"f{i}" for i in range(pairs)])

    for p in range(pairs):
        att[:, p * PAIR : (p + 1) * PAIR] = ot[p].T

    def branch(r, sl):
        a = att[sl, :]
        v = tok_early[sl, :].astype(f32) + vec(PB)
        v += jnp.concatenate([dg(a, w_proj(i), 1, 0) for i in range(2)], 1)
        res[sl, :] = v
        acc[sl, :] = v + vec(DB)
        gn2[sl, :] = jnp.zeros((rb, width), f32)
        n2[sl, :] = (norm_parts(v)[0] * vec(MG) + vec(MS)).astype(bf16)

    blocks(nb, rb, branch)
    n2t[...] = n2[...].T

    rm = 512
    order = [c * parts + k for k in range(parts) for c in range(2)]
    for turn, j in enumerate(order):
        tick(f"m{turn}")
        vg_one[4 + j : 5 + j, :] = jnp.zeros((1, width), f32)

        def stage_one(r, sl, j=j):
            a, g = up_step(n2[sl, :], cot_ref[sl, :], lambda: w_up(j), lambda: w_down(j), vec(UB + j))
            act[sl, :] = a
            gh[sl, :] = g
            acc[sl, :] += dg(a, w_down(j), 1, 0)
            gn2[sl, :] += dg(g, w_up(j), 1, 1)
            vg_one[4 + j : 5 + j, :] += jnp.sum(g.astype(f32), 0, keepdims=True)

        blocks(seq // rm, rm, stage_one)
        tick(f"m{turn}g")
        v = dg(act[...], cot_ref[...], 0, 0).astype(bf16)
        wdown[j // 2, zs * (j % 2) : zs * (j % 2) + zs] = v.reshape((zs,) + wdown.shape[2:])
        wup[j // parts, j % parts] = dg(n2t[...], gh[...], 1, 0).astype(bf16).reshape(wup.shape[2:])
    tick(f"m{chunks}")

    vg_one[0:4, :] = jnp.zeros((4, width), f32)

    def back_two(r, sl):
        n2[sl, :] = acc[sl, :].astype(bf16)
        g = gn2[sl, :]
        n, inv = norm_parts(res[sl, :])
        cot = cot_ref[sl, :].astype(f32)
        mid = cot + norm_back(n, inv, g * vec(MG))
        acc[sl, :] = mid
        low = mid.astype(bf16)
        act[sl, :] = low
        vg_one[0:1, :] += jnp.sum(g * n, 0, keepdims=True)
        vg_one[1:2, :] += jnp.sum(g, 0, keepdims=True)
        vg_one[2:3, :] += jnp.sum(low.astype(f32), 0, keepdims=True)
        vg_one[3:4, :] += jnp.sum(cot, 0, keepdims=True)
        back = dg(low[:, :half], w_proj(0), 1, 1) + dg(low[:, half:], w_proj(1), 1, 1)
        gh[sl, :] = back.astype(bf16)

    blocks(nb, rb, back_two)
    out_copy = pltpu.make_async_copy(n2, out_hbm, sems.at[0])
    out_copy.start()
    for i in range(2):
        v = dg(rows_of(ot[...]), act[:, i * half : (i + 1) * half], 1, 0).astype(bf16)
        wproj[i] = v.reshape(wproj.shape[1:])
    vg_two[...] = jnp.zeros(vg_two.shape, f32)
    tick("mid")

    def weight_gradient(p):
        cols = slice(p * PAIR, (p + 1) * PAIR)
        g = proj[p]
        sums = jnp.sum(g.astype(f32), 0, keepdims=True)
        vg_two[2:3, cols] = sums[:, 0:PAIR]
        vg_two[3:4, cols] = sums[:, 2 * PAIR :]
        v = dg(n1t[...], g, 1, 0).astype(bf16).reshape(g_qkv[0].shape[:-1] + (3 * PAIR,))
        g_qkv[p // 2][:, :, :, :, (p % 2) * 3 * PAIR : (p % 2 + 1) * 3 * PAIR] = v

    @pl.loop(0, pairs)
    def _(p):
        lanes = pl.ds(pl.multiple_of(p * PAIR, PAIR), PAIR)
        dqt, dk, dv = attend_back(
            lambda sl: proj[p, sl, 0:PAIR],
            proj[p, :, PAIR : 2 * PAIR],
            proj[p, :, 2 * PAIR :],
            lambda sl: gh[sl, lanes],
            lambda rows, sl: ot[p, rows, sl],
            lambda hh, sl: lse[pl.ds(2 * p + hh, 1), sl],
            bias_k,
            512,
            lambda: ticks(p, [f"b{i}h" for i in range(pairs)]),
        )
        proj[p, :, 0:PAIR] = dqt.T.astype(bf16)
        proj[p, :, PAIR : 2 * PAIR] = dk.astype(bf16)
        proj[p, :, 2 * PAIR :] = dv.astype(bf16)
        for i in range(1, pairs, 2):

            @pl.when(p == i)
            def _(i=i):
                weight_gradient(i - 1)
                weight_gradient(i)

        ticks(p, [f"b{i}" for i in range(pairs)])

    out_copy.wait()
    tok_copy = pltpu.make_async_copy(tok_hbm, tok_late, sems.at[0])
    tok_copy.start()
    tok_copy.wait()

    def back_one(r, sl):
        g = dg(proj[0, sl, :], rows_of(wqkv[0, 0]), 1, 1)
        for p in range(1, pairs):
            g += dg(proj[p, sl, :], rows_of(wqkv[p // 2, p % 2]), 1, 1)
        n, inv = norm_parts(tok_late[sl, :].astype(f32))
        gin[sl, :] = (acc[sl, :] + norm_back(n, inv, g * vec(AG))).astype(bf16)
        vg_two[0:1, :] += jnp.sum(g * n, 0, keepdims=True)
        vg_two[1:2, :] += jnp.sum(g, 0, keepdims=True)
        ticks(r, [f"r{i}" for i in range(nb)])

    blocks(nb, rb, back_one)
    gin_copy = pltpu.make_async_copy(gin, gin_hbm, sems.at[1])
    gin_copy.start()
    index = ((p_.y * p_.nz + p_.z) * 2 + p_.x) * 2 + p_.c
    each = width // rows
    one = vsum[0, 4]
    vg_out[0:8, :] = slice_lanes(one, index * own, own)
    up = slice_lanes(one, lax.rem(index, each) * rows, rows)
    row = lax.broadcasted_iota(jnp.int32, up.shape, 0)
    vg_out[4:5, :] = jnp.sum(jnp.where(row == 4 + lax.div(index, each), up, 0.0), 0, keepdims=True)
    tick("end")
    vg_out[8:16, :] = slice_lanes(vsum[1, 4], index * own, own)
    for i, item in items.items():
        if i not in finished:
            item.finish()
    for h in handovers:
        h.end()
    gin_copy.wait()


def forward_kernel(
    len_ref, tok_ref, cot_ref, vec_ref, wqkv, wproj, wup, wdown,
    out_hbm, proj_hbm, ot_hbm, lse_hbm, do_hbm, gmid_hbm, n1t_hbm, gup_hbm, gdown_hbm, gproj_hbm, vg_ref,
    n1, n1t, proj, ot, att, lse, res, n2, n2t, acc, gn2, act, gh, gstage, sems,
):
    seq, width = tok_ref.shape
    half = width // 2
    chunks, pairs = gup_hbm.shape[0], proj.shape[0]
    copies = []

    def send_out(src, dst, sem):
        cp = pltpu.make_async_copy(src, dst, sem)
        cp.start()
        copies.append(cp)

    def vec(i):
        return vec_ref[i : i + 1, :]

    rb = 256
    nb = seq // rb

    def norm(r, sl):
        n1[sl, :] = (norm_parts(tok_ref[sl, :].astype(f32))[0] * vec(AG) + vec(AS)).astype(bf16)

    blocks(nb, rb, norm)
    n1t[...] = n1[...].T
    send_out(n1t, n1t_hbm, sems.at[0])
    bias_k = key_bias(len_ref[0], seq)
    q_bias = [vec(QB)[:, i * PAIR : (i + 1) * PAIR] for i in range(pairs)]
    v_bias = [vec(VB)[:, i * PAIR : (i + 1) * PAIR] for i in range(pairs)]

    @pl.loop(0, pairs)
    def _(p):
        qkv = dg(n1[...], wqkv[p], 1, 0)
        proj[p, :, 0:PAIR] = (qkv[:, 0:PAIR] + pick(p, q_bias)).astype(bf16)
        proj[p, :, PAIR : 2 * PAIR] = qkv[:, PAIR : 2 * PAIR].astype(bf16)
        proj[p, :, 2 * PAIR :] = (qkv[:, 2 * PAIR :] + pick(p, v_bias)).astype(bf16)

        def write(hh, o, total):
            ot[p, HD * hh : HD * hh + HD, :] = o.astype(bf16)
            lse[pl.ds(2 * p + hh, 1), :] = total

        attend(
            proj[p, :, PAIR : 2 * PAIR], proj[p, :, 2 * PAIR :].T,
            proj[p, :, 0:PAIR] * jnp.asarray(HD**-0.5, bf16), bias_k, write,
        )

    for p in range(pairs):
        att[:, p * PAIR : (p + 1) * PAIR] = ot[p].T
    send_out(proj, proj_hbm, sems.at[1])
    send_out(ot, ot_hbm, sems.at[2])
    send_out(lse, lse_hbm, sems.at[3])

    def branch(r, sl):
        a = att[sl, :]
        v = tok_ref[sl, :].astype(f32) + vec(PB)
        v += jnp.concatenate([dg(a, wproj[i], 1, 0) for i in range(2)], 1)
        res[sl, :] = v
        acc[sl, :] = v + vec(DB)
        gn2[sl, :] = jnp.zeros((rb, width), f32)
        n2[sl, :] = (norm_parts(v)[0] * vec(MG) + vec(MS)).astype(bf16)

    blocks(nb, rb, branch)
    n2t[...] = n2[...].T
    rm = 512
    staged = []
    for j in range(chunks):
        vg_ref[4 + j : 5 + j, :] = jnp.zeros((1, width), f32)

        def stage_one(r, sl, j=j):
            a, g = up_step(n2[sl, :], cot_ref[sl, :], lambda: wup[j], lambda: wdown[j], vec(UB + j))
            act[sl, :] = a
            gh[sl, :] = g
            acc[sl, :] += dg(a, wdown[j], 1, 0)
            gn2[sl, :] += dg(g, wup[j], 1, 1)
            vg_ref[4 + j : 5 + j, :] += jnp.sum(g.astype(f32), 0, keepdims=True)

        blocks(seq // rm, rm, stage_one)
        for cp in staged:
            cp.wait()
        gstage[0] = dg(act[...], cot_ref[...], 0, 0).astype(bf16)
        gstage[1] = dg(n2t[...], gh[...], 1, 0).astype(bf16)
        staged = [
            pltpu.make_async_copy(gstage.at[0], gdown_hbm.at[j], sems.at[4]),
            pltpu.make_async_copy(gstage.at[1], gup_hbm.at[j], sems.at[5]),
        ]
        for cp in staged:
            cp.start()

    vg_ref[0:4, :] = jnp.zeros((4, width), f32)

    def back_two(r, sl):
        n2[sl, :] = acc[sl, :].astype(bf16)
        g = gn2[sl, :]
        n, inv = norm_parts(res[sl, :])
        cot = cot_ref[sl, :].astype(f32)
        mid = cot + norm_back(n, inv, g * vec(MG))
        acc[sl, :] = mid
        low = mid.astype(bf16)
        act[sl, :] = low
        vg_ref[0:1, :] += jnp.sum(g * n, 0, keepdims=True)
        vg_ref[1:2, :] += jnp.sum(g, 0, keepdims=True)
        vg_ref[2:3, :] += jnp.sum(low.astype(f32), 0, keepdims=True)
        vg_ref[3:4, :] += jnp.sum(cot, 0, keepdims=True)
        gh[sl, :] = (dg(low[:, :half], wproj[0], 1, 1) + dg(low[:, half:], wproj[1], 1, 1)).astype(bf16)

    blocks(nb, rb, back_two)
    send_out(n2, out_hbm, sems.at[6])
    send_out(acc, gmid_hbm, sems.at[7])
    for p in range(pairs):
        send_out(gh.at[:, p * PAIR : (p + 1) * PAIR], do_hbm.at[p], sems.at[8 + p])
    for cp in staged:
        cp.wait()
    for i in range(2):
        gstage[i, :, :half] = dg(rows_of(ot[...]), act[:, i * half : (i + 1) * half], 1, 0).astype(bf16)
        send_out(gstage.at[i, :, pl.ds(0, half)], gproj_hbm.at[i], sems.at[4 + i])
    for cp in copies:
        cp.wait()


def backward_kernel(
    len_ref, tok_ref, vec_ref, proj_hbm, ot_hbm, lse_hbm, do_hbm, gmid_hbm, n1t_hbm, wqkv_ref,
    gin_hbm, gqkv_hbm, vg_ref,
    proj, ot, lse, do, gmid, n1t, gqkv, gin, sems,
):
    seq, width = tok_ref.shape
    pairs = proj.shape[0]

    def start(src, dst, sem):
        cp = pltpu.make_async_copy(src, dst, sem)
        cp.start()
        return cp

    loads = [
        start(proj_hbm, proj, sems.at[0]),
        start(do_hbm, do, sems.at[1]),
        start(ot_hbm, ot, sems.at[2]),
        start(lse_hbm, lse, sems.at[3]),
        start(n1t_hbm, n1t, sems.at[4]),
        start(gmid_hbm, gmid, sems.at[5]),
    ]
    for cp in loads:
        cp.wait()
    vg_ref[...] = jnp.zeros(vg_ref.shape, f32)
    bias_k = key_bias(len_ref[0], seq)

    @pl.loop(0, pairs)
    def _(p):
        dqt, dk, dv = attend_back(
            lambda sl: proj[p, sl, 0:PAIR],
            proj[p, :, PAIR : 2 * PAIR],
            proj[p, :, 2 * PAIR :],
            lambda sl: do[p, sl, :],
            lambda rows, sl: ot[p, rows, sl],
            lambda hh, sl: lse[pl.ds(2 * p + hh, 1), sl],
            bias_k,
            512,
            lambda: None,
        )
        proj[p, :, 0:PAIR] = dqt.T.astype(bf16)
        proj[p, :, PAIR : 2 * PAIR] = dk.astype(bf16)
        proj[p, :, 2 * PAIR :] = dv.astype(bf16)

    outs = []
    for p in range(pairs):
        cols = slice(p * PAIR, (p + 1) * PAIR)
        g = proj[p]
        sums = jnp.sum(g.astype(f32), 0, keepdims=True)
        vg_ref[2:3, cols] = sums[:, 0:PAIR]
        vg_ref[3:4, cols] = sums[:, 2 * PAIR :]
        gqkv[p] = dg(n1t[...], g, 1, 0).astype(bf16)
        outs.append(start(gqkv.at[p], gqkv_hbm.at[p], sems.at[6 + p]))

    def back_one(r, sl):
        g = dg(proj[0, sl, :], wqkv_ref[0], 1, 1)
        for p in range(1, pairs):
            g += dg(proj[p, sl, :], wqkv_ref[p], 1, 1)
        n, inv = norm_parts(tok_ref[sl, :].astype(f32))
        gin[sl, :] = (gmid[sl, :] + norm_back(n, inv, g * vec_ref[AG : AG + 1, :])).astype(bf16)
        vg_ref[0:1, :] += jnp.sum(g * n, 0, keepdims=True)
        vg_ref[1:2, :] += jnp.sum(g, 0, keepdims=True)

    blocks(seq // 256, 256, back_one)
    outs.append(start(gin, gin_hbm, sems.at[0]))
    for cp in outs:
        cp.wait()


def specs(kinds):
    table = {"s": pltpu.SMEM, "v": pltpu.VMEM, "h": pl.ANY}
    return [pl.BlockSpec(memory_space=table[k]) for k in kinds]


def sds(shape, dtype):
    return jax.ShapeDtypeStruct(shape, dtype)


def run_layer(nz, lengths, tokens, cotangent, vecs, wqkv, wproj, wup, wdown):
    seq, width = tokens.shape
    half = width // 2
    pairs = width // PAIR
    groups = pairs // 2
    parts = wup.shape[1] // width // 2
    own, rows = wup.shape[0], wdown.shape[0]
    chip = (2, nz, 2)
    padded = -(-own // 16) * 16

    def vmem(*dims, dtype=bf16):
        return pltpu.VMEM(dims, dtype)

    def landing(lead, block):
        return [pltpu.VMEM(lead + dims + block, bf16) for dims in (chip, (2, nz), (nz,), (nz - 1,))]

    qkv_landing = landing((groups,), (2 * own, 3 * PAIR))
    handover = [
        vmem(parts, own, width, dtype=f32),
        vmem(own, half, dtype=f32),
        vmem(groups, own, 3 * PAIR, dtype=f32),
    ]
    scratch = (
        [
            vmem(seq, width),
            vmem(width, seq),
            vmem(pairs, seq, 3 * PAIR),
            vmem(pairs, PAIR, seq),
            vmem(seq, width),
            vmem(2 * pairs, seq, dtype=f32),
            vmem(seq, width, dtype=f32),
            vmem(width, seq),
            vmem(seq, width, dtype=f32),
            vmem(seq, width, dtype=f32),
            vmem(seq, width),
            vmem(16, width, dtype=f32),
            vmem(groups, 2, *chip, 2 * own, 3 * PAIR),
            vmem(2, *chip, 2 * own, half),
            vmem(2, parts, *chip, 2 * own, width),
            vmem(*chip, 2, rows, width),
            vmem(*chip, 2, 16, PAIR),
            vmem(groups, 2, padded, 3 * PAIR),
            vmem(2, padded, half),
            vmem(2, parts, padded, width),
            vmem(groups, padded, 3 * PAIR),
            vmem(padded, half),
            vmem(parts, padded, width),
            pltpu.SemaphoreType.DMA((9, 8 + nz - 1)),
            pltpu.SemaphoreType.DMA((9, 8 + nz - 1)),
            vmem(2, 5, 8, width, dtype=f32),
        ]
        + landing((parts,), (2 * own, width))
        + landing((parts,), (rows // 2, width))
        + landing((), (2 * own, half))
        + qkv_landing[1:]
        + qkv_landing[:1]
        + handover
        + handover
        + [
            vmem(2, 2 + nz, 8, width, dtype=f32),
            pltpu.SemaphoreType.DMA((10, 3 + nz)),
            pltpu.SemaphoreType.DMA((10, 3 + nz)),
            pltpu.SemaphoreType.DMA((10,)),
            pltpu.SemaphoreType.DMA((10,)),
            pltpu.SemaphoreType.DMA((2,)),
        ]
    )
    return pl.pallas_call(
        layer_kernel,
        in_specs=specs("shvvvvvv"),
        out_specs=specs("hhvvvvv"),
        out_shape=[
            sds((seq, width), bf16),
            sds((seq, width), bf16),
            sds((own, 3 * width), f32),
            sds((own, width), f32),
            sds((own, 2 * parts * width), f32),
            sds((rows, width), f32),
            sds((16, PAIR), f32),
        ],
        scratch_shapes=scratch,
        compiler_params=pltpu.CompilerParams(vmem_limit_bytes=VMEM_LIMIT, collective_id=0, has_side_effects=True),
        name="layer",
    )(lengths, tokens, cotangent, vecs, wqkv, wproj, wup, wdown)


def run_forward(lengths, tokens, cotangent, vecs, wqkv, wproj, wup, wdown):
    seq, width = tokens.shape
    pairs = width // PAIR
    chunks = wup.shape[0]
    return pl.pallas_call(
        forward_kernel,
        in_specs=specs("svvvvvvv"),
        out_specs=specs("hhhhhhhhhhv"),
        out_shape=[
            sds((seq, width), bf16),
            sds((pairs, seq, 3 * PAIR), bf16),
            sds((pairs, PAIR, seq), bf16),
            sds((2 * pairs, seq), f32),
            sds((pairs, seq, PAIR), bf16),
            sds((seq, width), f32),
            sds((width, seq), bf16),
            sds((chunks, width, width), bf16),
            sds((chunks, width, width), bf16),
            sds((2, width, width // 2), bf16),
            sds((8, width), f32),
        ],
        scratch_shapes=[
            pltpu.VMEM((seq, width), bf16),
            pltpu.VMEM((width, seq), bf16),
            pltpu.VMEM((pairs, seq, 3 * PAIR), bf16),
            pltpu.VMEM((pairs, PAIR, seq), bf16),
            pltpu.VMEM((seq, width), bf16),
            pltpu.VMEM((2 * pairs, seq), f32),
            pltpu.VMEM((seq, width), f32),
            pltpu.VMEM((seq, width), bf16),
            pltpu.VMEM((width, seq), bf16),
            pltpu.VMEM((seq, width), f32),
            pltpu.VMEM((seq, width), f32),
            pltpu.VMEM((seq, width), bf16),
            pltpu.VMEM((seq, width), bf16),
            pltpu.VMEM((2, width, width), bf16),
            pltpu.SemaphoreType.DMA((8 + pairs,)),
        ],
        compiler_params=pltpu.CompilerParams(vmem_limit_bytes=VMEM_LIMIT),
        name="layer_forward",
    )(lengths, tokens, cotangent, vecs, wqkv, wproj, wup, wdown)


def run_backward(lengths, tokens, vecs, proj, ot, lse, do, gmid, n1t, wqkv):
    seq, width = tokens.shape
    pairs = width // PAIR
    return pl.pallas_call(
        backward_kernel,
        in_specs=specs("svvhhhhhhv"),
        out_specs=specs("hhv"),
        out_shape=[
            sds((seq, width), bf16),
            sds((pairs, width, 3 * PAIR), bf16),
            sds((8, width), f32),
        ],
        scratch_shapes=[
            pltpu.VMEM((pairs, seq, 3 * PAIR), bf16),
            pltpu.VMEM((pairs, PAIR, seq), bf16),
            pltpu.VMEM((2 * pairs, seq), f32),
            pltpu.VMEM((pairs, seq, PAIR), bf16),
            pltpu.VMEM((seq, width), f32),
            pltpu.VMEM((width, seq), bf16),
            pltpu.VMEM((pairs, width, 3 * PAIR), bf16),
            pltpu.VMEM((seq, width), bf16),
            pltpu.SemaphoreType.DMA((6 + pairs,)),
        ],
        compiler_params=pltpu.CompilerParams(vmem_limit_bytes=VMEM_LIMIT),
        name="attention_backward",
    )(lengths, tokens, vecs, proj, ot, lse, do, gmid, n1t, wqkv)


def gathered(item, axis=0):
    return lax.all_gather(item, AXES, axis=axis, tiled=True)


def scattered(item, axis=0):
    return lax.psum_scatter(item, AXES, scatter_dimension=axis, tiled=True)


def per_device(
    nz, tokens, cotangent, lengths, attn_gain, attn_shift, qkv_weight, qv_bias, proj_weight, proj_bias,
    mlp_gain, mlp_shift, up_weight, up_bias, down_weight, down_bias,
):
    seq, width = tokens.shape
    pairs = width // PAIR
    own = attn_gain.shape[0]
    chunks = up_weight.shape[1] // width
    small = jnp.stack([attn_gain, attn_shift, qv_bias[0], qv_bias[1], proj_bias, mlp_gain, mlp_shift, down_bias])
    if nz:
        vecs = jnp.concatenate(
            [
                jnp.pad(small, ((0, 0), (0, PAIR - own))),
                jnp.pad(up_bias[None], ((0, 7), (0, PAIR - up_bias.shape[0]))),
            ]
        )
        block_out, input_grad, g_qkv, g_proj, g_up, g_down, v = run_layer(
            nz, lengths, tokens, cotangent, vecs, qkv_weight, proj_weight, up_weight, down_weight
        )
        w = v[:, :own]
        return (
            block_out, input_grad, w[8], w[9], g_qkv, w[10:12], g_proj, w[2], w[0], w[1],
            g_up, v[4, : up_bias.shape[0]], g_down, w[3],
        )
    allvec = gathered(jnp.concatenate([small.reshape(-1), up_bias])[None])
    many = allvec.shape[0]
    table = allvec[:, : 8 * own].reshape(many, 8, own).transpose(1, 0, 2).reshape(8, width)
    vecs = jnp.concatenate([table, allvec[:, 8 * own :].reshape(chunks, width)], 0).astype(f32)
    wqkv = gathered(qkv_weight).reshape(width, 3, pairs, PAIR).transpose(2, 0, 1, 3).reshape(pairs, width, 3 * PAIR)
    wproj = gathered(proj_weight).reshape(width, 2, width // 2).transpose(1, 0, 2)
    wup = gathered(up_weight).reshape(width, chunks, width).transpose(1, 0, 2)
    wdown = gathered(down_weight).reshape(chunks, width, width)
    block_out, proj, ot, lse, do, gmid, n1t, gup, gdown, gproj, vg_one = run_forward(
        lengths, tokens, cotangent, vecs, wqkv, wproj, wup, wdown
    )
    input_grad, gqkv, vg_two = run_backward(lengths, tokens, vecs, proj, ot, lse, do, gmid, n1t, wqkv)
    g_down = scattered(gdown.astype(f32).reshape(chunks * width, width))
    g_up = scattered(gup.astype(f32).transpose(1, 0, 2).reshape(width, chunks * width))
    g_proj = scattered(gproj.astype(f32).transpose(1, 0, 2).reshape(width, width))
    g_qkv = scattered(
        gqkv.astype(f32).reshape(pairs, width, 3, PAIR).transpose(1, 2, 0, 3).reshape(width, 3 * width)
    )
    rest = jnp.concatenate([vg_two[:4], vg_one[:4]], 0).reshape(8, many, own).transpose(1, 0, 2).reshape(many, -1)
    rest = jnp.concatenate([rest, vg_one[4:].reshape(many, -1)], 1)
    mine = scattered(rest)[0]
    v = mine[: 8 * own].reshape(8, own)
    return (
        block_out, input_grad, v[0], v[1], g_qkv, v[2:4], g_proj, v[6], v[4], v[5],
        g_up, mine[8 * own :], g_down, v[7],
    )


def chips_along_z(mesh):
    dp, shard = mesh.shape["dp"], mesh.shape["shard"]
    return shard // 4 if dp == 2 and shard == 16 else 0


def solution(mesh):
    one, two, mid = P(AXES), P(AXES, None), P(None, AXES)
    return jax.shard_map(
        functools.partial(per_device, chips_along_z(mesh)),
        mesh=mesh,
        in_specs=(two, two, one, one, one, two, mid, two, one, one, one, two, one, two, one),
        out_specs=(two, two, one, one, two, mid, two, one, one, one, two, one, two, one),
        check_vma=False,
    )
```

```python
import functools

import jax
import jax.numpy as jnp
from jax import lax
from jax.experimental import pallas as pl
from jax.experimental.pallas import tpu as pltpu
from jax.sharding import PartitionSpec as P

f32 = jnp.float32
bf16 = jnp.bfloat16
HD = 64
PAIR = 2 * HD
EPS = 1e-06
MASKED = -1e30
AXES = ("dp", "shard")
VMEM_LIMIT = 65280 * 2**10

AG, AS, QB, VB, PB, MG, MS, DB, UB = range(9)


def dg(a, b, ca, cb):
    return lax.dot_general(a, b, (((ca,), (cb,)), ((), ())), preferred_element_type=f32)


def rows_of(v):
    return v.reshape(-1, v.shape[-1])


def norm_parts(v):
    center = v - jnp.mean(v, -1, keepdims=True)
    inv = lax.rsqrt(jnp.mean(center * center, -1, keepdims=True) + EPS)
    return center * inv, inv


def norm_back(n, inv, z):
    return inv * (z - jnp.mean(z, -1, keepdims=True) - n * jnp.mean(z * n, -1, keepdims=True))


def key_bias(length, seq):
    return jnp.where(lax.broadcasted_iota(jnp.int32, (seq, 1), 0) < length, 0.0, MASKED).astype(f32)


def head_only(v, hh):
    lane = lax.broadcasted_iota(jnp.int32, (1, PAIR), 1)
    return jnp.where(lane // HD == hh, v, jnp.zeros((), v.dtype))


class Place:
    def __init__(self, nz):
        shard = lax.axis_index("shard")
        self.nz = nz
        self.y = lax.axis_index("dp")
        self.c = lax.rem(shard, 2)
        self.x = lax.rem(lax.div(shard, 2), 2)
        self.z = lax.div(shard, 4)
        fy, fx = 1 - 2 * self.y, 1 - 2 * self.x
        self.ay, self.ax = self.y + (1 - self.c) * fy, self.x + self.c * fx
        self.by, self.bx = self.y + self.c * fy, self.x + (1 - self.c) * fx

    def device(self, y, z, x, c):
        return (y, (z * 2 + x) * 2 + c)

    def peer(self):
        return self.device(self.y, self.z, self.x, 1 - self.c)

    def along_z(self, k):
        return self.device(self.y, lax.rem(self.z + k, self.nz), self.x, self.c)

    def a(self):
        return self.device(self.ay, self.z, self.ax, self.c)

    def b(self):
        return self.device(self.by, self.z, self.bx, self.c)

    def partners(self):
        return [self.peer(), self.a(), self.b()] + [self.along_z(k) for k in range(1, self.nz)]


def enter(place):
    barrier = pltpu.get_barrier_semaphore()
    partners = place.partners()
    for d in partners:
        pl.semaphore_signal(barrier, inc=1, device_id=d, device_id_type=pl.DeviceIdType.MESH)
    pl.semaphore_wait(barrier, len(partners))


def remote(src, dst, send, recv, device):
    return pltpu.make_async_remote_copy(
        src_ref=src, dst_ref=dst, send_sem=send, recv_sem=recv, device_id=device,
        device_id_type=pl.DeviceIdType.MESH,
    )


class Gather:
    def __init__(self, place, block, column, swap, send, recv):
        self.p, self.block, self.column, self.swap = place, block, column, swap
        self.send, self.recv = send, recv
        self.started = []

    def move(self, slot, src, dst, device):
        return remote(src, dst, self.send.at[slot], self.recv.at[slot], device)

    def go(self, copy):
        copy.start()
        self.started.append(copy)

    def exchange(self):
        src, dst, _ = self.swap
        return self.move(0, src, dst, self.p.peer())

    def X(self):
        self.go(self.exchange())

    def zs(self):
        p = self.p
        own = self.block(p.y, p.z, p.x, p.c)
        return [self.move(k, own, own, p.along_z(k)) for k in range(1, p.nz)]

    def over(self, slot, y, x, device):
        v = self.column(y, x, self.p.c)
        return self.move(slot, v, v, device)

    def to_b(self):
        return self.over(4, self.p.y, self.p.x, self.p.b())

    def to_a(self, second):
        p = self.p
        y, x = (p.by, p.bx) if second else (p.y, p.x)
        return self.over(5 + second, y, x, p.a())

    def across(self, i):
        p = self.p
        y, x = [(p.y, p.x), (p.by, p.bx), (p.ay, p.ax), (1 - p.y, 1 - p.x)][i]
        return self.over(7 + i, y, x, p.peer())

    def Z(self):
        if self.swap is not None:
            self.exchange().wait()
            self.swap[2]()
        for cp in self.zs():
            self.go(cp)

    def B(self):
        for cp in self.zs():
            cp.wait_recv()
        self.go(self.to_b())
        self.go(self.to_a(0))
        self.go(self.across(0))

    def A(self):
        self.to_b().wait_recv()
        self.go(self.to_a(1))
        self.go(self.across(1))

    def C(self):
        self.to_a(0).wait_recv()
        self.go(self.across(2))
        self.to_a(1).wait_recv()
        self.go(self.across(3))

    def D(self):
        for i in range(4):
            self.across(i).wait_recv()

    def finish(self):
        for cp in self.zs() + [self.to_b(), self.to_a(0), self.to_a(1)] + [self.across(i) for i in range(4)]:
            cp.wait_send()


class Scatter:
    def __init__(self, place, own, other, bufs, send, recv, total):
        self.p, self.own, self.other = place, own, other
        self.r0, self.r1, self.r2, self.r3 = bufs
        self.send, self.recv, self.total = send, recv, total

    def move(self, slot, src, dst, device):
        return remote(src, dst, self.send.at[slot], self.recv.at[slot], device)

    def swap(self):
        return self.move(0, self.other, self.r0, self.p.peer())

    def to_a(self, i):
        p = self.p
        src = self.own.at[p.ay, :, p.ax] if i == 0 else self.own.at[1 - p.y, :, 1 - p.x]
        return self.move(1 + i, src, self.r1.at[i], p.a())

    def to_b(self):
        p = self.p
        return self.move(3, self.own.at[p.by, :, p.bx], self.r2, p.b())

    def to_z(self, k):
        p = self.p
        return self.move(3 + k, self.own.at[p.y, lax.rem(p.z + k, p.nz), p.x], self.r3.at[k - 1], p.along_z(k))

    def add(self, y, x, other):
        self.own[y, :, x] = self.own[y, :, x] + other

    def S0(self):
        self.swap().start()

    def S1(self):
        p = self.p
        self.swap().wait()
        for i, (y, x) in enumerate([(p.ay, p.ax), (1 - p.y, 1 - p.x), (p.by, p.bx), (p.y, p.x)]):
            self.add(y, x, self.r0[y, :, x])
            if i < 2:
                self.to_a(i).start()

    def S2(self):
        p = self.p
        self.to_a(1).wait_recv()
        self.add(p.by, p.bx, self.r1[1])
        self.to_b().start()
        self.to_a(0).wait_recv()
        self.add(p.y, p.x, self.r1[0])

    def S3(self):
        p = self.p
        self.to_b().wait_recv()
        self.add(p.y, p.x, self.r2[...])
        for k in range(1, p.nz):
            self.to_z(k).start()

    def S4(self):
        p = self.p
        total = self.own[p.y, p.z, p.x].astype(f32)
        for k in range(1, p.nz):
            self.to_z(k).wait_recv()
            total += self.r3[k - 1].astype(f32)
        self.total(total)

    def finish(self):
        for cp in [self.to_a(0), self.to_a(1), self.to_b()] + [
            self.to_z(k) for k in range(1, self.p.nz)
        ]:
            cp.wait_send()


class Handover:
    def __init__(self, place, stage, landing, write, send, recv):
        self.p, self.stage, self.landing, self.write = place, stage, landing, write
        self.copy = remote(stage, landing, send, recv, place.peer())

    def start(self, total):
        own = total.shape[0] // 2
        top, bottom = total[:own], total[own:]
        self.stage[...] = jnp.where(self.p.c == 0, bottom, top)
        self.copy.start()
        self.write(self.p.c, jnp.where(self.p.c == 0, top, bottom))

    def S5(self):
        self.copy.wait_recv()
        self.write(1 - self.p.c, self.landing[...])

    def end(self):
        self.copy.wait_send()


class VectorSum:
    def __init__(self, place, value, bufs, send, recv):
        self.p, self.value, self.bufs, self.send, self.recv = place, value, bufs, send, recv

    def move(self, slot):
        p = self.p
        device = [p.peer(), p.a(), p.b()][slot] if slot < 3 else p.along_z(slot - 2)
        return remote(
            self.value.at[min(slot, 3)], self.bufs.at[slot], self.send.at[slot], self.recv.at[slot], device
        )

    def S0(self):
        self.move(0).start()

    def step(self, slot):
        self.move(slot - 1).wait_recv()
        self.value[slot] = self.value[slot - 1] + self.bufs[slot - 1]
        for k in range(self.p.nz - 1 if slot == 3 else 1):
            self.move(slot + k).start()

    def S1(self):
        self.step(1)

    def S2(self):
        self.step(2)

    def S3(self):
        self.step(3)

    def S4(self):
        total = self.value[3]
        for k in range(self.p.nz - 1):
            self.move(3 + k).wait_recv()
            total += self.bufs[3 + k]
        self.value[4] = total

    def finish(self):
        for slot in range(2 + self.p.nz):
            self.move(slot).wait_send()


def expand_table(vbuf, vec, ub, own, piece):
    many = vbuf.shape[0] * vbuf.shape[1] * vbuf.shape[2] * vbuf.shape[3]
    flat = vbuf[...].reshape(many * 16, PAIR)

    def spread(n, each, first=0):
        lane = lax.broadcasted_iota(jnp.int32, (PAIR, n), 1)
        row = lax.broadcasted_iota(jnp.int32, (PAIR, n), 0) - first
        return (lax.rem(lane, each) == row).astype(f32).astype(bf16)

    def mine(full, each):
        shape = (many,) + (1,) * (full.ndim - 2) + full.shape[-1:]
        where = lax.broadcasted_iota(jnp.int32, shape, len(shape) - 1) - each * lax.broadcasted_iota(
            jnp.int32, shape, 0
        )
        return jnp.where((where >= 0) & (where < each), full, 0.0)

    full = dg(flat, spread(vec.shape[1], own), 1, 0).reshape(many, 16, vec.shape[1])
    vec[...] = jnp.sum(mine(full, own), 0)
    pick = (
        lax.broadcasted_iota(jnp.int32, (many, many * 16), 1)
        == 16 * lax.broadcasted_iota(jnp.int32, (many, many * 16), 0) + 8
    )
    row = dg(pick.astype(f32).astype(bf16), flat, 1, 0).astype(bf16)
    for i in range(ub.shape[0]):
        full = dg(row, spread(ub.shape[2], piece, i * piece), 1, 0)
        ub[i] = jnp.sum(mine(full, piece), 0, keepdims=True)


def regroup(pieces, piece):
    n = pieces * PAIR
    src = lax.broadcasted_iota(jnp.int32, (n, n), 0)
    dst = lax.broadcasted_iota(jnp.int32, (n, n), 1)
    inner = lax.rem(dst, PAIR)
    want = lax.div(inner, piece) * (pieces * piece) + lax.div(dst, PAIR) * piece + lax.rem(inner, piece)
    return (src == want).astype(f32)


def gather_items(place, own_down, wqkv, wproj, wup, wdown, vbuf, xs, xr, send, recv):
    p = place
    (xs_qkv, xs_proj, xs_up), (xr_qkv, xr_proj, xr_up) = xs, xr
    own = wqkv.shape[-2] // 2

    def joined(mine, theirs, write):
        def go():
            m, t = mine()[:own].astype(f32), theirs()[:own].astype(f32)
            lo, hi = jnp.where(p.c == 0, m, t), jnp.where(p.c == 0, t, m)
            write(jnp.concatenate([lo, hi], 0).astype(bf16))
        return go

    items = []

    def add(block, column, swap):
        i = len(items)
        items.append(Gather(p, block, column, swap, send.at[i], recv.at[i]))

    add(lambda y, z, x, c: vbuf.at[y, z, x, c], lambda y, x, c: vbuf.at[y, :, x, c], None)

    def add_swapped(view, xs_of, xr_of):
        block = lambda y, z, x, c: view(c).at[y, z, x]
        column = lambda y, x, c: view(c).at[y, :, x]

        def write(v):
            view(p.c)[p.y, p.z, p.x] = v

        add(block, column, (xs_of(1 - p.c), xr_of, joined(lambda: xs_of(p.c)[...], lambda: xr_of[...], write)))

    for g in range(wqkv.shape[0]):
        add_swapped(lambda c, g=g: wqkv.at[g, c], lambda c, g=g: xs_qkv(g, c), xr_qkv.at[g])
    add_swapped(lambda c: wproj.at[c], xs_proj, xr_proj)
    for k in range(wup.shape[0]):
        add(
            lambda y, z, x, c, k=k: wdown.at[k, y, z, x, c],
            lambda y, x, c, k=k: wdown.at[k, y, :, x, c],
            None,
        )
        add_swapped(lambda c, k=k: wup.at[k, c], lambda c, k=k: xs_up(k, c), xr_up.at[k])
    return items


def slice_lanes(v, first, count):
    lane = lax.broadcasted_iota(jnp.int32, (v.shape[1], PAIR), 0) - first
    out = lax.broadcasted_iota(jnp.int32, (v.shape[1], PAIR), 1)
    pick = ((lane == out) & (out < count)).astype(f32)
    return lax.dot_general(
        v, pick, (((1,), (0,)), ((), ())), precision=lax.Precision.HIGHEST, preferred_element_type=f32
    )


def attend(k2, v2t, q2, bias_k, write):
    ones = jnp.ones((16, k2.shape[0]), bf16)
    for hh in range(2):
        s = dg(k2, head_only(q2, hh), 1, 1) + bias_k
        top = jnp.max(s, 0, keepdims=True)
        e = jnp.exp(s - top).astype(bf16)
        o = dg(jnp.concatenate([v2t[HD * hh : HD * hh + HD], ones], 0), e, 1, 0)
        total = o[HD : HD + 1]
        write(hh, o[:HD] / total, top + jnp.log(total))


def attend_back(q_of, k2, v2, do_of, ot_of, lse_of, bias_k, block, between):
    seq = k2.shape[0]
    scale = HD**-0.5
    k2t = k2.T
    dk = dv = None
    dqt = []
    for hh in range(2):
        rows = slice(HD * hh, HD * hh + HD)
        parts = []
        for i in range(seq // block):
            sl = slice(i * block, (i + 1) * block)
            qm = head_only(q_of(sl) * jnp.asarray(scale, bf16), hh)
            d = do_of(sl)
            dm = head_only(d, hh)
            delta = jnp.sum(d.astype(f32).T[rows] * ot_of(rows, sl).astype(f32), 0, keepdims=True)
            e = jnp.exp(dg(k2, qm, 1, 1) + bias_k - lse_of(hh, sl))
            ds = (e * (dg(v2, dm, 1, 1) - delta)).astype(bf16)
            t = dg(e.astype(bf16), dm, 1, 0)
            dv = t if dv is None else dv + t
            t = dg(ds, qm, 1, 0)
            dk = t if dk is None else dk + t
            parts.append(dg(k2t[rows], ds, 1, 0) * scale)
        dqt.append(jnp.concatenate(parts, 1))
        if hh == 0:
            between()
    return jnp.concatenate(dqt, 0), dk, dv


def up_step(n2, cot, up, down, up_bias):
    h = dg(n2, up(), 1, 0) + up_bias
    phi = 0.5 * (1.0 + lax.erf(h * 0.7071067811865476))
    a = (h * phi).astype(bf16)
    ga = dg(cot, down(), 1, 1)
    g = (ga * (phi + h * jnp.exp(-0.5 * h * h) * 0.3989422804014327)).astype(bf16)
    return a, g


def pick(index, choices):
    v = choices[0]
    for i in range(1, len(choices)):
        v = jnp.where(index == i, choices[i], v)
    return v


def blocks(count, size, body):
    @pl.loop(0, count)
    def _(r):
        body(r, pl.ds(pl.multiple_of(r * size, size), size))


VECI, G0, G1, G2, PROJ, D0, U0, D1, U1, D2, U2 = range(11)
SV1, SD0, SU0, SD1, SU1, SD2, SU2, SP, SG0, SG1, SG2, SV2 = range(20, 32)
PLAN = {
    "stats": [("B", VECI), ("B", G0), ("Z", G2), ("A", VECI), ("B", G1), ("A", G0), ("C", VECI), ("D", VECI)],
    "norm": [("Z", PROJ), ("C", G0), ("B", G2), ("A", G1), ("Z", D0), ("D", G0)],
    "f0": [("Z", U0), ("C", G1), ("A", G2), ("B", PROJ), ("B", D0)],
    "f1": [("Z", D1), ("D", G1), ("C", G2), ("A", PROJ), ("B", U0)],
    "f2": [("Z", U1), ("C", PROJ), ("A", D0), ("B", D1)],
    "f3": [("Z", D2), ("D", G2), ("A", U0), ("B", U1), ("C", D0)],
    "f4": [("Z", U2), ("A", D1), ("C", U0)],
    "f5": [("B", D2), ("D", PROJ), ("D", D0), ("C", D1)],
    "m0": [("D", U0), ("A", U1), ("B", U2)],
    "m0g": [("finish", D0), ("finish", U0)],
    "m1": [("A", D2), ("C", U1), ("D", D1)],
    "m2": [("S0", SD0), ("S0", SU0), ("D", U1), ("A", U2), ("C", D2)],
    "m2g": [("finish", D1), ("finish", U1)],
    "m3": [("C", U2), ("D", D2), ("S1", SD0), ("S1", SU0)],
    "m4": [("S0", SD1), ("S0", SU1), ("D", U2), ("S2", SD0)],
    "m4g": [("finish", D2), ("finish", U2)],
    "m5": [("S1", SD1), ("S2", SU0)],
    "m6": [("S0", SD2), ("S0", SU2), ("S1", SU1), ("S3", SD0), ("S2", SD1), ("finish", PROJ)],
    "mid": [("S0", SP), ("S0", SV1), ("S1", SD2), ("S3", SU0), ("S4", SD0), ("S2", SU1)],
    "b0h": [("S1", SU2), ("S3", SD1), ("S1", SV1)],
    "b0": [("S1", SP), ("S2", SD2), ("S3", SU1), ("S4", SU0), ("S2", SV1)],
    "b1h": [("S4", SD1), ("S5", SU0), ("S3", SV1)],
    "b1": [("S0", SG0), ("S2", SU2), ("S4", SU1), ("S4", SV1)],
    "b2h": [("S1", SG0), ("S2", SP), ("S3", SD2), ("S5", SU1), ("S3", SU2)],
    "b2": [("S4", SD2)],
    "b3h": [("S2", SG0), ("S3", SP), ("S4", SU2)],
    "b3": [("S0", SG1), ("S3", SG0), ("S5", SU2), ("S4", SP)],
    "b4h": [("S1", SG1), ("S5", SP)],
    "b4": [("S4", SG0)],
    "b5h": [("S2", SG1), ("S5", SG0)],
    "b5": [("S0", SG2), ("S3", SG1)],
    "r0": [("S1", SG2)],
    "r1": [("S4", SG1)],
    "r2": [("S5", SG1)],
    "r3": [("S0", SV2), ("S2", SG2)],
    "end": [("S1", SV2), ("S3", SG2), ("S2", SV2), ("S3", SV2), ("S4", SG2), ("S4", SV2), ("S5", SG2)],
}


def layer_kernel(
    len_ref, tok_hbm, cot_ref, vec_in, wqkv_in, wproj_in, wup_in, wdown_in,
    out_hbm, gin_hbm, oqkv, oproj, oup, odown, vg_out,
    n1, n1t, proj, ot, att, lse, res, n2t, acc, gn2, gh,
    vec_ref, ub_ref, wqkv, wproj, wup, wdown, vbuf, xr_qkv, xr_proj, xr_up, gsend, grecv,
    vsum, up0, up1, up2, up3, down0, down1, down2, down3, proj0, proj1, proj2, proj3, qkv1, qkv2, qkv3,
    qkv0, stage_up, stage_proj, stage_qkv, land_up, land_proj, land_qkv, vbufs, send, recv, hsend, hrecv, sems,
):
    seq, width = cot_ref.shape
    half = width // 2
    pairs = proj.shape[0]
    own, rows = wqkv_in.shape[0], wdown_in.shape[0]
    groups, pieces = wqkv.shape[0], wup.shape[0]
    piece = rows // pieces
    sub = wup.shape[-1]
    place = Place(wqkv.shape[3])
    p_ = place
    n2, act, gin, tok_early, tok_late = n1, att, att, gh, n1
    vg_one, vg_two = vsum.at[0, 0], vsum.at[1, 0]

    def own_gradient(g):
        return up0.at[g, :, :, :, :, pl.ds(0, 3 * PAIR)]

    def other_gradient(g):
        return wup.at[g, 1 - place.c, :, :, :, :, pl.ds(0, 3 * PAIR)]


    padded = xr_proj.shape[0]

    def staged(first, lanes):
        return lambda i, c: n2t.at[pl.ds(pl.multiple_of((first + 2 * i + c) * padded, padded), padded), 0:lanes]

    xs_qkv, xs_up = staged(0, 3 * PAIR), staged(2 * groups, sub)
    xs_proj = functools.partial(staged(2 * (groups + pieces), half), 0)

    items = dict(enumerate(gather_items(
        place, wdown_in, wqkv, wproj, wup, wdown, vbuf, (xs_qkv, xs_proj, xs_up), (xr_qkv, xr_proj, xr_up),
        gsend, grecv,
    )))
    handovers = []

    def add(i, own_half, other_half, bufs, total):
        k = i - SV1
        items[i] = Scatter(p_, own_half, other_half, bufs, send.at[k], recv.at[k], total)

    def add_shared(i, own_half, other_half, bufs, stage, landing, write):
        k = i - SV1
        h = Handover(p_, stage, landing, write, hsend.at[k], hrecv.at[k])
        handovers.append(h)
        add(i, own_half, other_half, bufs, h.start)
        items[i].S5 = h.S5

    for k in range(pieces):

        def write_down(total, k=k):
            odown[k * piece : (k + 1) * piece, :] = total

        add(
            SD0 + 2 * k, wdown.at[k, :, :, :, p_.c], wdown.at[k, :, :, :, 1 - p_.c],
            (down0.at[k], down1.at[k], down2.at[k], down3.at[k]), write_down,
        )

        def write_up(c, v, k=k):
            back = regroup(pieces, piece)[:, k * PAIR : (k + 1) * PAIR]
            for i in range(sub // PAIR):
                lanes = pl.ds(pl.multiple_of((c * (sub // PAIR) + i) * pieces * PAIR, PAIR), pieces * PAIR)
                oup[:, lanes] += lax.dot_general(
                    v[:, i * PAIR : (i + 1) * PAIR], back, (((1,), (1,)), ((), ())),
                    precision=lax.Precision.HIGHEST, preferred_element_type=f32,
                )

        add_shared(
            SU0 + 2 * k, wup.at[k, p_.c], wup.at[k, 1 - p_.c], (up0.at[k], up1.at[k], up2.at[k], up3.at[k]),
            stage_up.at[k], land_up.at[k], write_up,
        )

    def write_proj(c, v):
        oproj[:, pl.ds(pl.multiple_of(c * half, PAIR), half)] = v

    add_shared(SP, wproj.at[p_.c], wproj.at[1 - p_.c], (proj0, proj1, proj2, proj3), stage_proj, land_proj, write_proj)
    for g in range(groups):

        def write_qkv(c, v, g=g):
            for t in range(3):
                oqkv[:, pl.ds(pl.multiple_of(t * width + (2 * g + c) * PAIR, PAIR), PAIR)] = v[
                    :, t * PAIR : (t + 1) * PAIR
                ]

        add_shared(
            SG0 + g, own_gradient(g), other_gradient(g),
            (qkv0.at[g], qkv1.at[g], qkv2.at[g], qkv3.at[g]), stage_qkv.at[g], land_qkv.at[g], write_qkv,
        )
    for i, v in ((SV1, 0), (SV2, 1)):
        items[i] = VectorSum(p_, vsum.at[v], vbufs.at[v], send.at[i - SV1], recv.at[i - SV1])
    finished = set()

    def tick(name):
        for step, i in PLAN.get(name, ()):
            getattr(items[i], step)()
            if step == "finish":
                finished.add(i)

    def ticks(index, names):
        for i, name in enumerate(names):
            if PLAN.get(name):

                @pl.when(index == i)
                def _(name=name):
                    tick(name)

    def w_qkv(p):
        return rows_of(wqkv[lax.div(p, 2), lax.rem(p, 2)])

    def w_up(k, u):
        return rows_of(wup[k, u])

    def w_down(k, u):
        return rows_of(wdown[k, u])

    def w_proj(i):
        return rows_of(wproj[i])

    def vec(i):
        return vec_ref[i : i + 1, :]

    rb = 256
    nb = seq // rb
    tok_copy = pltpu.make_async_copy(tok_hbm, tok_early, sems.at[1])
    tok_copy.start()
    vbuf[p_.y, p_.z, p_.x, p_.c] = vec_in[...]
    for p in range(pairs):
        for t in range(3):
            lanes = slice(t * width + p * PAIR, t * width + (p + 1) * PAIR)
            n2t[p * padded : p * padded + own, t * PAIR : (t + 1) * PAIR] = wqkv_in[:, lanes]
    enter(place)
    for i in (G0, G1, G2):
        items[i].X()
    items[VECI].Z()
    items[G0].Z()
    for i in range(2):
        row = (2 * (groups + pieces) + i) * padded
        n2t[row : row + own, 0:half] = wproj_in[:, i * half : (i + 1) * half]
    order = regroup(pieces, piece).astype(bf16)
    for i in range(2 * sub // PAIR):
        u, q = divmod(i, sub // PAIR)
        v = dg(wup_in[:, i * pieces * PAIR : (i + 1) * pieces * PAIR], order, 1, 0).astype(bf16)
        for k in range(pieces):
            row = (2 * (groups + k) + u) * padded
            n2t[row : row + own, q * PAIR : (q + 1) * PAIR] = v[:, k * PAIR : (k + 1) * PAIR]
    items[G1].Z()
    for i in (PROJ, U0, U1, U2):
        items[i].X()
    for k in range(pieces):
        wdown[k, p_.y, p_.z, p_.x, p_.c] = wdown_in[k * piece : (k + 1) * piece, :]
    oup[...] = jnp.zeros(oup.shape, f32)
    tok_copy.wait()

    def stats(r, sl):
        res[sl, :] = norm_parts(tok_early[sl, :].astype(f32))[0]

    blocks(nb, rb, stats)
    tick("stats")
    expand_table(vbuf, vec_ref, ub_ref, own, piece)

    def norm(r, sl):
        n1[sl, :] = (res[sl, :] * vec(AG) + vec(AS)).astype(bf16)

    blocks(nb, rb, norm)
    n1t[...] = n1[...].T
    tick("norm")

    bias_k = key_bias(len_ref[0], seq)
    q_bias = [vec(QB)[:, i * PAIR : (i + 1) * PAIR] for i in range(pairs)]
    v_bias = [vec(VB)[:, i * PAIR : (i + 1) * PAIR] for i in range(pairs)]

    @pl.loop(0, pairs)
    def _(p):
        qkv = dg(n1[...], w_qkv(p), 1, 0)
        proj[p, :, 0:PAIR] = (qkv[:, 0:PAIR] + pick(p, q_bias)).astype(bf16)
        proj[p, :, PAIR : 2 * PAIR] = qkv[:, PAIR : 2 * PAIR].astype(bf16)
        proj[p, :, 2 * PAIR :] = (qkv[:, 2 * PAIR :] + pick(p, v_bias)).astype(bf16)

        def write(hh, o, total):
            ot[p, HD * hh : HD * hh + HD, :] = o.astype(bf16)
            lse[pl.ds(2 * p + hh, 1), :] = total

        attend(
            proj[p, :, PAIR : 2 * PAIR], proj[p, :, 2 * PAIR :].T,
            proj[p, :, 0:PAIR] * jnp.asarray(HD**-0.5, bf16), bias_k, write,
        )
        ticks(p, [f"f{i}" for i in range(pairs)])

    for p in range(pairs):
        att[:, p * PAIR : (p + 1) * PAIR] = ot[p].T

    def branch(r, sl):
        a = att[sl, :]
        v = tok_early[sl, :].astype(f32) + vec(PB)
        v += jnp.concatenate([dg(a, w_proj(i), 1, 0) for i in range(2)], 1)
        res[sl, :] = v
        acc[sl, :] = v + vec(DB)
        gn2[sl, :] = jnp.zeros((rb, width), f32)
        n2[sl, :] = (norm_parts(v)[0] * vec(MG) + vec(MS)).astype(bf16)

    blocks(nb, rb, branch)
    n2t[...] = n2[...].T

    rm = 512
    @pl.loop(0, 2 * pieces)
    def _(turn):
        k, u = lax.div(turn, 2), lax.rem(turn, 2)
        cols = pl.ds(pl.multiple_of(u * sub, PAIR), sub)
        total = pl.ds(4 + k, 1)
        ticks(turn, [f"m{i}" for i in range(2 * pieces)])
        vg_one[total, cols] = jnp.zeros((1, sub), f32)

        def stage_one(r, sl):
            a, g = up_step(n2[sl, :], cot_ref[sl, :], lambda: w_up(k, u), lambda: w_down(k, u), ub_ref[k, :, cols])
            act[sl, 0:sub] = a
            gh[sl, 0:sub] = g
            acc[sl, :] += dg(a, w_down(k, u), 1, 0)
            gn2[sl, :] += dg(g, w_up(k, u), 1, 1)
            vg_one[total, cols] += jnp.sum(g.astype(f32), 0, keepdims=True)

        blocks(seq // rm, rm, stage_one)
        ticks(turn, [f"m{i}g" for i in range(2 * pieces)])
        v = dg(act[:, 0:sub], cot_ref[...], 0, 0).astype(bf16)
        wdown[k, u] = v.reshape(wdown.shape[2:])
        wup[k, u] = dg(n2t[...], gh[:, 0:sub], 1, 0).astype(bf16).reshape(wup.shape[2:])

    tick(f"m{2 * pieces}")

    vg_one[0:4, :] = jnp.zeros((4, vg_one.shape[1]), f32)
    vg_one[7:8, :] = jnp.zeros((1, vg_one.shape[1]), f32)

    def back_two(r, sl):
        n2[sl, :] = acc[sl, :].astype(bf16)
        g = gn2[sl, :]
        n, inv = norm_parts(res[sl, :])
        cot = cot_ref[sl, :].astype(f32)
        mid = cot + norm_back(n, inv, g * vec(MG))
        acc[sl, :] = mid
        low = mid.astype(bf16)
        act[sl, :] = low
        vg_one[0:1, 0:width] += jnp.sum(g * n, 0, keepdims=True)
        vg_one[1:2, 0:width] += jnp.sum(g, 0, keepdims=True)
        vg_one[2:3, 0:width] += jnp.sum(low.astype(f32), 0, keepdims=True)
        vg_one[3:4, 0:width] += jnp.sum(cot, 0, keepdims=True)
        back = dg(low[:, :half], w_proj(0), 1, 1) + dg(low[:, half:], w_proj(1), 1, 1)
        gh[sl, :] = back.astype(bf16)

    blocks(nb, rb, back_two)
    out_copy = pltpu.make_async_copy(n2, out_hbm, sems.at[0])
    out_copy.start()
    for i in range(2):
        v = dg(rows_of(ot[...]), act[:, i * half : (i + 1) * half], 1, 0).astype(bf16)
        wproj[i] = v.reshape(wproj.shape[1:])
    vg_two[...] = jnp.zeros(vg_two.shape, f32)
    tick("mid")

    def weight_gradient(p, dst):
        g = proj[p]
        cols = pl.ds(pl.multiple_of(p * PAIR, PAIR), PAIR)
        sums = jnp.sum(g.astype(f32), 0, keepdims=True)
        vg_two[2:3, cols] = sums[:, 0:PAIR]
        vg_two[3:4, cols] = sums[:, 2 * PAIR :]
        dst[...] = dg(n1t[...], g, 1, 0).astype(bf16).reshape(dst.shape)

    @pl.loop(0, pairs)
    def _(p):
        lanes = pl.ds(pl.multiple_of(p * PAIR, PAIR), PAIR)
        dqt, dk, dv = attend_back(
            lambda sl: proj[p, sl, 0:PAIR],
            proj[p, :, PAIR : 2 * PAIR],
            proj[p, :, 2 * PAIR :],
            lambda sl: gh[sl, lanes],
            lambda rows, sl: ot[p, rows, sl],
            lambda hh, sl: lse[pl.ds(2 * p + hh, 1), sl],
            bias_k,
            512,
            lambda: ticks(p, [f"b{i}h" for i in range(pairs)]),
        )
        proj[p, :, 0:PAIR] = dqt.T.astype(bf16)
        proj[p, :, PAIR : 2 * PAIR] = dk.astype(bf16)
        proj[p, :, 2 * PAIR :] = dv.astype(bf16)

        @pl.when(lax.rem(p, 2) == 1)
        def _():
            g = lax.div(p, 2)
            weight_gradient(2 * g + p_.c, own_gradient(g))
            weight_gradient(2 * g + 1 - p_.c, other_gradient(g))

        ticks(p, [f"b{i}" for i in range(pairs)])

    out_copy.wait()
    tok_copy = pltpu.make_async_copy(tok_hbm, tok_late, sems.at[0])
    tok_copy.start()
    tok_copy.wait()

    def back_one(r, sl):
        g = dg(proj[0, sl, :], rows_of(wqkv[0, 0]), 1, 1)
        for p in range(1, pairs):
            g += dg(proj[p, sl, :], rows_of(wqkv[p // 2, p % 2]), 1, 1)
        n, inv = norm_parts(tok_late[sl, :].astype(f32))
        gin[sl, :] = (acc[sl, :] + norm_back(n, inv, g * vec(AG))).astype(bf16)
        vg_two[0:1, 0:width] += jnp.sum(g * n, 0, keepdims=True)
        vg_two[1:2, 0:width] += jnp.sum(g, 0, keepdims=True)
        ticks(r, [f"r{i}" for i in range(nb)])

    blocks(nb, rb, back_one)
    gin_copy = pltpu.make_async_copy(gin, gin_hbm, sems.at[1])
    gin_copy.start()
    index = ((p_.y * p_.nz + p_.z) * 2 + p_.x) * 2 + p_.c
    one = vsum[0, 4]
    vg_out[0:8, :] = slice_lanes(one, index * own, own)
    vg_out[4:7, :] = slice_lanes(one, index * piece, piece)[4:7]
    tick("end")
    vg_out[8:16, :] = slice_lanes(vsum[1, 4], index * own, own)
    for i, item in items.items():
        if i not in finished:
            item.finish()
    for h in handovers:
        h.end()
    gin_copy.wait()


def forward_kernel(
    len_ref, tok_ref, cot_ref, vec_ref, wqkv, wproj, wup, wdown,
    out_hbm, proj_hbm, ot_hbm, lse_hbm, do_hbm, gmid_hbm, n1t_hbm, gup_hbm, gdown_hbm, gproj_hbm, vg_ref,
    n1, n1t, proj, ot, att, lse, res, n2, n2t, acc, gn2, act, gh, gstage, sems,
):
    seq, width = tok_ref.shape
    half = width // 2
    chunks, pairs = gup_hbm.shape[0], proj.shape[0]
    copies = []

    def send_out(src, dst, sem):
        cp = pltpu.make_async_copy(src, dst, sem)
        cp.start()
        copies.append(cp)

    def vec(i):
        return vec_ref[i : i + 1, :]

    rb = 256
    nb = seq // rb

    def norm(r, sl):
        n1[sl, :] = (norm_parts(tok_ref[sl, :].astype(f32))[0] * vec(AG) + vec(AS)).astype(bf16)

    blocks(nb, rb, norm)
    n1t[...] = n1[...].T
    send_out(n1t, n1t_hbm, sems.at[0])
    bias_k = key_bias(len_ref[0], seq)
    q_bias = [vec(QB)[:, i * PAIR : (i + 1) * PAIR] for i in range(pairs)]
    v_bias = [vec(VB)[:, i * PAIR : (i + 1) * PAIR] for i in range(pairs)]

    @pl.loop(0, pairs)
    def _(p):
        qkv = dg(n1[...], wqkv[p], 1, 0)
        proj[p, :, 0:PAIR] = (qkv[:, 0:PAIR] + pick(p, q_bias)).astype(bf16)
        proj[p, :, PAIR : 2 * PAIR] = qkv[:, PAIR : 2 * PAIR].astype(bf16)
        proj[p, :, 2 * PAIR :] = (qkv[:, 2 * PAIR :] + pick(p, v_bias)).astype(bf16)

        def write(hh, o, total):
            ot[p, HD * hh : HD * hh + HD, :] = o.astype(bf16)
            lse[pl.ds(2 * p + hh, 1), :] = total

        attend(
            proj[p, :, PAIR : 2 * PAIR], proj[p, :, 2 * PAIR :].T,
            proj[p, :, 0:PAIR] * jnp.asarray(HD**-0.5, bf16), bias_k, write,
        )

    for p in range(pairs):
        att[:, p * PAIR : (p + 1) * PAIR] = ot[p].T
    send_out(proj, proj_hbm, sems.at[1])
    send_out(ot, ot_hbm, sems.at[2])
    send_out(lse, lse_hbm, sems.at[3])

    def branch(r, sl):
        a = att[sl, :]
        v = tok_ref[sl, :].astype(f32) + vec(PB)
        v += jnp.concatenate([dg(a, wproj[i], 1, 0) for i in range(2)], 1)
        res[sl, :] = v
        acc[sl, :] = v + vec(DB)
        gn2[sl, :] = jnp.zeros((rb, width), f32)
        n2[sl, :] = (norm_parts(v)[0] * vec(MG) + vec(MS)).astype(bf16)

    blocks(nb, rb, branch)
    n2t[...] = n2[...].T
    rm = 512
    staged = []
    for j in range(chunks):
        vg_ref[4 + j : 5 + j, :] = jnp.zeros((1, width), f32)

        def stage_one(r, sl, j=j):
            a, g = up_step(n2[sl, :], cot_ref[sl, :], lambda: wup[j], lambda: wdown[j], vec(UB + j))
            act[sl, :] = a
            gh[sl, :] = g
            acc[sl, :] += dg(a, wdown[j], 1, 0)
            gn2[sl, :] += dg(g, wup[j], 1, 1)
            vg_ref[4 + j : 5 + j, :] += jnp.sum(g.astype(f32), 0, keepdims=True)

        blocks(seq // rm, rm, stage_one)
        for cp in staged:
            cp.wait()
        gstage[0] = dg(act[...], cot_ref[...], 0, 0).astype(bf16)
        gstage[1] = dg(n2t[...], gh[...], 1, 0).astype(bf16)
        staged = [
            pltpu.make_async_copy(gstage.at[0], gdown_hbm.at[j], sems.at[4]),
            pltpu.make_async_copy(gstage.at[1], gup_hbm.at[j], sems.at[5]),
        ]
        for cp in staged:
            cp.start()

    vg_ref[0:4, :] = jnp.zeros((4, width), f32)

    def back_two(r, sl):
        n2[sl, :] = acc[sl, :].astype(bf16)
        g = gn2[sl, :]
        n, inv = norm_parts(res[sl, :])
        cot = cot_ref[sl, :].astype(f32)
        mid = cot + norm_back(n, inv, g * vec(MG))
        acc[sl, :] = mid
        low = mid.astype(bf16)
        act[sl, :] = low
        vg_ref[0:1, :] += jnp.sum(g * n, 0, keepdims=True)
        vg_ref[1:2, :] += jnp.sum(g, 0, keepdims=True)
        vg_ref[2:3, :] += jnp.sum(low.astype(f32), 0, keepdims=True)
        vg_ref[3:4, :] += jnp.sum(cot, 0, keepdims=True)
        gh[sl, :] = (dg(low[:, :half], wproj[0], 1, 1) + dg(low[:, half:], wproj[1], 1, 1)).astype(bf16)

    blocks(nb, rb, back_two)
    send_out(n2, out_hbm, sems.at[6])
    send_out(acc, gmid_hbm, sems.at[7])
    for p in range(pairs):
        send_out(gh.at[:, p * PAIR : (p + 1) * PAIR], do_hbm.at[p], sems.at[8 + p])
    for cp in staged:
        cp.wait()
    for i in range(2):
        gstage[i, :, :half] = dg(rows_of(ot[...]), act[:, i * half : (i + 1) * half], 1, 0).astype(bf16)
        send_out(gstage.at[i, :, pl.ds(0, half)], gproj_hbm.at[i], sems.at[4 + i])
    for cp in copies:
        cp.wait()


def backward_kernel(
    len_ref, tok_ref, vec_ref, proj_hbm, ot_hbm, lse_hbm, do_hbm, gmid_hbm, n1t_hbm, wqkv_ref,
    gin_hbm, gqkv_hbm, vg_ref,
    proj, ot, lse, do, gmid, n1t, gqkv, gin, sems,
):
    seq, width = tok_ref.shape
    pairs = proj.shape[0]

    def start(src, dst, sem):
        cp = pltpu.make_async_copy(src, dst, sem)
        cp.start()
        return cp

    loads = [
        start(proj_hbm, proj, sems.at[0]),
        start(do_hbm, do, sems.at[1]),
        start(ot_hbm, ot, sems.at[2]),
        start(lse_hbm, lse, sems.at[3]),
        start(n1t_hbm, n1t, sems.at[4]),
        start(gmid_hbm, gmid, sems.at[5]),
    ]
    for cp in loads:
        cp.wait()
    vg_ref[...] = jnp.zeros(vg_ref.shape, f32)
    bias_k = key_bias(len_ref[0], seq)

    @pl.loop(0, pairs)
    def _(p):
        dqt, dk, dv = attend_back(
            lambda sl: proj[p, sl, 0:PAIR],
            proj[p, :, PAIR : 2 * PAIR],
            proj[p, :, 2 * PAIR :],
            lambda sl: do[p, sl, :],
            lambda rows, sl: ot[p, rows, sl],
            lambda hh, sl: lse[pl.ds(2 * p + hh, 1), sl],
            bias_k,
            512,
            lambda: None,
        )
        proj[p, :, 0:PAIR] = dqt.T.astype(bf16)
        proj[p, :, PAIR : 2 * PAIR] = dk.astype(bf16)
        proj[p, :, 2 * PAIR :] = dv.astype(bf16)

    outs = []
    for p in range(pairs):
        cols = slice(p * PAIR, (p + 1) * PAIR)
        g = proj[p]
        sums = jnp.sum(g.astype(f32), 0, keepdims=True)
        vg_ref[2:3, cols] = sums[:, 0:PAIR]
        vg_ref[3:4, cols] = sums[:, 2 * PAIR :]
        gqkv[p] = dg(n1t[...], g, 1, 0).astype(bf16)
        outs.append(start(gqkv.at[p], gqkv_hbm.at[p], sems.at[6 + p]))

    def back_one(r, sl):
        g = dg(proj[0, sl, :], wqkv_ref[0], 1, 1)
        for p in range(1, pairs):
            g += dg(proj[p, sl, :], wqkv_ref[p], 1, 1)
        n, inv = norm_parts(tok_ref[sl, :].astype(f32))
        gin[sl, :] = (gmid[sl, :] + norm_back(n, inv, g * vec_ref[AG : AG + 1, :])).astype(bf16)
        vg_ref[0:1, :] += jnp.sum(g * n, 0, keepdims=True)
        vg_ref[1:2, :] += jnp.sum(g, 0, keepdims=True)

    blocks(seq // 256, 256, back_one)
    outs.append(start(gin, gin_hbm, sems.at[0]))
    for cp in outs:
        cp.wait()


def specs(kinds):
    table = {"s": pltpu.SMEM, "v": pltpu.VMEM, "h": pl.ANY}
    return [pl.BlockSpec(memory_space=table[k]) for k in kinds]


def sds(shape, dtype):
    return jax.ShapeDtypeStruct(shape, dtype)


def run_layer(nz, lengths, tokens, cotangent, vecs, wqkv, wproj, wup, wdown):
    seq, width = tokens.shape
    half = width // 2
    pairs = width // PAIR
    groups = pairs // 2
    own, rows = wup.shape[0], wdown.shape[0]
    piece = 32
    pieces = rows // piece
    sub = wup.shape[1] // pieces // 2
    chip = (2, nz, 2)
    padded = -(-own // 16) * 16

    def vmem(*dims, dtype=bf16):
        return pltpu.VMEM(dims, dtype)

    def landing(lead, block):
        return [pltpu.VMEM(lead + dims + block, bf16) for dims in (chip, (2, nz), (nz,), (nz - 1,))]

    qkv_landing = landing((groups,), (2 * own, 3 * PAIR))
    handover = [
        vmem(pieces, own, sub, dtype=f32),
        vmem(own, half, dtype=f32),
        vmem(groups, own, 3 * PAIR, dtype=f32),
    ]
    scratch = (
        [
            vmem(seq, width),
            vmem(width, seq),
            vmem(pairs, seq, 3 * PAIR),
            vmem(pairs, PAIR, seq),
            vmem(seq, width),
            vmem(2 * pairs, seq, dtype=f32),
            vmem(seq, width, dtype=f32),
            vmem(width, seq),
            vmem(seq, width, dtype=f32),
            vmem(seq, width, dtype=f32),
            vmem(seq, width),
            vmem(16, width, dtype=f32),
            vmem(pieces, 1, 2 * sub, dtype=f32),
            vmem(groups, 2, *chip, 2 * own, 3 * PAIR),
            vmem(2, *chip, 2 * own, half),
            vmem(pieces, 2, *chip, 2 * own, sub),
            vmem(pieces, *chip, 2, piece, width),
            vmem(*chip, 2, 16, PAIR),
            vmem(groups, padded, 3 * PAIR),
            vmem(padded, half),
            vmem(pieces, padded, sub),
            pltpu.SemaphoreType.DMA((5 + 2 * pieces, 8 + nz - 1)),
            pltpu.SemaphoreType.DMA((5 + 2 * pieces, 8 + nz - 1)),
            vmem(2, 5, 8, 2 * sub, dtype=f32),
        ]
        + landing((pieces,), (2 * own, sub))
        + landing((pieces,), (piece, width))
        + landing((), (2 * own, half))
        + qkv_landing[1:]
        + qkv_landing[:1]
        + handover
        + handover
        + [
            vmem(2, 2 + nz, 8, 2 * sub, dtype=f32),
            pltpu.SemaphoreType.DMA((12, 3 + nz)),
            pltpu.SemaphoreType.DMA((12, 3 + nz)),
            pltpu.SemaphoreType.DMA((12,)),
            pltpu.SemaphoreType.DMA((12,)),
            pltpu.SemaphoreType.DMA((2,)),
        ]
    )
    return pl.pallas_call(
        layer_kernel,
        in_specs=specs("shvvvvvv"),
        out_specs=specs("hhvvvvv"),
        out_shape=[
            sds((seq, width), bf16),
            sds((seq, width), bf16),
            sds((own, 3 * width), f32),
            sds((own, width), f32),
            sds((own, wup.shape[1]), f32),
            sds((rows, width), f32),
            sds((16, PAIR), f32),
        ],
        scratch_shapes=scratch,
        compiler_params=pltpu.CompilerParams(vmem_limit_bytes=VMEM_LIMIT, collective_id=0, has_side_effects=True),
        name="layer",
    )(lengths, tokens, cotangent, vecs, wqkv, wproj, wup, wdown)


def run_forward(lengths, tokens, cotangent, vecs, wqkv, wproj, wup, wdown):
    seq, width = tokens.shape
    pairs = width // PAIR
    chunks = wup.shape[0]
    return pl.pallas_call(
        forward_kernel,
        in_specs=specs("svvvvvvv"),
        out_specs=specs("hhhhhhhhhhv"),
        out_shape=[
            sds((seq, width), bf16),
            sds((pairs, seq, 3 * PAIR), bf16),
            sds((pairs, PAIR, seq), bf16),
            sds((2 * pairs, seq), f32),
            sds((pairs, seq, PAIR), bf16),
            sds((seq, width), f32),
            sds((width, seq), bf16),
            sds((chunks, width, width), bf16),
            sds((chunks, width, width), bf16),
            sds((2, width, width // 2), bf16),
            sds((8, width), f32),
        ],
        scratch_shapes=[
            pltpu.VMEM((seq, width), bf16),
            pltpu.VMEM((width, seq), bf16),
            pltpu.VMEM((pairs, seq, 3 * PAIR), bf16),
            pltpu.VMEM((pairs, PAIR, seq), bf16),
            pltpu.VMEM((seq, width), bf16),
            pltpu.VMEM((2 * pairs, seq), f32),
            pltpu.VMEM((seq, width), f32),
            pltpu.VMEM((seq, width), bf16),
            pltpu.VMEM((width, seq), bf16),
            pltpu.VMEM((seq, width), f32),
            pltpu.VMEM((seq, width), f32),
            pltpu.VMEM((seq, width), bf16),
            pltpu.VMEM((seq, width), bf16),
            pltpu.VMEM((2, width, width), bf16),
            pltpu.SemaphoreType.DMA((8 + pairs,)),
        ],
        compiler_params=pltpu.CompilerParams(vmem_limit_bytes=VMEM_LIMIT),
        name="layer_forward",
    )(lengths, tokens, cotangent, vecs, wqkv, wproj, wup, wdown)


def run_backward(lengths, tokens, vecs, proj, ot, lse, do, gmid, n1t, wqkv):
    seq, width = tokens.shape
    pairs = width // PAIR
    return pl.pallas_call(
        backward_kernel,
        in_specs=specs("svvhhhhhhv"),
        out_specs=specs("hhv"),
        out_shape=[
            sds((seq, width), bf16),
            sds((pairs, width, 3 * PAIR), bf16),
            sds((8, width), f32),
        ],
        scratch_shapes=[
            pltpu.VMEM((pairs, seq, 3 * PAIR), bf16),
            pltpu.VMEM((pairs, PAIR, seq), bf16),
            pltpu.VMEM((2 * pairs, seq), f32),
            pltpu.VMEM((pairs, seq, PAIR), bf16),
            pltpu.VMEM((seq, width), f32),
            pltpu.VMEM((width, seq), bf16),
            pltpu.VMEM((pairs, width, 3 * PAIR), bf16),
            pltpu.VMEM((seq, width), bf16),
            pltpu.SemaphoreType.DMA((6 + pairs,)),
        ],
        compiler_params=pltpu.CompilerParams(vmem_limit_bytes=VMEM_LIMIT),
        name="attention_backward",
    )(lengths, tokens, vecs, proj, ot, lse, do, gmid, n1t, wqkv)


def gathered(item, axis=0):
    return lax.all_gather(item, AXES, axis=axis, tiled=True)


def scattered(item, axis=0):
    return lax.psum_scatter(item, AXES, scatter_dimension=axis, tiled=True)


def per_device(
    nz, tokens, cotangent, lengths, attn_gain, attn_shift, qkv_weight, qv_bias, proj_weight, proj_bias,
    mlp_gain, mlp_shift, up_weight, up_bias, down_weight, down_bias,
):
    seq, width = tokens.shape
    pairs = width // PAIR
    own = attn_gain.shape[0]
    chunks = up_weight.shape[1] // width
    small = jnp.stack([attn_gain, attn_shift, qv_bias[0], qv_bias[1], proj_bias, mlp_gain, mlp_shift, down_bias])
    if nz:
        vecs = jnp.concatenate(
            [
                jnp.pad(small, ((0, 0), (0, PAIR - own))),
                jnp.pad(up_bias[None], ((0, 7), (0, PAIR - up_bias.shape[0]))),
            ]
        )
        block_out, input_grad, g_qkv, g_proj, g_up, g_down, v = run_layer(
            nz, lengths, tokens, cotangent, vecs, qkv_weight, proj_weight, up_weight, down_weight
        )
        w = v[:, :own]
        return (
            block_out, input_grad, w[8], w[9], g_qkv, w[10:12], g_proj, w[2], w[0], w[1],
            g_up, v[4:7, : up_bias.shape[0] // 3].reshape(-1), g_down, w[3],
        )
    allvec = gathered(jnp.concatenate([small.reshape(-1), up_bias])[None])
    many = allvec.shape[0]
    table = allvec[:, : 8 * own].reshape(many, 8, own).transpose(1, 0, 2).reshape(8, width)
    vecs = jnp.concatenate([table, allvec[:, 8 * own :].reshape(chunks, width)], 0).astype(f32)
    wqkv = gathered(qkv_weight).reshape(width, 3, pairs, PAIR).transpose(2, 0, 1, 3).reshape(pairs, width, 3 * PAIR)
    wproj = gathered(proj_weight).reshape(width, 2, width // 2).transpose(1, 0, 2)
    wup = gathered(up_weight).reshape(width, chunks, width).transpose(1, 0, 2)
    wdown = gathered(down_weight).reshape(chunks, width, width)
    block_out, proj, ot, lse, do, gmid, n1t, gup, gdown, gproj, vg_one = run_forward(
        lengths, tokens, cotangent, vecs, wqkv, wproj, wup, wdown
    )
    input_grad, gqkv, vg_two = run_backward(lengths, tokens, vecs, proj, ot, lse, do, gmid, n1t, wqkv)
    g_down = scattered(gdown.astype(f32).reshape(chunks * width, width))
    g_up = scattered(gup.astype(f32).transpose(1, 0, 2).reshape(width, chunks * width))
    g_proj = scattered(gproj.astype(f32).transpose(1, 0, 2).reshape(width, width))
    g_qkv = scattered(
        gqkv.astype(f32).reshape(pairs, width, 3, PAIR).transpose(1, 2, 0, 3).reshape(width, 3 * width)
    )
    rest = jnp.concatenate([vg_two[:4], vg_one[:4]], 0).reshape(8, many, own).transpose(1, 0, 2).reshape(many, -1)
    rest = jnp.concatenate([rest, vg_one[4:].reshape(many, -1)], 1)
    mine = scattered(rest)[0]
    v = mine[: 8 * own].reshape(8, own)
    return (
        block_out, input_grad, v[0], v[1], g_qkv, v[2:4], g_proj, v[6], v[4], v[5],
        g_up, mine[8 * own :], g_down, v[7],
    )


def chips_along_z(mesh):
    dp, shard = mesh.shape["dp"], mesh.shape["shard"]
    return shard // 4 if dp == 2 and shard == 16 else 0


def solution(mesh):
    one, two, mid = P(AXES), P(AXES, None), P(None, AXES)
    return jax.shard_map(
        functools.partial(per_device, chips_along_z(mesh)),
        mesh=mesh,
        in_specs=(two, two, one, one, one, two, mid, two, one, one, one, two, one, two, one),
        out_specs=(two, two, one, one, two, mid, two, one, one, one, two, one, two, one),
        check_vma=False,
    )
```

```python
import functools

import jax
import jax.numpy as jnp
from jax import lax
from jax.experimental import pallas as pl
from jax.experimental.pallas import tpu as pltpu
from jax.sharding import PartitionSpec as P

f32 = jnp.float32
bf16 = jnp.bfloat16
HD = 64
PAIR = 2 * HD
EPS = 1e-06
MASKED = -1e30
AXES = ("dp", "shard")
VMEM_LIMIT = 65280 * 2**10

AG, AS, QB, VB, PB, MG, MS, DB, UB = range(9)


def dg(a, b, ca, cb):
    return lax.dot_general(a, b, (((ca,), (cb,)), ((), ())), preferred_element_type=f32)


def rows_of(v):
    return v.reshape(-1, v.shape[-1])


def norm_parts(v):
    center = v - jnp.mean(v, -1, keepdims=True)
    inv = lax.rsqrt(jnp.mean(center * center, -1, keepdims=True) + EPS)
    return center * inv, inv


def norm_back(n, inv, z):
    return inv * (z - jnp.mean(z, -1, keepdims=True) - n * jnp.mean(z * n, -1, keepdims=True))


def key_bias(length, seq):
    return jnp.where(lax.broadcasted_iota(jnp.int32, (seq, 1), 0) < length, 0.0, MASKED).astype(f32)


def head_only(v, hh):
    lane = lax.broadcasted_iota(jnp.int32, (1, PAIR), 1)
    return jnp.where(lane // HD == hh, v, jnp.zeros((), v.dtype))


class Place:
    def __init__(self, nz):
        shard = lax.axis_index("shard")
        self.nz = nz
        self.y = lax.axis_index("dp")
        self.c = lax.rem(shard, 2)
        self.x = lax.rem(lax.div(shard, 2), 2)
        self.z = lax.div(shard, 4)
        fy, fx = 1 - 2 * self.y, 1 - 2 * self.x
        self.ay, self.ax = self.y + (1 - self.c) * fy, self.x + self.c * fx
        self.by, self.bx = self.y + self.c * fy, self.x + (1 - self.c) * fx

    def device(self, y, z, x, c):
        return (y, (z * 2 + x) * 2 + c)

    def peer(self):
        return self.device(self.y, self.z, self.x, 1 - self.c)

    def along_z(self, k):
        return self.device(self.y, lax.rem(self.z + k, self.nz), self.x, self.c)

    def a(self):
        return self.device(self.ay, self.z, self.ax, self.c)

    def b(self):
        return self.device(self.by, self.z, self.bx, self.c)

    def partners(self):
        return [self.peer(), self.a(), self.b()] + [self.along_z(k) for k in range(1, self.nz)]


def greet(place):
    for d in place.partners():
        pl.semaphore_signal(
            pltpu.get_barrier_semaphore(), inc=1, device_id=d, device_id_type=pl.DeviceIdType.MESH
        )


def met(place):
    pl.semaphore_wait(pltpu.get_barrier_semaphore(), len(place.partners()))


def remote(src, dst, send, recv, device):
    return pltpu.make_async_remote_copy(
        src_ref=src, dst_ref=dst, send_sem=send, recv_sem=recv, device_id=device,
        device_id_type=pl.DeviceIdType.MESH,
    )


class Gather:
    def __init__(self, place, block, column, swap, send, recv):
        self.p, self.block, self.column, self.swap = place, block, column, swap
        self.send, self.recv = send, recv
        self.started = []

    def move(self, slot, src, dst, device):
        return remote(src, dst, self.send.at[slot], self.recv.at[slot], device)

    def go(self, copy):
        copy.start()
        self.started.append(copy)

    def exchange(self):
        src, dst, _ = self.swap
        return self.move(0, src, dst, self.p.peer())

    def X(self):
        self.go(self.exchange())

    def zs(self):
        p = self.p
        own = self.block(p.y, p.z, p.x, p.c)
        return [self.move(k, own, own, p.along_z(k)) for k in range(1, p.nz)]

    def over(self, slot, y, x, device):
        v = self.column(y, x, self.p.c)
        return self.move(slot, v, v, device)

    def to_b(self):
        return self.over(4, self.p.y, self.p.x, self.p.b())

    def to_a(self, second):
        p = self.p
        y, x = (p.by, p.bx) if second else (p.y, p.x)
        return self.over(5 + second, y, x, p.a())

    def across(self, i):
        p = self.p
        y, x = [(p.y, p.x), (p.by, p.bx), (p.ay, p.ax), (1 - p.y, 1 - p.x)][i]
        return self.over(7 + i, y, x, p.peer())

    def Z(self):
        if self.swap is not None:
            self.exchange().wait()
            self.swap[2]()
        for cp in self.zs():
            self.go(cp)

    def B(self):
        for cp in self.zs():
            cp.wait_recv()
        self.go(self.to_b())
        self.go(self.to_a(0))
        self.go(self.across(0))

    def A(self):
        self.to_b().wait_recv()
        self.go(self.to_a(1))
        self.go(self.across(1))

    def C(self):
        self.to_a(0).wait_recv()
        self.go(self.across(2))
        self.to_a(1).wait_recv()
        self.go(self.across(3))

    def D(self):
        for i in range(4):
            self.across(i).wait_recv()

    def finish(self):
        for cp in self.zs() + [self.to_b(), self.to_a(0), self.to_a(1)] + [self.across(i) for i in range(4)]:
            cp.wait_send()


class Scatter:
    def __init__(self, place, own, other, bufs, send, recv, total):
        self.p, self.own, self.other = place, own, other
        self.r0, self.r1, self.r2, self.r3 = bufs
        self.send, self.recv, self.total = send, recv, total

    def move(self, slot, src, dst, device):
        return remote(src, dst, self.send.at[slot], self.recv.at[slot], device)

    def swap(self):
        return self.move(0, self.other, self.r0, self.p.peer())

    def to_a(self, i):
        p = self.p
        src = self.own.at[p.ay, :, p.ax] if i == 0 else self.own.at[1 - p.y, :, 1 - p.x]
        return self.move(1 + i, src, self.r1.at[i], p.a())

    def to_b(self):
        p = self.p
        return self.move(3, self.own.at[p.by, :, p.bx], self.r2, p.b())

    def to_z(self, k):
        p = self.p
        return self.move(3 + k, self.own.at[p.y, lax.rem(p.z + k, p.nz), p.x], self.r3.at[k - 1], p.along_z(k))

    def add(self, y, x, other):
        self.own[y, :, x] = self.own[y, :, x] + other

    def S0(self):
        self.swap().start()

    def S1(self):
        p = self.p
        self.swap().wait()
        for i, (y, x) in enumerate([(p.ay, p.ax), (1 - p.y, 1 - p.x), (p.by, p.bx), (p.y, p.x)]):
            self.add(y, x, self.r0[y, :, x])
            if i < 2:
                self.to_a(i).start()

    def S2(self):
        p = self.p
        self.to_a(1).wait_recv()
        self.add(p.by, p.bx, self.r1[1])
        self.to_b().start()
        self.to_a(0).wait_recv()
        self.add(p.y, p.x, self.r1[0])

    def S3(self):
        p = self.p
        self.to_b().wait_recv()
        self.add(p.y, p.x, self.r2[...])
        for k in range(1, p.nz):
            self.to_z(k).start()

    def S4(self):
        p = self.p
        total = self.own[p.y, p.z, p.x].astype(f32)
        for k in range(1, p.nz):
            self.to_z(k).wait_recv()
            total += self.r3[k - 1].astype(f32)
        self.total(total)

    def finish(self):
        for cp in [self.to_a(0), self.to_a(1), self.to_b()] + [
            self.to_z(k) for k in range(1, self.p.nz)
        ]:
            cp.wait_send()


class Handover:
    def __init__(self, place, stage, landing, write, send, recv):
        self.p, self.stage, self.landing, self.write = place, stage, landing, write
        self.copy = remote(stage, landing, send, recv, place.peer())

    def start(self, total):
        own = total.shape[0] // 2
        top, bottom = total[:own], total[own:]
        self.stage[...] = jnp.where(self.p.c == 0, bottom, top)
        self.copy.start()
        self.write(self.p.c, jnp.where(self.p.c == 0, top, bottom))

    def S5(self):
        self.copy.wait_recv()
        self.write(1 - self.p.c, self.landing[...])

    def end(self):
        self.copy.wait_send()


class VectorSum:
    def __init__(self, place, value, bufs, send, recv):
        self.p, self.value, self.bufs, self.send, self.recv = place, value, bufs, send, recv

    def move(self, slot):
        p = self.p
        device = [p.peer(), p.a(), p.b()][slot] if slot < 3 else p.along_z(slot - 2)
        return remote(
            self.value.at[min(slot, 3)], self.bufs.at[slot], self.send.at[slot], self.recv.at[slot], device
        )

    def S0(self):
        self.move(0).start()

    def step(self, slot):
        self.move(slot - 1).wait_recv()
        self.value[slot] = self.value[slot - 1] + self.bufs[slot - 1]
        for k in range(self.p.nz - 1 if slot == 3 else 1):
            self.move(slot + k).start()

    def S1(self):
        self.step(1)

    def S2(self):
        self.step(2)

    def S3(self):
        self.step(3)

    def S4(self):
        total = self.value[3]
        for k in range(self.p.nz - 1):
            self.move(3 + k).wait_recv()
            total += self.bufs[3 + k]
        self.value[4] = total

    def finish(self):
        for slot in range(2 + self.p.nz):
            self.move(slot).wait_send()


def expand_table(vbuf, vec, ub, own, piece):
    many = vbuf.shape[0] * vbuf.shape[1] * vbuf.shape[2] * vbuf.shape[3]
    flat = vbuf[...].reshape(many * 16, PAIR)

    def spread(n, each, first=0):
        lane = lax.broadcasted_iota(jnp.int32, (1, n), 1)
        row = lax.broadcasted_iota(jnp.int32, (PAIR, n), 0) - first
        return (lax.rem(lane, each) == row).astype(f32).astype(bf16)

    def mine(full, each):
        shape = (many,) + (1,) * (full.ndim - 2) + full.shape[-1:]
        where = lax.broadcasted_iota(jnp.int32, shape, len(shape) - 1) - each * lax.broadcasted_iota(
            jnp.int32, shape, 0
        )
        return jnp.where((where >= 0) & (where < each), full, 0.0)

    full = dg(flat, spread(vec.shape[1], own), 1, 0).reshape(many, 16, vec.shape[1])
    vec[...] = jnp.sum(mine(full, own), 0)
    pick = (
        lax.broadcasted_iota(jnp.int32, (many, many * 16), 1)
        == 16 * lax.broadcasted_iota(jnp.int32, (many, many * 16), 0) + 8
    )
    row = dg(pick.astype(f32).astype(bf16), flat, 1, 0).astype(bf16)
    for i in range(ub.shape[0]):
        full = dg(row, spread(ub.shape[2], piece, i * piece), 1, 0)
        ub[i] = jnp.sum(mine(full, piece), 0, keepdims=True)


def regroup(pieces, piece):
    n = pieces * PAIR
    src = lax.broadcasted_iota(jnp.int32, (n, n), 0)
    dst = lax.broadcasted_iota(jnp.int32, (1, n), 1)
    inner = lax.rem(dst, PAIR)
    want = lax.div(inner, piece) * (pieces * piece) + lax.div(dst, PAIR) * piece + lax.rem(inner, piece)
    return (src == want).astype(f32)


def gather_items(place, own_down, wqkv, wproj, wup, wdown, vbuf, xs, xr, send, recv):
    p = place
    (xs_qkv, xs_proj, xs_up), (xr_qkv, xr_proj, xr_up) = xs, xr
    own = wqkv.shape[-2] // 2

    def joined(mine, theirs, write):
        def go():
            m, t = mine()[:own].astype(f32), theirs()[:own].astype(f32)
            lo, hi = jnp.where(p.c == 0, m, t), jnp.where(p.c == 0, t, m)
            write(jnp.concatenate([lo, hi], 0).astype(bf16))
        return go

    items = []

    def add(block, column, swap):
        i = len(items)
        items.append(Gather(p, block, column, swap, send.at[i], recv.at[i]))

    add(lambda y, z, x, c: vbuf.at[y, z, x, c], lambda y, x, c: vbuf.at[y, :, x, c], None)

    def add_swapped(view, xs_of, xr_of):
        block = lambda y, z, x, c: view(c).at[y, z, x]
        column = lambda y, x, c: view(c).at[y, :, x]

        def write(v):
            view(p.c)[p.y, p.z, p.x] = v

        add(block, column, (xs_of(1 - p.c), xr_of, joined(lambda: xs_of(p.c)[...], lambda: xr_of[...], write)))

    for g in range(wqkv.shape[0]):
        add_swapped(lambda c, g=g: wqkv.at[g, c], lambda c, g=g: xs_qkv(g, c), xr_qkv.at[g])
    add_swapped(lambda c: wproj.at[c], xs_proj, xr_proj)
    for k in range(wup.shape[0]):
        add(
            lambda y, z, x, c, k=k: wdown.at[k, y, z, x, c],
            lambda y, x, c, k=k: wdown.at[k, y, :, x, c],
            None,
        )
        add_swapped(lambda c, k=k: wup.at[k, c], lambda c, k=k: xs_up(k, c), xr_up.at[k])
    return items


def slice_lanes(v, first, count, at=0):
    lane = lax.broadcasted_iota(jnp.int32, (v.shape[1], PAIR), 0) - first
    out = lax.broadcasted_iota(jnp.int32, (v.shape[1], PAIR), 1) - at
    pick = ((lane == out) & (out >= 0) & (out < count)).astype(f32)
    return lax.dot_general(
        v, pick, (((1,), (0,)), ((), ())), precision=lax.Precision.HIGHEST, preferred_element_type=f32
    )


def attend(k2, v2t, q2, bias_k, write):
    ones = jnp.ones((16, k2.shape[0]), bf16)
    for hh in range(2):
        s = dg(k2, head_only(q2, hh), 1, 1) + bias_k
        top = jnp.max(s, 0, keepdims=True)
        e = jnp.exp(s - top).astype(bf16)
        o = dg(jnp.concatenate([v2t[HD * hh : HD * hh + HD], ones], 0), e, 1, 0)
        total = o[HD : HD + 1]
        write(hh, o[:HD] / total, top + jnp.log(total))


def attend_back(q_of, k2, v2, do_of, ot_of, lse_of, bias_k, block, between):
    seq = k2.shape[0]
    scale = HD**-0.5
    k2t = k2.T
    dk = dv = None
    dqt = []
    for hh in range(2):
        rows = slice(HD * hh, HD * hh + HD)
        parts = []
        for i in range(seq // block):
            sl = slice(i * block, (i + 1) * block)
            qm = head_only(q_of(sl) * jnp.asarray(scale, bf16), hh)
            d = do_of(sl)
            dm = head_only(d, hh)
            delta = jnp.sum(d.astype(f32).T[rows] * ot_of(rows, sl).astype(f32), 0, keepdims=True)
            e = jnp.exp(dg(k2, qm, 1, 1) + bias_k - lse_of(hh, sl))
            ds = (e * (dg(v2, dm, 1, 1) - delta)).astype(bf16)
            t = dg(e.astype(bf16), dm, 1, 0)
            dv = t if dv is None else dv + t
            t = dg(ds, qm, 1, 0)
            dk = t if dk is None else dk + t
            parts.append(dg(k2t[rows], ds, 1, 0) * scale)
        dqt.append(jnp.concatenate(parts, 1))
        if hh == 0:
            between()
    return jnp.concatenate(dqt, 0), dk, dv


def up_step(n2, cot, up, down, up_bias):
    h = dg(n2, up(), 1, 0) + up_bias
    phi = 0.5 * (1.0 + lax.erf(h * 0.7071067811865476))
    a = (h * phi).astype(bf16)
    ga = dg(cot, down(), 1, 1)
    g = (ga * (phi + h * jnp.exp(-0.5 * h * h) * 0.3989422804014327)).astype(bf16)
    return a, g


def pick(index, choices):
    v = choices[0]
    for i in range(1, len(choices)):
        v = jnp.where(index == i, choices[i], v)
    return v


def blocks(count, size, body):
    @pl.loop(0, count)
    def _(r):
        body(r, pl.ds(pl.multiple_of(r * size, size), size))


VECI, G0, G1, G2, PROJ, D0, U0, D1, U1, D2, U2 = range(11)
SV1, SD0, SU0, SD1, SU1, SD2, SU2, SP, SG0, SG1, SG2, SV2 = range(20, 32)
PLAN = {
    "stats": [("B", VECI), ("B", G0), ("Z", G2), ("A", VECI), ("B", G1), ("Z", PROJ), ("A", G0), ("C", VECI),
              ("Z", D0), ("D", VECI), ("C", G0)],
    "norm": [("A", G1), ("B", G2), ("Z", U0), ("D", G0)],
    "f0": [("C", G1), ("A", G2), ("B", PROJ), ("B", D0), ("Z", D1)],
    "f1": [("D", G1), ("C", G2), ("B", U0), ("Z", U1)],
    "f2": [("A", PROJ), ("Z", D2)],
    "f3": [("D", G2), ("A", D0), ("B", D1), ("Z", U2)],
    "f4": [("A", U0), ("C", PROJ), ("B", U1)],
    "f5": [("D", PROJ), ("C", D0)],
    "m0": [("C", U0), ("A", D1), ("B", D2), ("D", D0), ("D", U0)],
    "m0g": [("finish", D0), ("finish", U0)],
    "m1": [("A", U1), ("C", D1), ("B", U2)],
    "m2": [("S0", SD0), ("S0", SU0), ("A", D2), ("C", U1), ("D", D1), ("D", U1)],
    "m2g": [("finish", D1), ("finish", U1)],
    "m3": [("A", U2), ("C", D2), ("S1", SD0), ("S1", SU0)],
    "m4": [("S0", SD1), ("S0", SU1), ("C", U2), ("S2", SD0), ("D", D2), ("D", U2)],
    "m4g": [("finish", D2), ("finish", U2)],
    "m5": [("S2", SU0), ("S1", SD1)],
    "m6": [("S0", SD2), ("S0", SU2), ("S3", SD0), ("S1", SU1), ("finish", PROJ)],
    "mid": [("S0", SP), ("S0", SV1), ("S3", SU0), ("S2", SD1), ("S2", SU1), ("S1", SD2), ("S4", SD0)],
    "b0h": [("S1", SV1), ("S1", SU2), ("S4", SU0)],
    "b0": [("S2", SV1), ("S3", SD1), ("S3", SU1), ("S1", SP), ("S5", SU0)],
    "b1h": [("S3", SV1), ("S2", SD2)],
    "b1": [("S0", SG0), ("S2", SU2), ("S4", SD1), ("S4", SU1), ("S4", SV1)],
    "b2h": [("S1", SG0), ("S2", SP), ("S5", SU1)],
    "b2": [("S3", SD2)],
    "b3h": [("S3", SU2), ("S2", SG0)],
    "b3": [("S0", SG1), ("S3", SP), ("S3", SG0), ("S4", SD2)],
    "b4h": [("S1", SG1), ("S4", SU2)],
    "b4": [("S4", SP), ("S4", SG0), ("S5", SU2)],
    "b5h": [("S2", SG1), ("S5", SP), ("S5", SG0)],
    "b5": [("S0", SG2), ("S3", SG1)],
    "r0": [("S1", SG2)],
    "r2": [("S4", SG1)],
    "r3": [("S0", SV2), ("S2", SG2), ("S5", SG1)],
    "end": [("S1", SV2), ("S3", SG2), ("S2", SV2), ("S3", SV2), ("S4", SG2), ("S4", SV2), ("S5", SG2)],
}


def layer_kernel(
    len_ref, tok_hbm, cot_ref, vec_in, wqkv_in, wproj_in, wup_in, wdown_in,
    out_hbm, gin_hbm, oqkv, oproj, oup, odown, vg_out,
    n1, n1t, proj, ot, att, lse, res, n2t, acc, gn2, gh,
    vec_ref, ub_ref, wqkv, wproj, wup, wdown, vbuf, xr_qkv, xr_proj, xr_up, gsend, grecv,
    vsum, up0, up1, up2, up3, down0, down1, down2, down3, proj0, proj1, proj2, proj3, qkv1, qkv2, qkv3,
    qkv0, stage_up, stage_proj, stage_qkv, land_up, land_proj, land_qkv, vbufs, send, recv, hsend, hrecv, sems,
):
    seq, width = cot_ref.shape
    half = width // 2
    pairs = proj.shape[0]
    own, rows = wqkv_in.shape[0], wdown_in.shape[0]
    groups, pieces = wqkv.shape[0], wup.shape[0]
    piece = rows // pieces
    sub = wup.shape[-1]
    place = Place(wqkv.shape[3])
    p_ = place
    n2, act, gin, tok_early, tok_late = n1, att, att, gh, n1
    vg_one, vg_two = vsum.at[0, 0], vsum.at[1, 0]

    def own_gradient(g):
        return up0.at[g, :, :, :, :, pl.ds(0, 3 * PAIR)]

    def other_gradient(g):
        return wup.at[g, 1 - place.c, :, :, :, :, pl.ds(0, 3 * PAIR)]


    padded = xr_proj.shape[0]

    def staged(first, lanes):
        return lambda i, c: n2t.at[pl.ds(pl.multiple_of((first + 2 * i + c) * padded, padded), padded), 0:lanes]

    xs_qkv, xs_up = staged(0, 3 * PAIR), staged(2 * groups, sub)
    xs_proj = functools.partial(staged(2 * (groups + pieces), half), 0)

    items = dict(enumerate(gather_items(
        place, wdown_in, wqkv, wproj, wup, wdown, vbuf, (xs_qkv, xs_proj, xs_up), (xr_qkv, xr_proj, xr_up),
        gsend, grecv,
    )))
    handovers = []

    def add(i, own_half, other_half, bufs, total):
        k = i - SV1
        items[i] = Scatter(p_, own_half, other_half, bufs, send.at[k], recv.at[k], total)

    def add_shared(i, own_half, other_half, bufs, stage, landing, write):
        k = i - SV1
        h = Handover(p_, stage, landing, write, hsend.at[k], hrecv.at[k])
        handovers.append(h)
        add(i, own_half, other_half, bufs, h.start)
        items[i].S5 = h.S5

    for k in range(pieces):

        def write_down(total, k=k):
            odown[k * piece : (k + 1) * piece, :] = total

        add(
            SD0 + 2 * k, wdown.at[k, :, :, :, p_.c], wdown.at[k, :, :, :, 1 - p_.c],
            (down0.at[k], down1.at[k], down2.at[k], down3.at[k]), write_down,
        )

        def write_up(c, v, k=k):
            back = regroup(pieces, piece)[:, k * PAIR : (k + 1) * PAIR]
            for i in range(sub // PAIR):
                lanes = pl.ds(pl.multiple_of((c * (sub // PAIR) + i) * pieces * PAIR, PAIR), pieces * PAIR)
                oup[:, lanes] += lax.dot_general(
                    v[:, i * PAIR : (i + 1) * PAIR], back, (((1,), (1,)), ((), ())),
                    precision=lax.Precision.HIGHEST, preferred_element_type=f32,
                )

        add_shared(
            SU0 + 2 * k, wup.at[k, p_.c], wup.at[k, 1 - p_.c], (up0.at[k], up1.at[k], up2.at[k], up3.at[k]),
            stage_up.at[k], land_up.at[k], write_up,
        )

    def write_proj(c, v):
        oproj[:, pl.ds(pl.multiple_of(c * half, PAIR), half)] = v

    add_shared(SP, wproj.at[p_.c], wproj.at[1 - p_.c], (proj0, proj1, proj2, proj3), stage_proj, land_proj, write_proj)
    for g in range(groups):

        def write_qkv(c, v, g=g):
            for t in range(3):
                oqkv[:, pl.ds(pl.multiple_of(t * width + (2 * g + c) * PAIR, PAIR), PAIR)] = v[
                    :, t * PAIR : (t + 1) * PAIR
                ]

        add_shared(
            SG0 + g, own_gradient(g), other_gradient(g),
            (qkv0.at[g], qkv1.at[g], qkv2.at[g], qkv3.at[g]), stage_qkv.at[g], land_qkv.at[g], write_qkv,
        )
    for i, v in ((SV1, 0), (SV2, 1)):
        items[i] = VectorSum(p_, vsum.at[v], vbufs.at[v], send.at[i - SV1], recv.at[i - SV1])
    finished = set()

    def tick(name):
        for step, i in PLAN.get(name, ()):
            getattr(items[i], step)()
            if step == "finish":
                finished.add(i)

    def ticks(index, names):
        for i, name in enumerate(names):
            if PLAN.get(name):

                @pl.when(index == i)
                def _(name=name):
                    tick(name)

    def w_qkv(p):
        return rows_of(wqkv[lax.div(p, 2), lax.rem(p, 2)])

    def w_up(k, u):
        return rows_of(wup[k, u])

    def w_down(k, u):
        return rows_of(wdown[k, u])

    def w_proj(i):
        return rows_of(wproj[i])

    def vec(i):
        return vec_ref[i : i + 1, :]

    rb = 256
    nb = seq // rb
    greet(place)
    tok_copy = pltpu.make_async_copy(tok_hbm, tok_early, sems.at[1])
    tok_copy.start()
    vbuf[p_.y, p_.z, p_.x, p_.c] = vec_in[...]
    for p in range(pairs):
        for t in range(3):
            lanes = slice(t * width + p * PAIR, t * width + (p + 1) * PAIR)
            n2t[p * padded : p * padded + own, t * PAIR : (t + 1) * PAIR] = wqkv_in[:, lanes]
    met(place)
    for i in (G0, G1, G2):
        items[i].X()
    items[VECI].Z()
    items[G0].Z()
    for i in range(2):
        row = (2 * (groups + pieces) + i) * padded
        n2t[row : row + own, 0:half] = wproj_in[:, i * half : (i + 1) * half]
    order = regroup(pieces, piece).astype(bf16)
    for i in range(2 * sub // PAIR):
        u, q = divmod(i, sub // PAIR)
        v = dg(wup_in[:, i * pieces * PAIR : (i + 1) * pieces * PAIR], order, 1, 0).astype(bf16)
        for k in range(pieces):
            row = (2 * (groups + k) + u) * padded
            n2t[row : row + own, q * PAIR : (q + 1) * PAIR] = v[:, k * PAIR : (k + 1) * PAIR]
    items[G1].Z()
    for i in (PROJ, U0, U1, U2):
        items[i].X()
    for k in range(pieces):
        wdown[k, p_.y, p_.z, p_.x, p_.c] = wdown_in[k * piece : (k + 1) * piece, :]
    oup[...] = jnp.zeros(oup.shape, f32)
    tok_copy.wait()

    def stats(r, sl):
        res[sl, :] = norm_parts(tok_early[sl, :].astype(f32))[0]

    blocks(nb, rb, stats)
    tick("stats")
    expand_table(vbuf, vec_ref, ub_ref, own, piece)

    def norm(r, sl):
        n1[sl, :] = (res[sl, :] * vec(AG) + vec(AS)).astype(bf16)

    blocks(nb, rb, norm)
    n1t[...] = n1[...].T
    tick("norm")

    bias_k = key_bias(len_ref[0], seq)
    q_bias = [vec(QB)[:, i * PAIR : (i + 1) * PAIR] for i in range(pairs)]
    v_bias = [vec(VB)[:, i * PAIR : (i + 1) * PAIR] for i in range(pairs)]

    @pl.loop(0, pairs)
    def _(p):
        qkv = dg(n1[...], w_qkv(p), 1, 0)
        proj[p, :, 0:PAIR] = (qkv[:, 0:PAIR] + pick(p, q_bias)).astype(bf16)
        proj[p, :, PAIR : 2 * PAIR] = qkv[:, PAIR : 2 * PAIR].astype(bf16)
        proj[p, :, 2 * PAIR :] = (qkv[:, 2 * PAIR :] + pick(p, v_bias)).astype(bf16)

        def write(hh, o, total):
            ot[p, HD * hh : HD * hh + HD, :] = o.astype(bf16)
            lse[pl.ds(2 * p + hh, 1), :] = total

        attend(
            proj[p, :, PAIR : 2 * PAIR], proj[p, :, 2 * PAIR :].T,
            proj[p, :, 0:PAIR] * jnp.asarray(HD**-0.5, bf16), bias_k, write,
        )
        ticks(p, [f"f{i}" for i in range(pairs)])

    for p in range(pairs):
        att[:, p * PAIR : (p + 1) * PAIR] = ot[p].T

    def branch(r, sl):
        a = att[sl, :]
        v = tok_early[sl, :].astype(f32) + vec(PB)
        v += jnp.concatenate([dg(a, w_proj(i), 1, 0) for i in range(2)], 1)
        res[sl, :] = v
        acc[sl, :] = v + vec(DB)
        gn2[sl, :] = jnp.zeros((rb, width), f32)
        n2[sl, :] = (norm_parts(v)[0] * vec(MG) + vec(MS)).astype(bf16)

    blocks(nb, rb, branch)
    n2t[...] = n2[...].T

    rm = 1024
    @pl.loop(0, 2 * pieces)
    def _(turn):
        k, u = lax.div(turn, 2), lax.rem(turn, 2)
        cols = pl.ds(pl.multiple_of(u * sub, PAIR), sub)
        total = pl.ds(4 + k, 1)
        ticks(turn, [f"m{i}" for i in range(2 * pieces)])
        vg_one[total, cols] = jnp.zeros((1, sub), f32)

        def stage_one(r, sl):
            a, g = up_step(n2[sl, :], cot_ref[sl, :], lambda: w_up(k, u), lambda: w_down(k, u), ub_ref[k, :, cols])
            act[sl, 0:sub] = a
            gh[sl, 0:sub] = g
            acc[sl, :] += dg(a, w_down(k, u), 1, 0)
            gn2[sl, :] += dg(g, w_up(k, u), 1, 1)
            vg_one[total, cols] += jnp.sum(g.astype(f32), 0, keepdims=True)

        blocks(seq // rm, rm, stage_one)
        ticks(turn, [f"m{i}g" for i in range(2 * pieces)])
        v = dg(act[:, 0:sub], cot_ref[...], 0, 0).astype(bf16)
        wdown[k, u] = v.reshape(wdown.shape[2:])
        wup[k, u] = dg(n2t[...], gh[:, 0:sub], 1, 0).astype(bf16).reshape(wup.shape[2:])

    tick(f"m{2 * pieces}")

    vg_one[0:4, :] = jnp.zeros((4, vg_one.shape[1]), f32)
    vg_one[7:8, :] = jnp.zeros((1, vg_one.shape[1]), f32)

    def back_two(r, sl):
        n2[sl, :] = acc[sl, :].astype(bf16)
        g = gn2[sl, :]
        n, inv = norm_parts(res[sl, :])
        cot = cot_ref[sl, :].astype(f32)
        mid = cot + norm_back(n, inv, g * vec(MG))
        acc[sl, :] = mid
        low = mid.astype(bf16)
        act[sl, :] = low
        vg_one[0:1, 0:width] += jnp.sum(g * n, 0, keepdims=True)
        vg_one[1:2, 0:width] += jnp.sum(g, 0, keepdims=True)
        vg_one[2:3, 0:width] += jnp.sum(low.astype(f32), 0, keepdims=True)
        vg_one[3:4, 0:width] += jnp.sum(cot, 0, keepdims=True)
        back = dg(low[:, :half], w_proj(0), 1, 1) + dg(low[:, half:], w_proj(1), 1, 1)
        gh[sl, :] = back.astype(bf16)

    blocks(nb, rb, back_two)
    out_copy = pltpu.make_async_copy(n2, out_hbm, sems.at[0])
    out_copy.start()
    tok_again = pltpu.make_async_copy(tok_hbm, tok_late, sems.at[2])
    for i in range(2):
        v = dg(rows_of(ot[...]), act[:, i * half : (i + 1) * half], 1, 0).astype(bf16)
        wproj[i] = v.reshape(wproj.shape[1:])
    vg_two[...] = jnp.zeros(vg_two.shape, f32)
    tick("mid")

    def weight_gradient(p, dst):
        g = proj[p]
        cols = pl.ds(pl.multiple_of(p * PAIR, PAIR), PAIR)
        sums = jnp.sum(g.astype(f32), 0, keepdims=True)
        vg_two[2:3, cols] = sums[:, 0:PAIR]
        vg_two[3:4, cols] = sums[:, 2 * PAIR :]
        dst[...] = dg(n1t[...], g, 1, 0).astype(bf16).reshape(dst.shape)

    @pl.loop(0, pairs)
    def _(p):
        lanes = pl.ds(pl.multiple_of(p * PAIR, PAIR), PAIR)
        dqt, dk, dv = attend_back(
            lambda sl: proj[p, sl, 0:PAIR],
            proj[p, :, PAIR : 2 * PAIR],
            proj[p, :, 2 * PAIR :],
            lambda sl: gh[sl, lanes],
            lambda rows, sl: ot[p, rows, sl],
            lambda hh, sl: lse[pl.ds(2 * p + hh, 1), sl],
            bias_k,
            512,
            lambda: ticks(p, [f"b{i}h" for i in range(pairs)]),
        )
        proj[p, :, 0:PAIR] = dqt.T.astype(bf16)
        proj[p, :, PAIR : 2 * PAIR] = dk.astype(bf16)
        proj[p, :, 2 * PAIR :] = dv.astype(bf16)

        @pl.when(p == 1)
        def _():
            out_copy.wait()
            tok_again.start()

        @pl.when(lax.rem(p, 2) == 1)
        def _():
            g = lax.div(p, 2)
            weight_gradient(2 * g + p_.c, own_gradient(g))
            weight_gradient(2 * g + 1 - p_.c, other_gradient(g))

        ticks(p, [f"b{i}" for i in range(pairs)])

    tok_again.wait()

    def back_one(r, sl):
        g = dg(proj[0, sl, :], rows_of(wqkv[0, 0]), 1, 1)
        for p in range(1, pairs):
            g += dg(proj[p, sl, :], rows_of(wqkv[p // 2, p % 2]), 1, 1)
        n, inv = norm_parts(tok_late[sl, :].astype(f32))
        gin[sl, :] = (acc[sl, :] + norm_back(n, inv, g * vec(AG))).astype(bf16)
        vg_two[0:1, 0:width] += jnp.sum(g * n, 0, keepdims=True)
        vg_two[1:2, 0:width] += jnp.sum(g, 0, keepdims=True)
        ticks(r, [f"r{i}" for i in range(nb)])

    blocks(nb, rb, back_one)
    gin_copy = pltpu.make_async_copy(gin, gin_hbm, sems.at[1])
    gin_copy.start()
    index = ((p_.y * p_.nz + p_.z) * 2 + p_.x) * 2 + p_.c
    one = vsum[0, 4]
    vg_out[0:8, :] = slice_lanes(one, index * own, own)
    vg_out[4:5, :] = sum(slice_lanes(one, index * piece, piece, k * piece)[4 + k : 5 + k] for k in range(pieces))
    tick("end")
    vg_out[8:16, :] = slice_lanes(vsum[1, 4], index * own, own)
    for i, item in items.items():
        if i not in finished:
            item.finish()
    for h in handovers:
        h.end()
    gin_copy.wait()


def forward_kernel(
    len_ref, tok_ref, cot_ref, vec_ref, wqkv, wproj, wup, wdown,
    out_hbm, proj_hbm, ot_hbm, lse_hbm, do_hbm, gmid_hbm, n1t_hbm, gup_hbm, gdown_hbm, gproj_hbm, vg_ref,
    n1, n1t, proj, ot, att, lse, res, n2, n2t, acc, gn2, act, gh, gstage, sems,
):
    seq, width = tok_ref.shape
    half = width // 2
    chunks, pairs = gup_hbm.shape[0], proj.shape[0]
    copies = []

    def send_out(src, dst, sem):
        cp = pltpu.make_async_copy(src, dst, sem)
        cp.start()
        copies.append(cp)

    def vec(i):
        return vec_ref[i : i + 1, :]

    rb = 256
    nb = seq // rb

    def norm(r, sl):
        n1[sl, :] = (norm_parts(tok_ref[sl, :].astype(f32))[0] * vec(AG) + vec(AS)).astype(bf16)

    blocks(nb, rb, norm)
    n1t[...] = n1[...].T
    send_out(n1t, n1t_hbm, sems.at[0])
    bias_k = key_bias(len_ref[0], seq)
    q_bias = [vec(QB)[:, i * PAIR : (i + 1) * PAIR] for i in range(pairs)]
    v_bias = [vec(VB)[:, i * PAIR : (i + 1) * PAIR] for i in range(pairs)]

    @pl.loop(0, pairs)
    def _(p):
        qkv = dg(n1[...], wqkv[p], 1, 0)
        proj[p, :, 0:PAIR] = (qkv[:, 0:PAIR] + pick(p, q_bias)).astype(bf16)
        proj[p, :, PAIR : 2 * PAIR] = qkv[:, PAIR : 2 * PAIR].astype(bf16)
        proj[p, :, 2 * PAIR :] = (qkv[:, 2 * PAIR :] + pick(p, v_bias)).astype(bf16)

        def write(hh, o, total):
            ot[p, HD * hh : HD * hh + HD, :] = o.astype(bf16)
            lse[pl.ds(2 * p + hh, 1), :] = total

        attend(
            proj[p, :, PAIR : 2 * PAIR], proj[p, :, 2 * PAIR :].T,
            proj[p, :, 0:PAIR] * jnp.asarray(HD**-0.5, bf16), bias_k, write,
        )

    for p in range(pairs):
        att[:, p * PAIR : (p + 1) * PAIR] = ot[p].T
    send_out(proj, proj_hbm, sems.at[1])
    send_out(ot, ot_hbm, sems.at[2])
    send_out(lse, lse_hbm, sems.at[3])

    def branch(r, sl):
        a = att[sl, :]
        v = tok_ref[sl, :].astype(f32) + vec(PB)
        v += jnp.concatenate([dg(a, wproj[i], 1, 0) for i in range(2)], 1)
        res[sl, :] = v
        acc[sl, :] = v + vec(DB)
        gn2[sl, :] = jnp.zeros((rb, width), f32)
        n2[sl, :] = (norm_parts(v)[0] * vec(MG) + vec(MS)).astype(bf16)

    blocks(nb, rb, branch)
    n2t[...] = n2[...].T
    rm = 512
    staged = []
    for j in range(chunks):
        vg_ref[4 + j : 5 + j, :] = jnp.zeros((1, width), f32)

        def stage_one(r, sl, j=j):
            a, g = up_step(n2[sl, :], cot_ref[sl, :], lambda: wup[j], lambda: wdown[j], vec(UB + j))
            act[sl, :] = a
            gh[sl, :] = g
            acc[sl, :] += dg(a, wdown[j], 1, 0)
            gn2[sl, :] += dg(g, wup[j], 1, 1)
            vg_ref[4 + j : 5 + j, :] += jnp.sum(g.astype(f32), 0, keepdims=True)

        blocks(seq // rm, rm, stage_one)
        for cp in staged:
            cp.wait()
        gstage[0] = dg(act[...], cot_ref[...], 0, 0).astype(bf16)
        gstage[1] = dg(n2t[...], gh[...], 1, 0).astype(bf16)
        staged = [
            pltpu.make_async_copy(gstage.at[0], gdown_hbm.at[j], sems.at[4]),
            pltpu.make_async_copy(gstage.at[1], gup_hbm.at[j], sems.at[5]),
        ]
        for cp in staged:
            cp.start()

    vg_ref[0:4, :] = jnp.zeros((4, width), f32)

    def back_two(r, sl):
        n2[sl, :] = acc[sl, :].astype(bf16)
        g = gn2[sl, :]
        n, inv = norm_parts(res[sl, :])
        cot = cot_ref[sl, :].astype(f32)
        mid = cot + norm_back(n, inv, g * vec(MG))
        acc[sl, :] = mid
        low = mid.astype(bf16)
        act[sl, :] = low
        vg_ref[0:1, :] += jnp.sum(g * n, 0, keepdims=True)
        vg_ref[1:2, :] += jnp.sum(g, 0, keepdims=True)
        vg_ref[2:3, :] += jnp.sum(low.astype(f32), 0, keepdims=True)
        vg_ref[3:4, :] += jnp.sum(cot, 0, keepdims=True)
        gh[sl, :] = (dg(low[:, :half], wproj[0], 1, 1) + dg(low[:, half:], wproj[1], 1, 1)).astype(bf16)

    blocks(nb, rb, back_two)
    send_out(n2, out_hbm, sems.at[6])
    send_out(acc, gmid_hbm, sems.at[7])
    for p in range(pairs):
        send_out(gh.at[:, p * PAIR : (p + 1) * PAIR], do_hbm.at[p], sems.at[8 + p])
    for cp in staged:
        cp.wait()
    for i in range(2):
        gstage[i, :, :half] = dg(rows_of(ot[...]), act[:, i * half : (i + 1) * half], 1, 0).astype(bf16)
        send_out(gstage.at[i, :, pl.ds(0, half)], gproj_hbm.at[i], sems.at[4 + i])
    for cp in copies:
        cp.wait()


def backward_kernel(
    len_ref, tok_ref, vec_ref, proj_hbm, ot_hbm, lse_hbm, do_hbm, gmid_hbm, n1t_hbm, wqkv_ref,
    gin_hbm, gqkv_hbm, vg_ref,
    proj, ot, lse, do, gmid, n1t, gqkv, gin, sems,
):
    seq, width = tok_ref.shape
    pairs = proj.shape[0]

    def start(src, dst, sem):
        cp = pltpu.make_async_copy(src, dst, sem)
        cp.start()
        return cp

    loads = [
        start(proj_hbm, proj, sems.at[0]),
        start(do_hbm, do, sems.at[1]),
        start(ot_hbm, ot, sems.at[2]),
        start(lse_hbm, lse, sems.at[3]),
        start(n1t_hbm, n1t, sems.at[4]),
        start(gmid_hbm, gmid, sems.at[5]),
    ]
    for cp in loads:
        cp.wait()
    vg_ref[...] = jnp.zeros(vg_ref.shape, f32)
    bias_k = key_bias(len_ref[0], seq)

    @pl.loop(0, pairs)
    def _(p):
        dqt, dk, dv = attend_back(
            lambda sl: proj[p, sl, 0:PAIR],
            proj[p, :, PAIR : 2 * PAIR],
            proj[p, :, 2 * PAIR :],
            lambda sl: do[p, sl, :],
            lambda rows, sl: ot[p, rows, sl],
            lambda hh, sl: lse[pl.ds(2 * p + hh, 1), sl],
            bias_k,
            512,
            lambda: None,
        )
        proj[p, :, 0:PAIR] = dqt.T.astype(bf16)
        proj[p, :, PAIR : 2 * PAIR] = dk.astype(bf16)
        proj[p, :, 2 * PAIR :] = dv.astype(bf16)

    outs = []
    for p in range(pairs):
        cols = slice(p * PAIR, (p + 1) * PAIR)
        g = proj[p]
        sums = jnp.sum(g.astype(f32), 0, keepdims=True)
        vg_ref[2:3, cols] = sums[:, 0:PAIR]
        vg_ref[3:4, cols] = sums[:, 2 * PAIR :]
        gqkv[p] = dg(n1t[...], g, 1, 0).astype(bf16)
        outs.append(start(gqkv.at[p], gqkv_hbm.at[p], sems.at[6 + p]))

    def back_one(r, sl):
        g = dg(proj[0, sl, :], wqkv_ref[0], 1, 1)
        for p in range(1, pairs):
            g += dg(proj[p, sl, :], wqkv_ref[p], 1, 1)
        n, inv = norm_parts(tok_ref[sl, :].astype(f32))
        gin[sl, :] = (gmid[sl, :] + norm_back(n, inv, g * vec_ref[AG : AG + 1, :])).astype(bf16)
        vg_ref[0:1, :] += jnp.sum(g * n, 0, keepdims=True)
        vg_ref[1:2, :] += jnp.sum(g, 0, keepdims=True)

    blocks(seq // 256, 256, back_one)
    outs.append(start(gin, gin_hbm, sems.at[0]))
    for cp in outs:
        cp.wait()


def specs(kinds):
    table = {"s": pltpu.SMEM, "v": pltpu.VMEM, "h": pl.ANY}
    return [pl.BlockSpec(memory_space=table[k]) for k in kinds]


def sds(shape, dtype):
    return jax.ShapeDtypeStruct(shape, dtype)


def run_layer(nz, lengths, tokens, cotangent, vecs, wqkv, wproj, wup, wdown):
    seq, width = tokens.shape
    half = width // 2
    pairs = width // PAIR
    groups = pairs // 2
    own, rows = wup.shape[0], wdown.shape[0]
    piece = 32
    pieces = rows // piece
    sub = wup.shape[1] // pieces // 2
    chip = (2, nz, 2)
    padded = -(-own // 16) * 16

    def vmem(*dims, dtype=bf16):
        return pltpu.VMEM(dims, dtype)

    def landing(lead, block):
        return [pltpu.VMEM(lead + dims + block, bf16) for dims in (chip, (2, nz), (nz,), (nz - 1,))]

    qkv_landing = landing((groups,), (2 * own, 3 * PAIR))
    handover = [
        vmem(pieces, own, sub, dtype=f32),
        vmem(own, half, dtype=f32),
        vmem(groups, own, 3 * PAIR, dtype=f32),
    ]
    scratch = (
        [
            vmem(seq, width),
            vmem(width, seq),
            vmem(pairs, seq, 3 * PAIR),
            vmem(pairs, PAIR, seq),
            vmem(seq, width),
            vmem(2 * pairs, seq, dtype=f32),
            vmem(seq, width, dtype=f32),
            vmem(width, seq),
            vmem(seq, width, dtype=f32),
            vmem(seq, width, dtype=f32),
            vmem(seq, width),
            vmem(16, width, dtype=f32),
            vmem(pieces, 1, 2 * sub, dtype=f32),
            vmem(groups, 2, *chip, 2 * own, 3 * PAIR),
            vmem(2, *chip, 2 * own, half),
            vmem(pieces, 2, *chip, 2 * own, sub),
            vmem(pieces, *chip, 2, piece, width),
            vmem(*chip, 2, 16, PAIR),
            vmem(groups, padded, 3 * PAIR),
            vmem(padded, half),
            vmem(pieces, padded, sub),
            pltpu.SemaphoreType.DMA((5 + 2 * pieces, 8 + nz - 1)),
            pltpu.SemaphoreType.DMA((5 + 2 * pieces, 8 + nz - 1)),
            vmem(2, 5, 8, 2 * sub, dtype=f32),
        ]
        + landing((pieces,), (2 * own, sub))
        + landing((pieces,), (piece, width))
        + landing((), (2 * own, half))
        + qkv_landing[1:]
        + qkv_landing[:1]
        + handover
        + handover
        + [
            vmem(2, 2 + nz, 8, 2 * sub, dtype=f32),
            pltpu.SemaphoreType.DMA((12, 3 + nz)),
            pltpu.SemaphoreType.DMA((12, 3 + nz)),
            pltpu.SemaphoreType.DMA((12,)),
            pltpu.SemaphoreType.DMA((12,)),
            pltpu.SemaphoreType.DMA((3,)),
        ]
    )
    return pl.pallas_call(
        layer_kernel,
        in_specs=specs("shvvvvvv"),
        out_specs=specs("hhvvvvv"),
        out_shape=[
            sds((seq, width), bf16),
            sds((seq, width), bf16),
            sds((own, 3 * width), f32),
            sds((own, width), f32),
            sds((own, wup.shape[1]), f32),
            sds((rows, width), f32),
            sds((16, PAIR), f32),
        ],
        scratch_shapes=scratch,
        compiler_params=pltpu.CompilerParams(vmem_limit_bytes=VMEM_LIMIT, collective_id=0, has_side_effects=True),
        name="layer",
    )(lengths, tokens, cotangent, vecs, wqkv, wproj, wup, wdown)


def run_forward(lengths, tokens, cotangent, vecs, wqkv, wproj, wup, wdown):
    seq, width = tokens.shape
    pairs = width // PAIR
    chunks = wup.shape[0]
    return pl.pallas_call(
        forward_kernel,
        in_specs=specs("svvvvvvv"),
        out_specs=specs("hhhhhhhhhhv"),
        out_shape=[
            sds((seq, width), bf16),
            sds((pairs, seq, 3 * PAIR), bf16),
            sds((pairs, PAIR, seq), bf16),
            sds((2 * pairs, seq), f32),
            sds((pairs, seq, PAIR), bf16),
            sds((seq, width), f32),
            sds((width, seq), bf16),
            sds((chunks, width, width), bf16),
            sds((chunks, width, width), bf16),
            sds((2, width, width // 2), bf16),
            sds((8, width), f32),
        ],
        scratch_shapes=[
            pltpu.VMEM((seq, width), bf16),
            pltpu.VMEM((width, seq), bf16),
            pltpu.VMEM((pairs, seq, 3 * PAIR), bf16),
            pltpu.VMEM((pairs, PAIR, seq), bf16),
            pltpu.VMEM((seq, width), bf16),
            pltpu.VMEM((2 * pairs, seq), f32),
            pltpu.VMEM((seq, width), f32),
            pltpu.VMEM((seq, width), bf16),
            pltpu.VMEM((width, seq), bf16),
            pltpu.VMEM((seq, width), f32),
            pltpu.VMEM((seq, width), f32),
            pltpu.VMEM((seq, width), bf16),
            pltpu.VMEM((seq, width), bf16),
            pltpu.VMEM((2, width, width), bf16),
            pltpu.SemaphoreType.DMA((8 + pairs,)),
        ],
        compiler_params=pltpu.CompilerParams(vmem_limit_bytes=VMEM_LIMIT),
        name="layer_forward",
    )(lengths, tokens, cotangent, vecs, wqkv, wproj, wup, wdown)


def run_backward(lengths, tokens, vecs, proj, ot, lse, do, gmid, n1t, wqkv):
    seq, width = tokens.shape
    pairs = width // PAIR
    return pl.pallas_call(
        backward_kernel,
        in_specs=specs("svvhhhhhhv"),
        out_specs=specs("hhv"),
        out_shape=[
            sds((seq, width), bf16),
            sds((pairs, width, 3 * PAIR), bf16),
            sds((8, width), f32),
        ],
        scratch_shapes=[
            pltpu.VMEM((pairs, seq, 3 * PAIR), bf16),
            pltpu.VMEM((pairs, PAIR, seq), bf16),
            pltpu.VMEM((2 * pairs, seq), f32),
            pltpu.VMEM((pairs, seq, PAIR), bf16),
            pltpu.VMEM((seq, width), f32),
            pltpu.VMEM((width, seq), bf16),
            pltpu.VMEM((pairs, width, 3 * PAIR), bf16),
            pltpu.VMEM((seq, width), bf16),
            pltpu.SemaphoreType.DMA((6 + pairs,)),
        ],
        compiler_params=pltpu.CompilerParams(vmem_limit_bytes=VMEM_LIMIT),
        name="attention_backward",
    )(lengths, tokens, vecs, proj, ot, lse, do, gmid, n1t, wqkv)


def gathered(item, axis=0):
    return lax.all_gather(item, AXES, axis=axis, tiled=True)


def scattered(item, axis=0):
    return lax.psum_scatter(item, AXES, scatter_dimension=axis, tiled=True)


def per_device(
    nz, tokens, cotangent, lengths, attn_gain, attn_shift, qkv_weight, qv_bias, proj_weight, proj_bias,
    mlp_gain, mlp_shift, up_weight, up_bias, down_weight, down_bias,
):
    seq, width = tokens.shape
    pairs = width // PAIR
    own = attn_gain.shape[0]
    chunks = up_weight.shape[1] // width
    small = jnp.stack([attn_gain, attn_shift, qv_bias[0], qv_bias[1], proj_bias, mlp_gain, mlp_shift, down_bias])
    if nz:
        vecs = jnp.concatenate(
            [
                jnp.pad(small, ((0, 0), (0, PAIR - own))),
                jnp.pad(up_bias[None], ((0, 7), (0, PAIR - up_bias.shape[0]))),
            ]
        )
        block_out, input_grad, g_qkv, g_proj, g_up, g_down, v = run_layer(
            nz, lengths, tokens, cotangent, vecs, qkv_weight, proj_weight, up_weight, down_weight
        )
        w = v[:, :own]
        return (
            block_out, input_grad, w[8], w[9], g_qkv, w[10:12], g_proj, w[2], w[0], w[1],
            g_up, v[4, : up_bias.shape[0]], g_down, w[3],
        )
    allvec = gathered(jnp.concatenate([small.reshape(-1), up_bias])[None])
    many = allvec.shape[0]
    table = allvec[:, : 8 * own].reshape(many, 8, own).transpose(1, 0, 2).reshape(8, width)
    vecs = jnp.concatenate([table, allvec[:, 8 * own :].reshape(chunks, width)], 0).astype(f32)
    wqkv = gathered(qkv_weight).reshape(width, 3, pairs, PAIR).transpose(2, 0, 1, 3).reshape(pairs, width, 3 * PAIR)
    wproj = gathered(proj_weight).reshape(width, 2, width // 2).transpose(1, 0, 2)
    wup = gathered(up_weight).reshape(width, chunks, width).transpose(1, 0, 2)
    wdown = gathered(down_weight).reshape(chunks, width, width)
    block_out, proj, ot, lse, do, gmid, n1t, gup, gdown, gproj, vg_one = run_forward(
        lengths, tokens, cotangent, vecs, wqkv, wproj, wup, wdown
    )
    input_grad, gqkv, vg_two = run_backward(lengths, tokens, vecs, proj, ot, lse, do, gmid, n1t, wqkv)
    g_down = scattered(gdown.astype(f32).reshape(chunks * width, width))
    g_up = scattered(gup.astype(f32).transpose(1, 0, 2).reshape(width, chunks * width))
    g_proj = scattered(gproj.astype(f32).transpose(1, 0, 2).reshape(width, width))
    g_qkv = scattered(
        gqkv.astype(f32).reshape(pairs, width, 3, PAIR).transpose(1, 2, 0, 3).reshape(width, 3 * width)
    )
    rest = jnp.concatenate([vg_two[:4], vg_one[:4]], 0).reshape(8, many, own).transpose(1, 0, 2).reshape(many, -1)
    rest = jnp.concatenate([rest, vg_one[4:].reshape(many, -1)], 1)
    mine = scattered(rest)[0]
    v = mine[: 8 * own].reshape(8, own)
    return (
        block_out, input_grad, v[0], v[1], g_qkv, v[2:4], g_proj, v[6], v[4], v[5],
        g_up, mine[8 * own :], g_down, v[7],
    )


def chips_along_z(mesh):
    dp, shard = mesh.shape["dp"], mesh.shape["shard"]
    return shard // 4 if dp == 2 and shard == 16 else 0


def solution(mesh):
    one, two, mid = P(AXES), P(AXES, None), P(None, AXES)
    return jax.shard_map(
        functools.partial(per_device, chips_along_z(mesh)),
        mesh=mesh,
        in_specs=(two, two, one, one, one, two, mid, two, one, one, one, two, one, two, one),
        out_specs=(two, two, one, one, two, mid, two, one, one, one, two, one, two, one),
        check_vma=False,
    )
```

```python
import functools

import jax
import jax.numpy as jnp
from jax import lax
from jax.experimental import pallas as pl
from jax.experimental.pallas import tpu as pltpu
from jax.sharding import PartitionSpec as P

f32 = jnp.float32
bf16 = jnp.bfloat16
HD = 64
PAIR = 2 * HD
EPS = 1e-06
MASKED = -1e30
AXES = ("dp", "shard")
VMEM_LIMIT = 65280 * 2**10

AG, AS, QB, VB, PB, MG, MS, DB, UB = range(9)


def dg(a, b, ca, cb):
    return lax.dot_general(a, b, (((ca,), (cb,)), ((), ())), preferred_element_type=f32)


def rows_of(v):
    return v.reshape(-1, v.shape[-1])


def norm_parts(v):
    center = v - jnp.mean(v, -1, keepdims=True)
    inv = lax.rsqrt(jnp.mean(center * center, -1, keepdims=True) + EPS)
    return center * inv, inv


def norm_back(n, inv, z):
    return inv * (z - jnp.mean(z, -1, keepdims=True) - n * jnp.mean(z * n, -1, keepdims=True))


def key_bias(length, seq):
    return jnp.where(lax.broadcasted_iota(jnp.int32, (seq, 1), 0) < length, 0.0, MASKED).astype(f32)


def head_only(v, hh):
    lane = lax.broadcasted_iota(jnp.int32, (1, PAIR), 1)
    return jnp.where(lane // HD == hh, v, jnp.zeros((), v.dtype))


class Place:
    def __init__(self, nz):
        shard = lax.axis_index("shard")
        self.nz = nz
        self.y = lax.axis_index("dp")
        self.c = lax.rem(shard, 2)
        self.x = lax.rem(lax.div(shard, 2), 2)
        self.z = lax.div(shard, 4)
        fy, fx = 1 - 2 * self.y, 1 - 2 * self.x
        self.ay, self.ax = self.y + (1 - self.c) * fy, self.x + self.c * fx
        self.by, self.bx = self.y + self.c * fy, self.x + (1 - self.c) * fx

    def device(self, y, z, x, c):
        return (y, (z * 2 + x) * 2 + c)

    def peer(self):
        return self.device(self.y, self.z, self.x, 1 - self.c)

    def along_z(self, k):
        return self.device(self.y, lax.rem(self.z + k, self.nz), self.x, self.c)

    def a(self):
        return self.device(self.ay, self.z, self.ax, self.c)

    def b(self):
        return self.device(self.by, self.z, self.bx, self.c)

    def partners(self):
        return [self.peer(), self.a(), self.b()] + [self.along_z(k) for k in range(1, self.nz)]


def greet(place):
    for d in place.partners():
        pl.semaphore_signal(
            pltpu.get_barrier_semaphore(), inc=1, device_id=d, device_id_type=pl.DeviceIdType.MESH
        )


def met(place):
    pl.semaphore_wait(pltpu.get_barrier_semaphore(), len(place.partners()))


def remote(src, dst, send, recv, device):
    return pltpu.make_async_remote_copy(
        src_ref=src, dst_ref=dst, send_sem=send, recv_sem=recv, device_id=device,
        device_id_type=pl.DeviceIdType.MESH,
    )


class Gather:
    def __init__(self, place, block, column, swap, send, recv):
        self.p, self.block, self.column, self.swap = place, block, column, swap
        self.send, self.recv = send, recv
        self.started = []

    def move(self, slot, src, dst, device):
        return remote(src, dst, self.send.at[slot], self.recv.at[slot], device)

    def go(self, copy):
        copy.start()
        self.started.append(copy)

    def exchange(self):
        src, dst, _ = self.swap
        return self.move(0, src, dst, self.p.peer())

    def X(self):
        self.go(self.exchange())

    def zs(self):
        p = self.p
        own = self.block(p.y, p.z, p.x, p.c)
        return [self.move(k, own, own, p.along_z(k)) for k in range(1, p.nz)]

    def over(self, slot, y, x, device):
        v = self.column(y, x, self.p.c)
        return self.move(slot, v, v, device)

    def to_b(self):
        return self.over(4, self.p.y, self.p.x, self.p.b())

    def to_a(self, second):
        p = self.p
        y, x = (p.by, p.bx) if second else (p.y, p.x)
        return self.over(5 + second, y, x, p.a())

    def across(self, i):
        p = self.p
        y, x = [(p.y, p.x), (p.by, p.bx), (p.ay, p.ax), (1 - p.y, 1 - p.x)][i]
        return self.over(7 + i, y, x, p.peer())

    def Z(self):
        if self.swap is not None:
            self.exchange().wait()
            self.swap[2]()
        for cp in self.zs():
            self.go(cp)

    def B(self):
        for cp in self.zs():
            cp.wait_recv()
        self.go(self.to_b())
        self.go(self.to_a(0))
        self.go(self.across(0))

    def A(self):
        self.to_b().wait_recv()
        self.go(self.to_a(1))
        self.go(self.across(1))

    def C(self):
        self.to_a(0).wait_recv()
        self.go(self.across(2))
        self.to_a(1).wait_recv()
        self.go(self.across(3))

    def D(self):
        for i in range(4):
            self.across(i).wait_recv()

    def finish(self):
        for cp in self.zs() + [self.to_b(), self.to_a(0), self.to_a(1)] + [self.across(i) for i in range(4)]:
            cp.wait_send()


class Scatter:
    def __init__(self, place, own, other, bufs, send, recv, total):
        self.p, self.own, self.other = place, own, other
        self.r0, self.r1, self.r2, self.r3 = bufs
        self.send, self.recv, self.total = send, recv, total

    def move(self, slot, src, dst, device):
        return remote(src, dst, self.send.at[slot], self.recv.at[slot], device)

    def swap(self):
        return self.move(0, self.other, self.r0, self.p.peer())

    def to_a(self, i):
        p = self.p
        src = self.own.at[p.ay, :, p.ax] if i == 0 else self.own.at[1 - p.y, :, 1 - p.x]
        return self.move(1 + i, src, self.r1.at[i], p.a())

    def to_b(self):
        p = self.p
        return self.move(3, self.own.at[p.by, :, p.bx], self.r2, p.b())

    def to_z(self, k):
        p = self.p
        return self.move(3 + k, self.own.at[p.y, lax.rem(p.z + k, p.nz), p.x], self.r3.at[k - 1], p.along_z(k))

    def add(self, y, x, other):
        self.own[y, :, x] = self.own[y, :, x] + other

    def S0(self):
        self.swap().start()

    def S1(self):
        p = self.p
        self.swap().wait()
        for i, (y, x) in enumerate([(p.ay, p.ax), (1 - p.y, 1 - p.x), (p.by, p.bx), (p.y, p.x)]):
            self.add(y, x, self.r0[y, :, x])
            if i < 2:
                self.to_a(i).start()

    def S2(self):
        p = self.p
        self.to_a(1).wait_recv()
        self.add(p.by, p.bx, self.r1[1])
        self.to_b().start()
        self.to_a(0).wait_recv()
        self.add(p.y, p.x, self.r1[0])

    def S3(self):
        p = self.p
        self.to_b().wait_recv()
        self.add(p.y, p.x, self.r2[...])
        for k in range(1, p.nz):
            self.to_z(k).start()

    def S4(self):
        p = self.p
        total = self.own[p.y, p.z, p.x].astype(f32)
        for k in range(1, p.nz):
            self.to_z(k).wait_recv()
            total += self.r3[k - 1].astype(f32)
        self.total(total)

    def finish(self):
        for cp in [self.to_a(0), self.to_a(1), self.to_b()] + [
            self.to_z(k) for k in range(1, self.p.nz)
        ]:
            cp.wait_send()


class Handover:
    def __init__(self, place, stage, landing, write, send, recv):
        self.p, self.stage, self.landing, self.write = place, stage, landing, write
        self.copy = remote(stage, landing, send, recv, place.peer())

    def start(self, total):
        own = total.shape[0] // 2
        top, bottom = total[:own], total[own:]
        self.stage[...] = jnp.where(self.p.c == 0, bottom, top)
        self.copy.start()
        self.write(self.p.c, jnp.where(self.p.c == 0, top, bottom))

    def S5(self):
        self.copy.wait_recv()
        self.write(1 - self.p.c, self.landing[...])

    def end(self):
        self.copy.wait_send()


class VectorSum:
    def __init__(self, place, value, bufs, send, recv):
        self.p, self.value, self.bufs, self.send, self.recv = place, value, bufs, send, recv

    def move(self, slot):
        p = self.p
        device = [p.peer(), p.a(), p.b()][slot] if slot < 3 else p.along_z(slot - 2)
        return remote(
            self.value.at[min(slot, 3)], self.bufs.at[slot], self.send.at[slot], self.recv.at[slot], device
        )

    def S0(self):
        self.move(0).start()

    def step(self, slot):
        self.move(slot - 1).wait_recv()
        self.value[slot] = self.value[slot - 1] + self.bufs[slot - 1]
        for k in range(self.p.nz - 1 if slot == 3 else 1):
            self.move(slot + k).start()

    def S1(self):
        self.step(1)

    def S2(self):
        self.step(2)

    def S3(self):
        self.step(3)

    def S4(self):
        total = self.value[3]
        for k in range(self.p.nz - 1):
            self.move(3 + k).wait_recv()
            total += self.bufs[3 + k]
        self.value[4] = total

    def finish(self):
        for slot in range(2 + self.p.nz):
            self.move(slot).wait_send()


def expand_table(vbuf, vec, ub, own, piece):
    many = vbuf.shape[0] * vbuf.shape[1] * vbuf.shape[2] * vbuf.shape[3]
    flat = vbuf[...].reshape(many * 16, PAIR)

    def spread(n, each, first=0):
        lane = lax.broadcasted_iota(jnp.int32, (1, n), 1)
        row = lax.broadcasted_iota(jnp.int32, (PAIR, n), 0) - first
        return (lax.rem(lane, each) == row).astype(f32).astype(bf16)

    def mine(full, each):
        shape = (many,) + (1,) * (full.ndim - 2) + full.shape[-1:]
        where = lax.broadcasted_iota(jnp.int32, shape, len(shape) - 1) - each * lax.broadcasted_iota(
            jnp.int32, shape, 0
        )
        return jnp.where((where >= 0) & (where < each), full, 0.0)

    full = dg(flat, spread(vec.shape[1], own), 1, 0).reshape(many, 16, vec.shape[1])
    vec[...] = jnp.sum(mine(full, own), 0)
    pick = (
        lax.broadcasted_iota(jnp.int32, (many, many * 16), 1)
        == 16 * lax.broadcasted_iota(jnp.int32, (many, many * 16), 0) + 8
    )
    row = dg(pick.astype(f32).astype(bf16), flat, 1, 0).astype(bf16)
    for i in range(ub.shape[0]):
        full = dg(row, spread(ub.shape[2], piece, i * piece), 1, 0)
        ub[i] = jnp.sum(mine(full, piece), 0, keepdims=True)


def regroup(pieces, piece):
    n = pieces * PAIR
    src = lax.broadcasted_iota(jnp.int32, (n, n), 0)
    dst = lax.broadcasted_iota(jnp.int32, (1, n), 1)
    inner = lax.rem(dst, PAIR)
    want = lax.div(inner, piece) * (pieces * piece) + lax.div(dst, PAIR) * piece + lax.rem(inner, piece)
    return (src == want).astype(f32)


def gather_items(place, own_down, wqkv, wproj, wup, wdown, vbuf, xs, xr, send, recv):
    p = place
    (xs_qkv, xs_proj, xs_up), (xr_qkv, xr_proj, xr_up) = xs, xr
    own = wqkv.shape[-2] // 2

    def joined(mine, theirs, write):
        def go():
            m, t = mine()[:own].astype(f32), theirs()[:own].astype(f32)
            lo, hi = jnp.where(p.c == 0, m, t), jnp.where(p.c == 0, t, m)
            write(jnp.concatenate([lo, hi], 0).astype(bf16))
        return go

    items = []

    def add(block, column, swap):
        i = len(items)
        items.append(Gather(p, block, column, swap, send.at[i], recv.at[i]))

    add(lambda y, z, x, c: vbuf.at[y, z, x, c], lambda y, x, c: vbuf.at[y, :, x, c], None)

    def add_swapped(view, xs_of, xr_of):
        block = lambda y, z, x, c: view(c).at[y, z, x]
        column = lambda y, x, c: view(c).at[y, :, x]

        def write(v):
            view(p.c)[p.y, p.z, p.x] = v

        add(block, column, (xs_of(1 - p.c), xr_of, joined(lambda: xs_of(p.c)[...], lambda: xr_of[...], write)))

    for g in range(wqkv.shape[0]):
        add_swapped(lambda c, g=g: wqkv.at[g, c], lambda c, g=g: xs_qkv(g, c), xr_qkv.at[g])
    add_swapped(lambda c: wproj.at[c], xs_proj, xr_proj)
    for k in range(wup.shape[0]):
        add(
            lambda y, z, x, c, k=k: wdown.at[k, y, z, x, c],
            lambda y, x, c, k=k: wdown.at[k, y, :, x, c],
            None,
        )
        add_swapped(lambda c, k=k: wup.at[k, c], lambda c, k=k: xs_up(k, c), xr_up.at[k])
    return items


def slice_lanes(v, first, count, at=0):
    lane = lax.broadcasted_iota(jnp.int32, (v.shape[1], PAIR), 0) - first
    out = lax.broadcasted_iota(jnp.int32, (v.shape[1], PAIR), 1) - at
    pick = ((lane == out) & (out >= 0) & (out < count)).astype(f32)
    return lax.dot_general(
        v, pick, (((1,), (0,)), ((), ())), precision=lax.Precision.HIGHEST, preferred_element_type=f32
    )


def attend(k2, v2t, q2, bias_k, write):
    ones = jnp.ones((16, k2.shape[0]), bf16)
    for hh in range(2):
        s = dg(k2, head_only(q2, hh), 1, 1) + bias_k
        top = jnp.max(s, 0, keepdims=True)
        e = jnp.exp(s - top).astype(bf16)
        o = dg(jnp.concatenate([v2t[HD * hh : HD * hh + HD], ones], 0), e, 1, 0)
        total = o[HD : HD + 1]
        write(hh, o[:HD] / total, top + jnp.log(total))


def attend_back(q_of, k2, v2, do_of, ot_of, lse_of, bias_k, block, between):
    seq = k2.shape[0]
    scale = HD**-0.5
    k2t = k2.T
    dk = dv = None
    dqt = []
    for hh in range(2):
        rows = slice(HD * hh, HD * hh + HD)
        parts = []
        for i in range(seq // block):
            sl = slice(i * block, (i + 1) * block)
            qm = head_only(q_of(sl) * jnp.asarray(scale, bf16), hh)
            d = do_of(sl)
            dm = head_only(d, hh)
            delta = jnp.sum(d.astype(f32).T[rows] * ot_of(rows, sl).astype(f32), 0, keepdims=True)
            e = jnp.exp(dg(k2, qm, 1, 1) + bias_k - lse_of(hh, sl))
            ds = (e * (dg(v2, dm, 1, 1) - delta)).astype(bf16)
            t = dg(e.astype(bf16), dm, 1, 0)
            dv = t if dv is None else dv + t
            t = dg(ds, qm, 1, 0)
            dk = t if dk is None else dk + t
            parts.append(dg(k2t[rows], ds, 1, 0) * scale)
        dqt.append(jnp.concatenate(parts, 1))
        if hh == 0:
            between()
    return jnp.concatenate(dqt, 0), dk, dv


def up_step(n2, cot, up, down, up_bias):
    h = dg(n2, up(), 1, 0) + up_bias
    phi = 0.5 * (1.0 + lax.erf(h * 0.7071067811865476))
    a = (h * phi).astype(bf16)
    ga = dg(cot, down(), 1, 1)
    g = (ga * (phi + h * jnp.exp(-0.5 * h * h) * 0.3989422804014327)).astype(bf16)
    return a, g


def pick(index, choices):
    v = choices[0]
    for i in range(1, len(choices)):
        v = jnp.where(index == i, choices[i], v)
    return v


def blocks(count, size, body):
    @pl.loop(0, count)
    def _(r):
        body(r, pl.ds(pl.multiple_of(r * size, size), size))


VECI, G0, G1, G2, PROJ, D0, U0, D1, U1, D2, U2 = range(11)
SV1, SD0, SU0, SD1, SU1, SD2, SU2, SP, SG0, SG1, SG2, SV2 = range(20, 32)
PLAN = {
    "stats": [("B", VECI), ("B", G0), ("Z", G2), ("A", VECI), ("B", G1), ("Z", PROJ), ("A", G0), ("C", VECI),
              ("Z", D0), ("D", VECI), ("C", G0)],
    "norm": [("A", G1), ("B", G2), ("Z", U0), ("D", G0)],
    "f0": [("C", G1), ("A", G2), ("B", PROJ), ("B", D0), ("Z", D1)],
    "f1": [("D", G1), ("C", G2), ("B", U0), ("Z", U1)],
    "f2": [("A", PROJ), ("Z", D2)],
    "f3": [("D", G2), ("A", D0), ("B", D1), ("Z", U2)],
    "f4": [("A", U0), ("C", PROJ), ("B", U1)],
    "f5": [("D", PROJ), ("C", D0)],
    "m0": [("C", U0), ("A", D1), ("B", D2), ("D", D0), ("D", U0)],
    "m0g": [("finish", D0), ("finish", U0)],
    "m1": [("A", U1), ("C", D1), ("B", U2)],
    "m2": [("S0", SD0), ("S0", SU0), ("A", D2), ("C", U1), ("D", D1), ("D", U1)],
    "m2g": [("finish", D1), ("finish", U1)],
    "m3": [("A", U2), ("C", D2), ("S1", SD0), ("S1", SU0)],
    "m4": [("S0", SD1), ("S0", SU1), ("C", U2), ("S2", SD0), ("D", D2), ("D", U2)],
    "m4g": [("finish", D2), ("finish", U2)],
    "m5": [("S2", SU0), ("S1", SD1)],
    "m6": [("S0", SD2), ("S0", SU2), ("S3", SD0), ("S1", SU1), ("finish", PROJ)],
    "mid": [("S0", SP), ("S0", SV1), ("S3", SU0), ("S2", SD1), ("S2", SU1), ("S1", SD2), ("S4", SD0)],
    "b0h": [("S1", SV1), ("S1", SU2), ("S4", SU0)],
    "b0": [("S2", SV1), ("S3", SD1), ("S3", SU1), ("S1", SP), ("S5", SU0)],
    "b1h": [("S3", SV1), ("S2", SD2)],
    "b1": [("S0", SG0), ("S2", SU2), ("S4", SD1), ("S4", SU1), ("S4", SV1)],
    "b2h": [("S1", SG0), ("S2", SP), ("S5", SU1)],
    "b2": [("S3", SD2)],
    "b3h": [("S3", SU2), ("S2", SG0)],
    "b3": [("S0", SG1), ("S3", SP), ("S3", SG0), ("S4", SD2)],
    "b4h": [("S1", SG1), ("S4", SU2)],
    "b4": [("S4", SP), ("S4", SG0), ("S5", SU2)],
    "b5h": [("S2", SG1), ("S5", SP), ("S5", SG0)],
    "b5": [("S0", SG2), ("S3", SG1)],
    "r0": [("S1", SG2)],
    "r2": [("S4", SG1)],
    "r3": [("S0", SV2), ("S2", SG2), ("S5", SG1)],
    "end": [("S1", SV2), ("S3", SG2), ("S2", SV2), ("S3", SV2), ("S4", SG2), ("S4", SV2), ("S5", SG2)],
}


def layer_kernel(
    len_ref, tok_hbm, cot_ref, vec_in, wqkv_in, wproj_in, wup_in, wdown_in,
    out_hbm, gin_hbm, oqkv, oproj, oup, odown, vg_out, qv_out, ub_out,
    n1, n1t, proj, ot, att, lse, res, n2t, acc, gn2, gh,
    vec_ref, ub_ref, wqkv, wproj, wup, wdown, vbuf, xr_qkv, xr_proj, xr_up, gsend, grecv,
    vsum, up0, up1, up2, up3, down0, down1, down2, down3, proj0, proj1, proj2, proj3, qkv1, qkv2, qkv3,
    qkv0, stage_up, stage_proj, stage_qkv, land_up, land_proj, land_qkv, vbufs, send, recv, hsend, hrecv, sems,
):
    seq, width = cot_ref.shape
    half = width // 2
    pairs = proj.shape[0]
    own, rows = wqkv_in.shape[0], wdown_in.shape[0]
    groups, pieces = wqkv.shape[0], wup.shape[0]
    piece = rows // pieces
    sub = wup.shape[-1]
    place = Place(wqkv.shape[3])
    p_ = place
    n2, act, gin, tok_early, tok_late = n1, att, att, gh, n1
    vg_one, vg_two = vsum.at[0, 0], vsum.at[1, 0]

    def own_gradient(g):
        return up0.at[g, :, :, :, :, pl.ds(0, 3 * PAIR)]

    def other_gradient(g):
        return wup.at[g, 1 - place.c, :, :, :, :, pl.ds(0, 3 * PAIR)]


    padded = xr_proj.shape[0]

    def staged(first, lanes):
        return lambda i, c: n2t.at[pl.ds(pl.multiple_of((first + 2 * i + c) * padded, padded), padded), 0:lanes]

    xs_qkv, xs_up = staged(0, 3 * PAIR), staged(2 * groups, sub)
    xs_proj = functools.partial(staged(2 * (groups + pieces), half), 0)

    items = dict(enumerate(gather_items(
        place, wdown_in, wqkv, wproj, wup, wdown, vbuf, (xs_qkv, xs_proj, xs_up), (xr_qkv, xr_proj, xr_up),
        gsend, grecv,
    )))
    handovers = []

    def add(i, own_half, other_half, bufs, total):
        k = i - SV1
        items[i] = Scatter(p_, own_half, other_half, bufs, send.at[k], recv.at[k], total)

    def add_shared(i, own_half, other_half, bufs, stage, landing, write):
        k = i - SV1
        h = Handover(p_, stage, landing, write, hsend.at[k], hrecv.at[k])
        handovers.append(h)
        add(i, own_half, other_half, bufs, h.start)
        items[i].S5 = h.S5

    for k in range(pieces):

        def write_down(total, k=k):
            odown[k * piece : (k + 1) * piece, :] = total

        add(
            SD0 + 2 * k, wdown.at[k, :, :, :, p_.c], wdown.at[k, :, :, :, 1 - p_.c],
            (down0.at[k], down1.at[k], down2.at[k], down3.at[k]), write_down,
        )

        def write_up(c, v, k=k):
            back = regroup(pieces, piece)[:, k * PAIR : (k + 1) * PAIR]
            for i in range(sub // PAIR):
                lanes = pl.ds(pl.multiple_of((c * (sub // PAIR) + i) * pieces * PAIR, PAIR), pieces * PAIR)
                oup[:, lanes] += lax.dot_general(
                    v[:, i * PAIR : (i + 1) * PAIR], back, (((1,), (1,)), ((), ())),
                    precision=lax.Precision.HIGHEST, preferred_element_type=f32,
                )

        add_shared(
            SU0 + 2 * k, wup.at[k, p_.c], wup.at[k, 1 - p_.c], (up0.at[k], up1.at[k], up2.at[k], up3.at[k]),
            stage_up.at[k], land_up.at[k], write_up,
        )

    def write_proj(c, v):
        oproj[:, pl.ds(pl.multiple_of(c * half, PAIR), half)] = v

    add_shared(SP, wproj.at[p_.c], wproj.at[1 - p_.c], (proj0, proj1, proj2, proj3), stage_proj, land_proj, write_proj)
    for g in range(groups):

        def write_qkv(c, v, g=g):
            for t in range(3):
                oqkv[:, pl.ds(pl.multiple_of(t * width + (2 * g + c) * PAIR, PAIR), PAIR)] = v[
                    :, t * PAIR : (t + 1) * PAIR
                ]

        add_shared(
            SG0 + g, own_gradient(g), other_gradient(g),
            (qkv0.at[g], qkv1.at[g], qkv2.at[g], qkv3.at[g]), stage_qkv.at[g], land_qkv.at[g], write_qkv,
        )
    for i, v in ((SV1, 0), (SV2, 1)):
        items[i] = VectorSum(p_, vsum.at[v], vbufs.at[v], send.at[i - SV1], recv.at[i - SV1])
    finished = set()

    def tick(name):
        for step, i in PLAN.get(name, ()):
            getattr(items[i], step)()
            if step == "finish":
                finished.add(i)

    def ticks(index, names):
        for i, name in enumerate(names):
            if PLAN.get(name):

                @pl.when(index == i)
                def _(name=name):
                    tick(name)

    def w_qkv(p):
        return rows_of(wqkv[lax.div(p, 2), lax.rem(p, 2)])

    def w_up(k, u):
        return rows_of(wup[k, u])

    def w_down(k, u):
        return rows_of(wdown[k, u])

    def w_proj(i):
        return rows_of(wproj[i])

    def vec(i):
        return vec_ref[i : i + 1, :]

    rb = 256
    nb = seq // rb
    greet(place)
    tok_copy = pltpu.make_async_copy(tok_hbm, tok_early, sems.at[1])
    tok_copy.start()
    vbuf[p_.y, p_.z, p_.x, p_.c] = vec_in[...]
    for p in range(pairs):
        for t in range(3):
            lanes = slice(t * width + p * PAIR, t * width + (p + 1) * PAIR)
            n2t[p * padded : p * padded + own, t * PAIR : (t + 1) * PAIR] = wqkv_in[:, lanes]
    met(place)
    for i in (G0, G1, G2):
        items[i].X()
    items[VECI].Z()
    items[G0].Z()
    for i in range(2):
        row = (2 * (groups + pieces) + i) * padded
        n2t[row : row + own, 0:half] = wproj_in[:, i * half : (i + 1) * half]
    order = regroup(pieces, piece).astype(bf16)
    for i in range(2 * sub // PAIR):
        u, q = divmod(i, sub // PAIR)
        v = dg(wup_in[:, i * pieces * PAIR : (i + 1) * pieces * PAIR], order, 1, 0).astype(bf16)
        for k in range(pieces):
            row = (2 * (groups + k) + u) * padded
            n2t[row : row + own, q * PAIR : (q + 1) * PAIR] = v[:, k * PAIR : (k + 1) * PAIR]
    items[G1].Z()
    for i in (PROJ, U0, U1, U2):
        items[i].X()
    for k in range(pieces):
        wdown[k, p_.y, p_.z, p_.x, p_.c] = wdown_in[k * piece : (k + 1) * piece, :]
    oup[...] = jnp.zeros(oup.shape, f32)
    tok_copy.wait()

    def stats(r, sl):
        res[sl, :] = norm_parts(tok_early[sl, :].astype(f32))[0]

    blocks(nb, rb, stats)
    tick("stats")
    expand_table(vbuf, vec_ref, ub_ref, own, piece)

    def norm(r, sl):
        n1[sl, :] = (res[sl, :] * vec(AG) + vec(AS)).astype(bf16)

    blocks(nb, rb, norm)
    n1t[...] = n1[...].T
    tick("norm")

    bias_k = key_bias(len_ref[0], seq)
    q_bias = [vec(QB)[:, i * PAIR : (i + 1) * PAIR] for i in range(pairs)]
    v_bias = [vec(VB)[:, i * PAIR : (i + 1) * PAIR] for i in range(pairs)]

    @pl.loop(0, pairs)
    def _(p):
        qkv = dg(n1[...], w_qkv(p), 1, 0)
        proj[p, :, 0:PAIR] = (qkv[:, 0:PAIR] + pick(p, q_bias)).astype(bf16)
        proj[p, :, PAIR : 2 * PAIR] = qkv[:, PAIR : 2 * PAIR].astype(bf16)
        proj[p, :, 2 * PAIR :] = (qkv[:, 2 * PAIR :] + pick(p, v_bias)).astype(bf16)

        def write(hh, o, total):
            ot[p, HD * hh : HD * hh + HD, :] = o.astype(bf16)
            lse[pl.ds(2 * p + hh, 1), :] = total

        attend(
            proj[p, :, PAIR : 2 * PAIR], proj[p, :, 2 * PAIR :].T,
            proj[p, :, 0:PAIR] * jnp.asarray(HD**-0.5, bf16), bias_k, write,
        )
        ticks(p, [f"f{i}" for i in range(pairs)])

    for p in range(pairs):
        att[:, p * PAIR : (p + 1) * PAIR] = ot[p].T

    def branch(r, sl):
        a = att[sl, :]
        v = tok_early[sl, :].astype(f32) + vec(PB)
        v += jnp.concatenate([dg(a, w_proj(i), 1, 0) for i in range(2)], 1)
        res[sl, :] = v
        acc[sl, :] = v + vec(DB)
        gn2[sl, :] = jnp.zeros((rb, width), f32)
        n2[sl, :] = (norm_parts(v)[0] * vec(MG) + vec(MS)).astype(bf16)

    blocks(nb, rb, branch)
    n2t[...] = n2[...].T

    rm = 1024
    @pl.loop(0, 2 * pieces)
    def _(turn):
        k, u = lax.div(turn, 2), lax.rem(turn, 2)
        cols = pl.ds(pl.multiple_of(u * sub, PAIR), sub)
        total = pl.ds(4 + k, 1)
        ticks(turn, [f"m{i}" for i in range(2 * pieces)])
        vg_one[total, cols] = jnp.zeros((1, sub), f32)

        def stage_one(r, sl):
            a, g = up_step(n2[sl, :], cot_ref[sl, :], lambda: w_up(k, u), lambda: w_down(k, u), ub_ref[k, :, cols])
            act[sl, 0:sub] = a
            gh[sl, 0:sub] = g
            acc[sl, :] += dg(a, w_down(k, u), 1, 0)
            gn2[sl, :] += dg(g, w_up(k, u), 1, 1)
            vg_one[total, cols] += jnp.sum(g.astype(f32), 0, keepdims=True)

        blocks(seq // rm, rm, stage_one)
        ticks(turn, [f"m{i}g" for i in range(2 * pieces)])
        v = dg(act[:, 0:sub], cot_ref[...], 0, 0).astype(bf16)
        wdown[k, u] = v.reshape(wdown.shape[2:])
        wup[k, u] = dg(n2t[...], gh[:, 0:sub], 1, 0).astype(bf16).reshape(wup.shape[2:])

    tick(f"m{2 * pieces}")

    vg_one[0:4, :] = jnp.zeros((4, vg_one.shape[1]), f32)
    vg_one[7:8, :] = jnp.zeros((1, vg_one.shape[1]), f32)

    def back_two(r, sl):
        n2[sl, :] = acc[sl, :].astype(bf16)
        g = gn2[sl, :]
        n, inv = norm_parts(res[sl, :])
        cot = cot_ref[sl, :].astype(f32)
        mid = cot + norm_back(n, inv, g * vec(MG))
        acc[sl, :] = mid
        low = mid.astype(bf16)
        act[sl, :] = low
        vg_one[0:1, 0:width] += jnp.sum(g * n, 0, keepdims=True)
        vg_one[1:2, 0:width] += jnp.sum(g, 0, keepdims=True)
        vg_one[2:3, 0:width] += jnp.sum(low.astype(f32), 0, keepdims=True)
        vg_one[3:4, 0:width] += jnp.sum(cot, 0, keepdims=True)
        back = dg(low[:, :half], w_proj(0), 1, 1) + dg(low[:, half:], w_proj(1), 1, 1)
        gh[sl, :] = back.astype(bf16)

    blocks(nb, rb, back_two)
    out_copy = pltpu.make_async_copy(n2, out_hbm, sems.at[0])
    out_copy.start()
    tok_again = pltpu.make_async_copy(tok_hbm, tok_late, sems.at[2])
    for i in range(2):
        v = dg(rows_of(ot[...]), act[:, i * half : (i + 1) * half], 1, 0).astype(bf16)
        wproj[i] = v.reshape(wproj.shape[1:])
    vg_two[...] = jnp.zeros(vg_two.shape, f32)
    tick("mid")

    def weight_gradient(p, dst):
        g = proj[p]
        cols = pl.ds(pl.multiple_of(p * PAIR, PAIR), PAIR)
        sums = jnp.sum(g.astype(f32), 0, keepdims=True)
        vg_two[2:3, cols] = sums[:, 0:PAIR]
        vg_two[3:4, cols] = sums[:, 2 * PAIR :]
        dst[...] = dg(n1t[...], g, 1, 0).astype(bf16).reshape(dst.shape)

    @pl.loop(0, pairs)
    def _(p):
        lanes = pl.ds(pl.multiple_of(p * PAIR, PAIR), PAIR)
        dqt, dk, dv = attend_back(
            lambda sl: proj[p, sl, 0:PAIR],
            proj[p, :, PAIR : 2 * PAIR],
            proj[p, :, 2 * PAIR :],
            lambda sl: gh[sl, lanes],
            lambda rows, sl: ot[p, rows, sl],
            lambda hh, sl: lse[pl.ds(2 * p + hh, 1), sl],
            bias_k,
            512,
            lambda: ticks(p, [f"b{i}h" for i in range(pairs)]),
        )
        proj[p, :, 0:PAIR] = dqt.T.astype(bf16)
        proj[p, :, PAIR : 2 * PAIR] = dk.astype(bf16)
        proj[p, :, 2 * PAIR :] = dv.astype(bf16)

        @pl.when(p == 1)
        def _():
            out_copy.wait()
            tok_again.start()

        @pl.when(lax.rem(p, 2) == 1)
        def _():
            g = lax.div(p, 2)
            weight_gradient(2 * g + p_.c, own_gradient(g))
            weight_gradient(2 * g + 1 - p_.c, other_gradient(g))

        ticks(p, [f"b{i}" for i in range(pairs)])

    tok_again.wait()

    def back_one(r, sl):
        g = dg(proj[0, sl, :], rows_of(wqkv[0, 0]), 1, 1)
        for p in range(1, pairs):
            g += dg(proj[p, sl, :], rows_of(wqkv[p // 2, p % 2]), 1, 1)
        n, inv = norm_parts(tok_late[sl, :].astype(f32))
        gin[sl, :] = (acc[sl, :] + norm_back(n, inv, g * vec(AG))).astype(bf16)
        vg_two[0:1, 0:width] += jnp.sum(g * n, 0, keepdims=True)
        vg_two[1:2, 0:width] += jnp.sum(g, 0, keepdims=True)
        ticks(r, [f"r{i}" for i in range(nb)])

    blocks(nb, rb, back_one)
    gin_copy = pltpu.make_async_copy(gin, gin_hbm, sems.at[1])
    gin_copy.start()
    index = ((p_.y * p_.nz + p_.z) * 2 + p_.x) * 2 + p_.c
    one = vsum[0, 4]
    vg_out[0:8, :] = slice_lanes(one, index * own, own)
    up = sum(slice_lanes(one, index * piece, piece, k * piece)[4 + k : 5 + k] for k in range(pieces))
    ub_out[...] = up[:, 0:rows]
    tick("end")
    late = slice_lanes(vsum[1, 4], index * own, own)
    vg_out[8:16, :] = late
    qv_out[...] = late[2:4, 0:own]
    for i, item in items.items():
        if i not in finished:
            item.finish()
    for h in handovers:
        h.end()
    gin_copy.wait()


def forward_kernel(
    len_ref, tok_ref, cot_ref, vec_ref, wqkv, wproj, wup, wdown,
    out_hbm, proj_hbm, ot_hbm, lse_hbm, do_hbm, gmid_hbm, n1t_hbm, gup_hbm, gdown_hbm, gproj_hbm, vg_ref,
    n1, n1t, proj, ot, att, lse, res, n2, n2t, acc, gn2, act, gh, gstage, sems,
):
    seq, width = tok_ref.shape
    half = width // 2
    chunks, pairs = gup_hbm.shape[0], proj.shape[0]
    copies = []

    def send_out(src, dst, sem):
        cp = pltpu.make_async_copy(src, dst, sem)
        cp.start()
        copies.append(cp)

    def vec(i):
        return vec_ref[i : i + 1, :]

    rb = 256
    nb = seq // rb

    def norm(r, sl):
        n1[sl, :] = (norm_parts(tok_ref[sl, :].astype(f32))[0] * vec(AG) + vec(AS)).astype(bf16)

    blocks(nb, rb, norm)
    n1t[...] = n1[...].T
    send_out(n1t, n1t_hbm, sems.at[0])
    bias_k = key_bias(len_ref[0], seq)
    q_bias = [vec(QB)[:, i * PAIR : (i + 1) * PAIR] for i in range(pairs)]
    v_bias = [vec(VB)[:, i * PAIR : (i + 1) * PAIR] for i in range(pairs)]

    @pl.loop(0, pairs)
    def _(p):
        qkv = dg(n1[...], wqkv[p], 1, 0)
        proj[p, :, 0:PAIR] = (qkv[:, 0:PAIR] + pick(p, q_bias)).astype(bf16)
        proj[p, :, PAIR : 2 * PAIR] = qkv[:, PAIR : 2 * PAIR].astype(bf16)
        proj[p, :, 2 * PAIR :] = (qkv[:, 2 * PAIR :] + pick(p, v_bias)).astype(bf16)

        def write(hh, o, total):
            ot[p, HD * hh : HD * hh + HD, :] = o.astype(bf16)
            lse[pl.ds(2 * p + hh, 1), :] = total

        attend(
            proj[p, :, PAIR : 2 * PAIR], proj[p, :, 2 * PAIR :].T,
            proj[p, :, 0:PAIR] * jnp.asarray(HD**-0.5, bf16), bias_k, write,
        )

    for p in range(pairs):
        att[:, p * PAIR : (p + 1) * PAIR] = ot[p].T
    send_out(proj, proj_hbm, sems.at[1])
    send_out(ot, ot_hbm, sems.at[2])
    send_out(lse, lse_hbm, sems.at[3])

    def branch(r, sl):
        a = att[sl, :]
        v = tok_ref[sl, :].astype(f32) + vec(PB)
        v += jnp.concatenate([dg(a, wproj[i], 1, 0) for i in range(2)], 1)
        res[sl, :] = v
        acc[sl, :] = v + vec(DB)
        gn2[sl, :] = jnp.zeros((rb, width), f32)
        n2[sl, :] = (norm_parts(v)[0] * vec(MG) + vec(MS)).astype(bf16)

    blocks(nb, rb, branch)
    n2t[...] = n2[...].T
    rm = 512
    staged = []
    for j in range(chunks):
        vg_ref[4 + j : 5 + j, :] = jnp.zeros((1, width), f32)

        def stage_one(r, sl, j=j):
            a, g = up_step(n2[sl, :], cot_ref[sl, :], lambda: wup[j], lambda: wdown[j], vec(UB + j))
            act[sl, :] = a
            gh[sl, :] = g
            acc[sl, :] += dg(a, wdown[j], 1, 0)
            gn2[sl, :] += dg(g, wup[j], 1, 1)
            vg_ref[4 + j : 5 + j, :] += jnp.sum(g.astype(f32), 0, keepdims=True)

        blocks(seq // rm, rm, stage_one)
        for cp in staged:
            cp.wait()
        gstage[0] = dg(act[...], cot_ref[...], 0, 0).astype(bf16)
        gstage[1] = dg(n2t[...], gh[...], 1, 0).astype(bf16)
        staged = [
            pltpu.make_async_copy(gstage.at[0], gdown_hbm.at[j], sems.at[4]),
            pltpu.make_async_copy(gstage.at[1], gup_hbm.at[j], sems.at[5]),
        ]
        for cp in staged:
            cp.start()

    vg_ref[0:4, :] = jnp.zeros((4, width), f32)

    def back_two(r, sl):
        n2[sl, :] = acc[sl, :].astype(bf16)
        g = gn2[sl, :]
        n, inv = norm_parts(res[sl, :])
        cot = cot_ref[sl, :].astype(f32)
        mid = cot + norm_back(n, inv, g * vec(MG))
        acc[sl, :] = mid
        low = mid.astype(bf16)
        act[sl, :] = low
        vg_ref[0:1, :] += jnp.sum(g * n, 0, keepdims=True)
        vg_ref[1:2, :] += jnp.sum(g, 0, keepdims=True)
        vg_ref[2:3, :] += jnp.sum(low.astype(f32), 0, keepdims=True)
        vg_ref[3:4, :] += jnp.sum(cot, 0, keepdims=True)
        gh[sl, :] = (dg(low[:, :half], wproj[0], 1, 1) + dg(low[:, half:], wproj[1], 1, 1)).astype(bf16)

    blocks(nb, rb, back_two)
    send_out(n2, out_hbm, sems.at[6])
    send_out(acc, gmid_hbm, sems.at[7])
    for p in range(pairs):
        send_out(gh.at[:, p * PAIR : (p + 1) * PAIR], do_hbm.at[p], sems.at[8 + p])
    for cp in staged:
        cp.wait()
    for i in range(2):
        gstage[i, :, :half] = dg(rows_of(ot[...]), act[:, i * half : (i + 1) * half], 1, 0).astype(bf16)
        send_out(gstage.at[i, :, pl.ds(0, half)], gproj_hbm.at[i], sems.at[4 + i])
    for cp in copies:
        cp.wait()


def backward_kernel(
    len_ref, tok_ref, vec_ref, proj_hbm, ot_hbm, lse_hbm, do_hbm, gmid_hbm, n1t_hbm, wqkv_ref,
    gin_hbm, gqkv_hbm, vg_ref,
    proj, ot, lse, do, gmid, n1t, gqkv, gin, sems,
):
    seq, width = tok_ref.shape
    pairs = proj.shape[0]

    def start(src, dst, sem):
        cp = pltpu.make_async_copy(src, dst, sem)
        cp.start()
        return cp

    loads = [
        start(proj_hbm, proj, sems.at[0]),
        start(do_hbm, do, sems.at[1]),
        start(ot_hbm, ot, sems.at[2]),
        start(lse_hbm, lse, sems.at[3]),
        start(n1t_hbm, n1t, sems.at[4]),
        start(gmid_hbm, gmid, sems.at[5]),
    ]
    for cp in loads:
        cp.wait()
    vg_ref[...] = jnp.zeros(vg_ref.shape, f32)
    bias_k = key_bias(len_ref[0], seq)

    @pl.loop(0, pairs)
    def _(p):
        dqt, dk, dv = attend_back(
            lambda sl: proj[p, sl, 0:PAIR],
            proj[p, :, PAIR : 2 * PAIR],
            proj[p, :, 2 * PAIR :],
            lambda sl: do[p, sl, :],
            lambda rows, sl: ot[p, rows, sl],
            lambda hh, sl: lse[pl.ds(2 * p + hh, 1), sl],
            bias_k,
            512,
            lambda: None,
        )
        proj[p, :, 0:PAIR] = dqt.T.astype(bf16)
        proj[p, :, PAIR : 2 * PAIR] = dk.astype(bf16)
        proj[p, :, 2 * PAIR :] = dv.astype(bf16)

    outs = []
    for p in range(pairs):
        cols = slice(p * PAIR, (p + 1) * PAIR)
        g = proj[p]
        sums = jnp.sum(g.astype(f32), 0, keepdims=True)
        vg_ref[2:3, cols] = sums[:, 0:PAIR]
        vg_ref[3:4, cols] = sums[:, 2 * PAIR :]
        gqkv[p] = dg(n1t[...], g, 1, 0).astype(bf16)
        outs.append(start(gqkv.at[p], gqkv_hbm.at[p], sems.at[6 + p]))

    def back_one(r, sl):
        g = dg(proj[0, sl, :], wqkv_ref[0], 1, 1)
        for p in range(1, pairs):
            g += dg(proj[p, sl, :], wqkv_ref[p], 1, 1)
        n, inv = norm_parts(tok_ref[sl, :].astype(f32))
        gin[sl, :] = (gmid[sl, :] + norm_back(n, inv, g * vec_ref[AG : AG + 1, :])).astype(bf16)
        vg_ref[0:1, :] += jnp.sum(g * n, 0, keepdims=True)
        vg_ref[1:2, :] += jnp.sum(g, 0, keepdims=True)

    blocks(seq // 256, 256, back_one)
    outs.append(start(gin, gin_hbm, sems.at[0]))
    for cp in outs:
        cp.wait()


def specs(kinds):
    table = {"s": pltpu.SMEM, "v": pltpu.VMEM, "h": pl.ANY}
    return [pl.BlockSpec(memory_space=table[k]) for k in kinds]


def sds(shape, dtype):
    return jax.ShapeDtypeStruct(shape, dtype)


def run_layer(nz, lengths, tokens, cotangent, vecs, wqkv, wproj, wup, wdown):
    seq, width = tokens.shape
    half = width // 2
    pairs = width // PAIR
    groups = pairs // 2
    own, rows = wup.shape[0], wdown.shape[0]
    piece = 32
    pieces = rows // piece
    sub = wup.shape[1] // pieces // 2
    chip = (2, nz, 2)
    padded = -(-own // 16) * 16

    def vmem(*dims, dtype=bf16):
        return pltpu.VMEM(dims, dtype)

    def landing(lead, block):
        return [pltpu.VMEM(lead + dims + block, bf16) for dims in (chip, (2, nz), (nz,), (nz - 1,))]

    qkv_landing = landing((groups,), (2 * own, 3 * PAIR))
    handover = [
        vmem(pieces, own, sub, dtype=f32),
        vmem(own, half, dtype=f32),
        vmem(groups, own, 3 * PAIR, dtype=f32),
    ]
    scratch = (
        [
            vmem(seq, width),
            vmem(width, seq),
            vmem(pairs, seq, 3 * PAIR),
            vmem(pairs, PAIR, seq),
            vmem(seq, width),
            vmem(2 * pairs, seq, dtype=f32),
            vmem(seq, width, dtype=f32),
            vmem(width, seq),
            vmem(seq, width, dtype=f32),
            vmem(seq, width, dtype=f32),
            vmem(seq, width),
            vmem(16, width, dtype=f32),
            vmem(pieces, 1, 2 * sub, dtype=f32),
            vmem(groups, 2, *chip, 2 * own, 3 * PAIR),
            vmem(2, *chip, 2 * own, half),
            vmem(pieces, 2, *chip, 2 * own, sub),
            vmem(pieces, *chip, 2, piece, width),
            vmem(*chip, 2, 16, PAIR),
            vmem(groups, padded, 3 * PAIR),
            vmem(padded, half),
            vmem(pieces, padded, sub),
            pltpu.SemaphoreType.DMA((5 + 2 * pieces, 8 + nz - 1)),
            pltpu.SemaphoreType.DMA((5 + 2 * pieces, 8 + nz - 1)),
            vmem(2, 5, 8, 2 * sub, dtype=f32),
        ]
        + landing((pieces,), (2 * own, sub))
        + landing((pieces,), (piece, width))
        + landing((), (2 * own, half))
        + qkv_landing[1:]
        + qkv_landing[:1]
        + handover
        + handover
        + [
            vmem(2, 2 + nz, 8, 2 * sub, dtype=f32),
            pltpu.SemaphoreType.DMA((12, 3 + nz)),
            pltpu.SemaphoreType.DMA((12, 3 + nz)),
            pltpu.SemaphoreType.DMA((12,)),
            pltpu.SemaphoreType.DMA((12,)),
            pltpu.SemaphoreType.DMA((3,)),
        ]
    )
    return pl.pallas_call(
        layer_kernel,
        in_specs=specs("shvvvvvv"),
        out_specs=specs("hhvvvvvvv"),
        out_shape=[
            sds((seq, width), bf16),
            sds((seq, width), bf16),
            sds((own, 3 * width), f32),
            sds((own, width), f32),
            sds((own, wup.shape[1]), f32),
            sds((rows, width), f32),
            sds((16, PAIR), f32),
            sds((2, own), f32),
            sds((1, rows), f32),
        ],
        scratch_shapes=scratch,
        compiler_params=pltpu.CompilerParams(vmem_limit_bytes=VMEM_LIMIT, collective_id=0, has_side_effects=True),
        name="layer",
    )(lengths, tokens, cotangent, vecs, wqkv, wproj, wup, wdown)


def run_forward(lengths, tokens, cotangent, vecs, wqkv, wproj, wup, wdown):
    seq, width = tokens.shape
    pairs = width // PAIR
    chunks = wup.shape[0]
    return pl.pallas_call(
        forward_kernel,
        in_specs=specs("svvvvvvv"),
        out_specs=specs("hhhhhhhhhhv"),
        out_shape=[
            sds((seq, width), bf16),
            sds((pairs, seq, 3 * PAIR), bf16),
            sds((pairs, PAIR, seq), bf16),
            sds((2 * pairs, seq), f32),
            sds((pairs, seq, PAIR), bf16),
            sds((seq, width), f32),
            sds((width, seq), bf16),
            sds((chunks, width, width), bf16),
            sds((chunks, width, width), bf16),
            sds((2, width, width // 2), bf16),
            sds((8, width), f32),
        ],
        scratch_shapes=[
            pltpu.VMEM((seq, width), bf16),
            pltpu.VMEM((width, seq), bf16),
            pltpu.VMEM((pairs, seq, 3 * PAIR), bf16),
            pltpu.VMEM((pairs, PAIR, seq), bf16),
            pltpu.VMEM((seq, width), bf16),
            pltpu.VMEM((2 * pairs, seq), f32),
            pltpu.VMEM((seq, width), f32),
            pltpu.VMEM((seq, width), bf16),
            pltpu.VMEM((width, seq), bf16),
            pltpu.VMEM((seq, width), f32),
            pltpu.VMEM((seq, width), f32),
            pltpu.VMEM((seq, width), bf16),
            pltpu.VMEM((seq, width), bf16),
            pltpu.VMEM((2, width, width), bf16),
            pltpu.SemaphoreType.DMA((8 + pairs,)),
        ],
        compiler_params=pltpu.CompilerParams(vmem_limit_bytes=VMEM_LIMIT),
        name="layer_forward",
    )(lengths, tokens, cotangent, vecs, wqkv, wproj, wup, wdown)


def run_backward(lengths, tokens, vecs, proj, ot, lse, do, gmid, n1t, wqkv):
    seq, width = tokens.shape
    pairs = width // PAIR
    return pl.pallas_call(
        backward_kernel,
        in_specs=specs("svvhhhhhhv"),
        out_specs=specs("hhv"),
        out_shape=[
            sds((seq, width), bf16),
            sds((pairs, width, 3 * PAIR), bf16),
            sds((8, width), f32),
        ],
        scratch_shapes=[
            pltpu.VMEM((pairs, seq, 3 * PAIR), bf16),
            pltpu.VMEM((pairs, PAIR, seq), bf16),
            pltpu.VMEM((2 * pairs, seq), f32),
            pltpu.VMEM((pairs, seq, PAIR), bf16),
            pltpu.VMEM((seq, width), f32),
            pltpu.VMEM((width, seq), bf16),
            pltpu.VMEM((pairs, width, 3 * PAIR), bf16),
            pltpu.VMEM((seq, width), bf16),
            pltpu.SemaphoreType.DMA((6 + pairs,)),
        ],
        compiler_params=pltpu.CompilerParams(vmem_limit_bytes=VMEM_LIMIT),
        name="attention_backward",
    )(lengths, tokens, vecs, proj, ot, lse, do, gmid, n1t, wqkv)


def gathered(item, axis=0):
    return lax.all_gather(item, AXES, axis=axis, tiled=True)


def scattered(item, axis=0):
    return lax.psum_scatter(item, AXES, scatter_dimension=axis, tiled=True)


def per_device(
    nz, tokens, cotangent, lengths, attn_gain, attn_shift, qkv_weight, qv_bias, proj_weight, proj_bias,
    mlp_gain, mlp_shift, up_weight, up_bias, down_weight, down_bias,
):
    seq, width = tokens.shape
    pairs = width // PAIR
    own = attn_gain.shape[0]
    chunks = up_weight.shape[1] // width
    small = jnp.stack([attn_gain, attn_shift, qv_bias[0], qv_bias[1], proj_bias, mlp_gain, mlp_shift, down_bias])
    if nz:
        vecs = jnp.concatenate(
            [
                jnp.pad(small, ((0, 0), (0, PAIR - own))),
                jnp.pad(up_bias[None], ((0, 7), (0, PAIR - up_bias.shape[0]))),
            ]
        )
        block_out, input_grad, g_qkv, g_proj, g_up, g_down, v, g_qv, g_ub = run_layer(
            nz, lengths, tokens, cotangent, vecs, qkv_weight, proj_weight, up_weight, down_weight
        )
        w = v[:, :own]
        return (
            block_out, input_grad, w[8], w[9], g_qkv, g_qv, g_proj, w[2], w[0], w[1],
            g_up, g_ub.reshape(-1), g_down, w[3],
        )
    allvec = gathered(jnp.concatenate([small.reshape(-1), up_bias])[None])
    many = allvec.shape[0]
    table = allvec[:, : 8 * own].reshape(many, 8, own).transpose(1, 0, 2).reshape(8, width)
    vecs = jnp.concatenate([table, allvec[:, 8 * own :].reshape(chunks, width)], 0).astype(f32)
    wqkv = gathered(qkv_weight).reshape(width, 3, pairs, PAIR).transpose(2, 0, 1, 3).reshape(pairs, width, 3 * PAIR)
    wproj = gathered(proj_weight).reshape(width, 2, width // 2).transpose(1, 0, 2)
    wup = gathered(up_weight).reshape(width, chunks, width).transpose(1, 0, 2)
    wdown = gathered(down_weight).reshape(chunks, width, width)
    block_out, proj, ot, lse, do, gmid, n1t, gup, gdown, gproj, vg_one = run_forward(
        lengths, tokens, cotangent, vecs, wqkv, wproj, wup, wdown
    )
    input_grad, gqkv, vg_two = run_backward(lengths, tokens, vecs, proj, ot, lse, do, gmid, n1t, wqkv)
    g_down = scattered(gdown.astype(f32).reshape(chunks * width, width))
    g_up = scattered(gup.astype(f32).transpose(1, 0, 2).reshape(width, chunks * width))
    g_proj = scattered(gproj.astype(f32).transpose(1, 0, 2).reshape(width, width))
    g_qkv = scattered(
        gqkv.astype(f32).reshape(pairs, width, 3, PAIR).transpose(1, 2, 0, 3).reshape(width, 3 * width)
    )
    rest = jnp.concatenate([vg_two[:4], vg_one[:4]], 0).reshape(8, many, own).transpose(1, 0, 2).reshape(many, -1)
    rest = jnp.concatenate([rest, vg_one[4:].reshape(many, -1)], 1)
    mine = scattered(rest)[0]
    v = mine[: 8 * own].reshape(8, own)
    return (
        block_out, input_grad, v[0], v[1], g_qkv, v[2:4], g_proj, v[6], v[4], v[5],
        g_up, mine[8 * own :], g_down, v[7],
    )


def chips_along_z(mesh):
    dp, shard = mesh.shape["dp"], mesh.shape["shard"]
    return shard // 4 if dp == 2 and shard == 16 else 0


def solution(mesh):
    one, two, mid = P(AXES), P(AXES, None), P(None, AXES)
    return jax.shard_map(
        functools.partial(per_device, chips_along_z(mesh)),
        mesh=mesh,
        in_specs=(two, two, one, one, one, two, mid, two, one, one, one, two, one, two, one),
        out_specs=(two, two, one, one, two, mid, two, one, one, one, two, one, two, one),
        check_vma=False,
    )
```
